32 devices in a mesh: dp: 16 (over z, y, x), tensor: 2 (over core).
Axes of the slice: x: 2, y: 2, z: 4, core: 2. Of those that a mesh axis runs over, the one named last changes fastest.
Arguments:
- tokens: bfloat16 [16, 1024, 768], P('dp', 'tensor'), may hold values from -6 to 6
- lengths: int32 [16], replicated, may hold values from 576 to 1024, as said below
- drop_in: int32 [16, 2, 1024, 768], P('dp', None, 'tensor'), may hold values 0 or 1
- drop_attn: int32 [16, 2, 1024, 768], P('dp', None, 'tensor'), may hold values 0 or 1
- drop_ffn: int32 [16, 2, 1024, 768], P('dp', None, 'tensor'), may hold values 0 or 1
- qkv_weight: bfloat16 [768, 3, 768], P(None, None, 'tensor'), may hold values from -0.21875 to 0.21875
- out_weight: bfloat16 [768, 768], P('tensor'), may hold values from -6 to 6
- up_weight: bfloat16 [768, 3072], P(None, 'tensor'), may hold values from -0.21875 to 0.21875
- down_weight: bfloat16 [3072, 768], P('tensor'), may hold values from -0.109375 to 0.109375
- gain_first: float32 [768], replicated, may hold values from 0.5 to 1.5
- shift_first: float32 [768], replicated, may hold values from -0.5 to 0.5
- gain_second: float32 [768], replicated, may hold values from 0.5 to 1.5
- shift_second: float32 [768], replicated, may hold values from -0.46875 to 0.46875
- cotangent: bfloat16 [16, 2, 1024, 768], P('dp', None, 'tensor'), may hold values from -0.00063323975 to 0.00063323975
Outputs:
- layer_out: bfloat16 [16, 2, 1024, 768], P('dp', None, 'tensor')
- grad_tokens: float32 [16, 1024, 768], P('dp', 'tensor')
- grad_qkv: float32 [768, 3, 768], P(None, None, 'tensor')
- grad_out: float32 [768, 768], P('tensor')
- grad_up: float32 [768, 3072], P(None, 'tensor')
- grad_down: float32 [3072, 768], P('tensor')
- grad_gain_first: float32 [768], replicated
- grad_shift_first: float32 [768], replicated
- grad_gain_second: float32 [768], replicated
- grad_shift_second: float32 [768], replicated
- loss: float32 [], replicated
- alignment: float32 [], replicated
- uniformity: float32 [], replicated
The draws below stay inside these ranges and needn't reach their ends.
Inputs may be any that keep to these rules, and one draw needn't show every extreme that they name: `lengths`: at least one pair is 1024 tokens long.
All inputs are finite; a program needn't handle non-finite values. No bound on the sum of `drop_in` or of `drop_attn` or of `drop_ffn` on one device may be relied on, other than what follows from the above.
Results may differ from the reference program's by a relative error of at most 0.019.
The reference program's roundings to bfloat16 on the way count: a program that leaves them out, or rounds other values in their place, can miss the bound.
Values may be sent and summed in bfloat16 or wider, within the bound.
A program may use at most 192 MiB of HBM per device.

```python
import jax
import jax.numpy as jnp
from jax import lax

D = 768
HEADS = 12
HEAD_DIM = 64
FF = 3072
SEQ = 1024
PAIRS = 16


def draw_lengths(key, part):
    key = jax.random.fold_in(key, 7)
    first_key, second_key = jax.random.split(key)
    low_end = SEQ // 2 + SEQ // 16
    drawn = jax.random.randint(first_key, (PAIRS,), low_end, SEQ + 1, dtype=jnp.int32)
    longest = jax.random.randint(second_key, (), 0, PAIRS, dtype=jnp.int32)
    return drawn.at[longest].set(SEQ).astype(jnp.int32)


def with_ends(result, stream_key, low, top_value):
    place = [jax.random.randint(jax.random.fold_in(stream_key, axis), (), 0, length) for axis, length in enumerate(result.shape)]
    main_axis = result.shape.index(max(result.shape))
    next_to = place[:main_axis] + [(place[main_axis] + 1) % result.shape[main_axis]] + place[main_axis + 1:]
    return result.at[tuple(place)].set(low).at[tuple(next_to)].set(top_value)


def block_scale(key, dims, cuts, low, high):
    def one(axis_at, shards_of):
        draws = jax.random.uniform(jax.random.fold_in(jax.random.fold_in(key, 6), axis_at), (shards_of,), jnp.float32, low / len(cuts), high / len(cuts))
        return jnp.repeat(jnp.exp(draws), dims[axis_at] // shards_of).reshape((-1,) + (1,) * (len(dims) - axis_at - 1))

    level = one(*cuts[0])
    for cut in cuts[1:]:
        level = level * one(*cut)
    return level


def normal_values(key, extent, deviation, reach, cuts=(), kind=jnp.bfloat16):
    entries = deviation * jax.random.normal(key, extent, jnp.float32)
    if cuts:
        entries = entries * block_scale(key, extent, cuts, -0.22, 0.18)
    return jnp.clip(entries, -reach, reach).astype(kind)


def setup_inputs(seed: int = 0) -> dict:
    key_list = jax.random.split(jax.random.key(seed), 15)
    return {
        "tokens": normal_values(key_list[0], (PAIRS, SEQ, D), 1.0, 6.0, ((0, 16), (1, 2))),
        "lengths": draw_lengths(jax.random.fold_in(key_list[14], 71), 0),
        "drop_in": with_ends((jax.random.randint(key_list[2], (PAIRS, 2, SEQ, D), 0, 10) < 9).astype(jnp.int32), jax.random.fold_in(key_list[2], 1), 0, 1),
        "drop_attn": with_ends((jax.random.randint(key_list[3], (PAIRS, 2, SEQ, D), 0, 10) < 9).astype(jnp.int32), jax.random.fold_in(key_list[3], 1), 0, 1),
        "drop_ffn": with_ends((jax.random.randint(key_list[4], (PAIRS, 2, SEQ, D), 0, 10) < 9).astype(jnp.int32), jax.random.fold_in(key_list[4], 1), 0, 1),
        "qkv_weight": normal_values(key_list[5], (D, 3, D), D ** -0.5, 0.21875, ((2, 2),)),
        "out_weight": normal_values(key_list[6], (D, D), (SEQ ** 0.5 * D ** -0.5), 6.0, ((0, 2),)),
        "up_weight": normal_values(key_list[7], (D, FF), D ** -0.5, 0.21875, ((1, 2),)),
        "down_weight": normal_values(key_list[8], (FF, D), FF ** -0.5, 0.109375, ((0, 2),)),
        "gain_first": jnp.clip(1.0 + 0.1 * jax.random.normal(key_list[9], (D,), jnp.float32), 0.5, 1.5),
        "shift_first": normal_values(key_list[10], (D,), 0.1, 0.5, (), jnp.float32),
        "gain_second": jnp.clip(1.0 + 0.1 * jax.random.normal(key_list[11], (D,), jnp.float32), 0.5, 1.5),
        "shift_second": normal_values(key_list[12], (D,), (3 * SEQ ** -0.5), 0.46875, (), jnp.float32),
        "cotangent": normal_values(key_list[13], (PAIRS, 2, SEQ, D), (3 * D ** -0.5 / SEQ), 0.00063323975, ((0, 16), (2, 2))),
    }


EXACT_PRECISION = lax.Precision.HIGHEST
KEEP_RATE = 0.9
SOFTMAX_WARMTH = 0.05
EPSILON = 1e-06
MASKED_SCORE = -1e+30

@jax.custom_vjp
def low(v):
    return lax.optimization_barrier(v.astype(jnp.bfloat16)).astype(jnp.float32)

@jax.custom_vjp
def low_back(v):
    return v

def low_keep(v):
    return (low(v), None)

def low_pass(kept, grad):
    return (grad,)

def back_keep(v):
    return (v, None)

def back_low(kept, grad):
    return (low(grad),)
low.defvjp(low_keep, low_pass)
low_back.defvjp(back_keep, back_low)

def layer_norm(resid, gain_vec, shift_vec):
    row_mean = lax.optimization_barrier(jnp.mean(resid, axis=-1, keepdims=True))
    centred = resid - row_mean
    row_var = lax.optimization_barrier(jnp.mean(centred * centred, axis=-1, keepdims=True))
    return centred * lax.rsqrt(row_var + EPSILON) * gain_vec + shift_vec

def pair_layer(weights, members):
    qkv_w, out_w, up_w, down_w, gain_a, shift_a, gain_b, shift_b = weights
    token_rows, keep_in, keep_attn, keep_ffn, length = members
    x_view = token_rows[None] * keep_in / KEEP_RATE
    x_low = low(x_view)
    qkv = low_back(low(jnp.einsum('vtd,dce->vtce', x_low, qkv_w, precision=EXACT_PRECISION)))
    queries = qkv[:, :, 0].reshape(2, SEQ, HEADS, HEAD_DIM)
    keys = qkv[:, :, 1].reshape(2, SEQ, HEADS, HEAD_DIM)
    values = qkv[:, :, 2].reshape(2, SEQ, HEADS, HEAD_DIM)
    scores = low_back(jnp.einsum('vqhd,vkhd->vhqk', queries, keys, precision=EXACT_PRECISION) * HEAD_DIM ** (-0.5))
    live_keys = jnp.arange(SEQ, dtype=jnp.int32) < length
    scores = jnp.where(live_keys, scores, MASKED_SCORE)
    probs = jax.nn.softmax(scores, axis=-1)
    context = jnp.einsum('vhqk,vkhd->vqhd', low(probs), values, precision=EXACT_PRECISION).reshape(2, SEQ, D)
    context = low(low_back(context))
    attn_branch = low_back(jnp.einsum('vtd,de->vte', context, out_w, precision=EXACT_PRECISION))
    h_one = layer_norm(x_view + attn_branch * keep_attn / KEEP_RATE, gain_a, shift_a)
    pre_act = low_back(jnp.einsum('vtd,df->vtf', low(h_one), up_w, precision=EXACT_PRECISION))
    activated = low(jax.nn.gelu(pre_act, approximate=False))
    ffn_branch = low_back(jnp.einsum('vtf,fd->vtd', activated, down_w, precision=EXACT_PRECISION))
    return layer_norm(h_one + ffn_branch * keep_ffn / KEEP_RATE, gain_b, shift_b)

def reference(tokens, lengths, drop_in, drop_attn, drop_ffn, qkv_weight, out_weight, up_weight, down_weight, gain_first, shift_first, gain_second, shift_second, cotangent):
    keep_in = drop_in.astype(jnp.float32)
    keep_attn = drop_attn.astype(jnp.float32)
    keep_ffn = drop_ffn.astype(jnp.float32)

    def forward(token_data, qkv_w, out_w, up_w, down_w, gain_a, shift_a, gain_b, shift_b):
        weights = (qkv_w, out_w, up_w, down_w, gain_a, shift_a, gain_b, shift_b)

        def one_pair(members):
            return pair_layer(weights, members)
        layer_rows = lax.map(jax.checkpoint(one_pair), (token_data, keep_in, keep_attn, keep_ffn, lengths))
        live_rows = jnp.arange(SEQ, dtype=jnp.int32)[None, :] < lengths[:, None]
        pooled = lax.optimization_barrier(jnp.sum(jnp.where(live_rows[:, None, :, None], layer_rows, 0.0), axis=2)) / lengths.astype(jnp.float32)[:, None, None]
        unit_vectors = pooled * lax.rsqrt(lax.optimization_barrier(jnp.sum(pooled * pooled, axis=-1, keepdims=True)) + EPSILON)
        first_dropout_view = unit_vectors[:, 0]
        second_dropout_view = unit_vectors[:, 1]
        cosine_scores = jnp.dot(first_dropout_view, second_dropout_view.T, precision=EXACT_PRECISION) / SOFTMAX_WARMTH
        row_top = lax.optimization_barrier(jnp.max(cosine_scores, axis=1, keepdims=True))
        log_total = row_top[:, 0] + jnp.log(lax.optimization_barrier(jnp.sum(jnp.exp(cosine_scores - row_top), axis=1)))
        loss_mean = jnp.mean(log_total - jnp.diagonal(cosine_scores))
        gap = first_dropout_view - second_dropout_view
        alignment = jnp.mean(lax.optimization_barrier(jnp.sum(gap * gap, axis=-1)))
        sq_norms = lax.optimization_barrier(jnp.sum(first_dropout_view * first_dropout_view, axis=-1))
        sq_dist = sq_norms[:, None] + sq_norms[None, :] - 2.0 * jnp.dot(first_dropout_view, first_dropout_view.T, precision=EXACT_PRECISION)
        indices = jnp.arange(PAIRS, dtype=jnp.int32)
        off_diag = indices[:, None] != indices[None, :]
        potential = jnp.sum(jnp.where(off_diag, jnp.exp(-2.0 * sq_dist), 0.0))
        uniformity = jnp.log(potential / (PAIRS * (PAIRS - 1)))
        return (layer_rows, loss_mean, alignment, uniformity)
    outputs, pullback = jax.vjp(forward, tokens.astype(jnp.float32), qkv_weight.astype(jnp.float32), out_weight.astype(jnp.float32), up_weight.astype(jnp.float32), down_weight.astype(jnp.float32), gain_first, shift_first, gain_second, shift_second)
    layer_rows, loss_mean, alignment, uniformity = outputs
    gradients = pullback((cotangent.astype(jnp.float32), jnp.float32(PAIRS), jnp.float32(0.0), jnp.float32(0.0)))
    return (layer_rows.astype(jnp.bfloat16), gradients[0], gradients[1], gradients[2], gradients[3], gradients[4], gradients[5], gradients[6], gradients[7], gradients[8], loss_mean, alignment, uniformity)
```

```python
import functools
import math

import jax
import jax.numpy as jnp
from jax import lax
from jax.experimental import pallas as pl
from jax.experimental.pallas import tpu as pltpu
from jax.sharding import PartitionSpec as P

HEAD_DIM = 64
INV_KEEP = 1.0 / 0.9
SOFTMAX_WARMTH = 0.05
EPSILON = 1e-06
MASKED_SCORE = -1e30
MESH = pl.DeviceIdType.MESH
F32 = jnp.float32
BF16 = jnp.bfloat16
VMEM_LIMIT = 60 * 2**20
HIGHEST = lax.Precision.HIGHEST

TAIL_P = 0.3
TAIL = (
    0.11962929778234735,
    0.12075397394392673,
    0.09991336806236217,
    0.1285620774207718,
    -0.05368457414666341,
    0.20635459819946347,
    -0.15720376083821283,
    0.03567494667807555,
)


def dot_nn(a, b):
    return jnp.dot(a, b, preferred_element_type=F32)


def dot_nt(a, b):
    return lax.dot_general(a, b, (((1,), (1,)), ((), ())), preferred_element_type=F32)


def dot_tn(a, b):
    return lax.dot_general(a, b, (((0,), (0,)), ((), ())), preferred_element_type=F32)


def gelu_pair(x):
    z = jnp.abs(x)
    bell = jnp.exp(x * x * -0.5)
    t = 1.0 / (1.0 + TAIL_P * z)
    acc = jnp.full_like(t, TAIL[-1])
    for c in TAIL[-2::-1]:
        acc = acc * t + c
    tail = acc * t * bell
    cdf = jnp.where(x < 0.0, tail, 1.0 - tail)
    return x * cdf, cdf + x * (bell * (1.0 / math.sqrt(2.0 * math.pi)))


def split_three(v):
    hi = v.astype(BF16).astype(F32)
    rest = v - hi
    mid = rest.astype(BF16).astype(F32)
    return hi, mid, rest - mid


def front_kernel(
    lens, tok, d_in, d_at, d_ff, cot, wq, wo, wu, wd,
    x0_o, ma_o, mf_o, cot_o, wq_o, wo_o, wu_o, wd_o, qkv_o, qb_o, ctx_o,
    xv, xl, wv, qs, ms, tokv, st, qbv, ctxv, in_sem, loc_sem, send_sem, recv_sem, out_sem,
):
    d = lax.axis_index("dp")
    t = lax.axis_index("tensor")
    other = 1 - t
    peer = (d, other)
    loc = tok.shape[0]
    full = 2 * loc
    half_w = wq.shape[1]
    hw = half_w // 3
    pairs = hw // 128

    barrier = pltpu.get_barrier_semaphore()
    pl.semaphore_signal(barrier, inc=1, device_id=peer, device_id_type=MESH)

    loads = [
        pltpu.make_async_copy(tok, tokv, in_sem.at[0]),
        pltpu.make_async_copy(d_in, ms.at[0], in_sem.at[1]),
        pltpu.make_async_copy(wq, wv.at[t], in_sem.at[2]),
        pltpu.make_async_copy(d_at, ms.at[1], in_sem.at[3]),
        pltpu.make_async_copy(d_ff, ms.at[2], in_sem.at[4]),
    ]
    for c in loads:
        c.start()
    own_rows = pl.ds(pl.multiple_of(t * loc, loc), loc)

    local = [
        pltpu.make_async_copy(cot.at[t], cot_o.at[own_rows], loc_sem.at[0]),
        pltpu.make_async_copy(wo, wo_o.at[t], loc_sem.at[1]),
        pltpu.make_async_copy(wu, wu_o.at[t], loc_sem.at[2]),
        pltpu.make_async_copy(wd, wd_o.at[t], loc_sem.at[3]),
        pltpu.make_async_copy(wq, wq_o.at[t], loc_sem.at[4]),
    ]

    def remote(i, src, dst):
        return pltpu.make_async_remote_copy(
            src_ref=src, dst_ref=dst, send_sem=send_sem.at[i], recv_sem=recv_sem.at[i],
            device_id=peer, device_id_type=MESH,
        )

    pl.semaphore_wait(barrier, 1)
    send_wq = remote(0, wq, wv.at[t])
    send_wq.start()
    loads[0].wait()
    loads[1].wait()
    st[0] = jnp.where(ms[0, other] != 0, tokv[...].astype(F32), 0.0).astype(BF16)
    send_x = remote(1, st.at[0], xv.at[own_rows])
    send_x.start()
    own_x = jnp.where(ms[0, t] != 0, tokv[...].astype(F32), 0.0)
    xv[own_rows, :] = own_x.astype(BF16)
    xl[own_rows, :] = (own_x * INV_KEEP).astype(BF16)
    for c in local:
        c.start()
    loads[3].wait()
    st[1] = ms[1, other].astype(F32).astype(BF16)
    st[2] = ms[1, t].astype(F32).astype(BF16)
    loads[4].wait()
    st[3] = ms[2, other].astype(F32).astype(BF16)
    st[4] = ms[2, t].astype(F32).astype(BF16)
    sends = [
        remote(2, wo, wo_o.at[t]),
        remote(3, st.at[1], ma_o.at[own_rows]),
        remote(4, wu, wu_o.at[t]),
        remote(5, wd, wd_o.at[t]),
        remote(6, st.at[3], mf_o.at[own_rows]),
        remote(7, cot.at[other], cot_o.at[own_rows]),
        remote(8, wq, wq_o.at[t]),
    ]
    for c in sends:
        c.start()
    more = [
        pltpu.make_async_copy(st.at[2], ma_o.at[own_rows], loc_sem.at[5]),
        pltpu.make_async_copy(st.at[4], mf_o.at[own_rows], loc_sem.at[6]),
    ]
    for c in more:
        c.start()

    loads[2].wait()
    send_wq.wait_recv()
    send_x.wait_recv()
    oth_rows = pl.ds(pl.multiple_of(other * loc, loc), loc)
    xl[oth_rows, :] = (xv[oth_rows, :].astype(F32) * INV_KEEP).astype(BF16)
    save_x = pltpu.make_async_copy(xv, x0_o, loc_sem.at[7])
    save_x.start()

    for h in range(2):
        for c in range(3):
            def project(b, _, h=h, c=c):
                rows = pl.ds(pl.multiple_of(b * 512, 512), 512)
                qs[h, rows, c * hw : (c + 1) * hw] = dot_nn(
                    xl[rows, :], wv[h, :, c * hw : (c + 1) * hw]
                ).astype(BF16)
                return 0

            lax.fori_loop(0, full // 512, project, 0)
    save_qkv = pltpu.make_async_copy(qs, qkv_o, loc_sem.at[8])
    save_qkv.start()

    length = lens[d]
    bias = jnp.where(
        lax.broadcasted_iota(jnp.int32, (full, 128), 0) < length, 0.0, MASKED_SCORE
    )
    lane = lax.broadcasted_iota(jnp.int32, (full, 128), 1)
    lane_q = lax.broadcasted_iota(jnp.int32, (512, 128), 1)

    def out_copies(i):
        return [
            pltpu.make_async_copy(qbv.at[pl.ds(2 * i, 2)], qb_o.at[pl.ds(2 * i, 2)], out_sem.at[0, i]),
            pltpu.make_async_copy(ctxv.at[i], ctx_o.at[i], out_sem.at[1, i]),
        ]

    def head_pair(i, _):
        h = i // pairs
        off = (i - h * pairs) * 128

        def part(c):
            return qs[h, :, pl.ds(pl.multiple_of(c * hw + off, 128), 128)].astype(F32)

        q2 = part(0) * HEAD_DIM**-0.5
        k2 = part(1)
        v2 = part(2)
        keys, vals, ques = [], [], []
        for a in range(2):
            own = (lane < 64) if a == 0 else (lane >= 64)
            first = 64 if a == 0 else 0
            keys.append(jnp.where(own, k2, jnp.where(lane == first, bias, 0.0)).astype(BF16))
            ques.append(jnp.where(own, q2, jnp.where(lane == first, 1.0, 0.0)).astype(BF16))
            vals.append(jnp.where(own, v2, 1.0).astype(BF16))
        for b in range(full // 512):
            rows = slice(b * 512, (b + 1) * 512)
            tops, outs = [], []
            for a in range(2):
                s = dot_nt(ques[a][rows], keys[a])
                top = jnp.max(s, axis=1, keepdims=True)
                p = jnp.exp(s - top).astype(BF16)
                outs.append(dot_nn(p, vals[a]))
                tops.append(top)
            low_half = lane_q < 64
            num = jnp.where(low_half, outs[0], outs[1])
            den = pltpu.roll(jnp.where(low_half, outs[1], outs[0]), 64, 1)
            ctxv[i, rows, :] = num / den
            for a in range(2):
                hi, mid, lo = split_three(tops[a] + jnp.log(outs[a]))
                own = low_half if a == 0 else jnp.logical_not(low_half)
                first = 64 if a == 0 else 0
                extra = jnp.where(
                    lane_q == first, hi,
                    jnp.where(lane_q == first + 1, mid,
                              jnp.where(lane_q == first + 2, lo,
                                        jnp.where(lane_q == first + 3, 1.0, 0.0))),
                )
                qbv[2 * i + a, rows, :] = jnp.where(own, q2[rows], extra).astype(BF16)
        for c in out_copies(i):
            c.start()
        return 0

    lax.fori_loop(0, 2 * pairs, head_pair, 0)

    def drain(i, _):
        for c in out_copies(i):
            c.wait()
        return 0

    lax.fori_loop(0, 2 * pairs, drain, 0)
    send_wq.wait_send()
    send_x.wait_send()
    for c in sends:
        c.wait()
    for c in local + more + [save_x, save_qkv]:
        c.wait()


def front(lengths, tok, d_in, d_at, d_ff, cot, wq, wo, wu, wd):
    loc, width = tok.shape
    full = 2 * loc
    half_w = wq.shape[1]
    groups = width // 128
    sds = jax.ShapeDtypeStruct
    anyspec = pl.BlockSpec(memory_space=pl.ANY)
    outs = [
        sds((full, width), BF16), sds((full, width), BF16), sds((full, width), BF16),
        sds((full, width), BF16),
        sds((2,) + wq.shape, BF16), sds((2,) + wo.shape, BF16), sds((2,) + wu.shape, BF16),
        sds((2,) + wd.shape, BF16),
        sds((2, full, half_w), BF16), sds((2 * groups, full, 128), BF16),
        sds((groups, full, 128), F32),
    ]
    return pl.pallas_call(
        front_kernel,
        out_shape=outs,
        in_specs=[pl.BlockSpec(memory_space=pltpu.SMEM)] + [anyspec] * 9,
        out_specs=[anyspec] * len(outs),
        scratch_shapes=[
            pltpu.VMEM((full, width), BF16), pltpu.VMEM((full, width), BF16),
            pltpu.VMEM((2,) + wq.shape, BF16), pltpu.VMEM((2, full, half_w), BF16),
            pltpu.VMEM((3, 2, loc, width), jnp.int32), pltpu.VMEM((loc, width), BF16),
            pltpu.VMEM((5, loc, width), BF16),
            pltpu.VMEM((2 * groups, full, 128), BF16), pltpu.VMEM((groups, full, 128), F32),
            pltpu.SemaphoreType.DMA((5,)), pltpu.SemaphoreType.DMA((9,)),
            pltpu.SemaphoreType.DMA((9,)), pltpu.SemaphoreType.DMA((9,)),
            pltpu.SemaphoreType.DMA((2, groups)),
        ],
        compiler_params=pltpu.CompilerParams(
            collective_id=0, has_side_effects=True, vmem_limit_bytes=VMEM_LIMIT
        ),
        name="front",
    )(lengths, tok, d_in, d_at, d_ff, cot, wq, wo, wu, wd)


CH = 512


def middle_kernel(
    lens, lens_b, vecs, ctx, x0, ma, mf, cot, wo, wu, wd,
    lay_o, loss_o, gd_o, gu_o, go_o, ng_o, dr1_o, dob_o,
    ctxv, x0v, mav, mfv, cotv, wov, wuv, wdv,
    n1, n2, rs1, rs2, hl, act, dg, g2, dr2, yb, sbuf, pool_all, gch, uch, dov, facc,
    in_sem, lay_sem, send_sem, recv_sem, ch_sem, out_sem,
):
    d = lax.axis_index("dp")
    t = lax.axis_index("tensor")
    other = 1 - t
    peer = (d, other)
    n_dp = lax.axis_size("dp")
    n_dev = 2 * n_dp
    full, width = x0v.shape
    loc = full // 2
    groups = width // 128
    ff_half = wuv.shape[2]
    n_ch = 2 * ff_half // CH
    per_half = ff_half // CH
    me = d * 2 + t

    barrier = pltpu.get_barrier_semaphore()

    def greet(k, _):
        lin = lax.rem(me + k, n_dev)
        pl.semaphore_signal(
            barrier, inc=1, device_id=(lin // 2, lax.rem(lin, 2)), device_id_type=MESH
        )
        return 0

    lax.fori_loop(1, n_dev, greet, 0)

    srcs = (ctx, wo, x0, ma, wu, wd, mf, cot)
    dsts = (ctxv, wov, x0v, mav, wuv, wdv, mfv, cotv)
    loads = [pltpu.make_async_copy(s, v, in_sem.at[i]) for i, (s, v) in enumerate(zip(srcs, dsts))]
    for c in loads:
        c.start()
    gain1, shift1, gain2, shift2 = (vecs[i : i + 1, :] for i in range(4))
    length = lens[d]

    for c in loads[:4]:
        c.wait()

    def norm_one(b, _):
        rows = pl.ds(pl.multiple_of(b * 256, 256), 256)
        c2 = jnp.concatenate([ctxv[g, rows, :].astype(BF16) for g in range(groups)], axis=1)
        branch = dot_nn(c2, wov[...])
        r = (x0v[rows, :].astype(F32) + branch * mav[rows, :].astype(F32)) * INV_KEEP
        cen = r - jnp.mean(r, axis=1, keepdims=True)
        rstd = lax.rsqrt(jnp.mean(cen * cen, axis=1, keepdims=True) + EPSILON)
        n = cen * rstd
        n1[rows, :] = n
        rs1[rows, :] = jnp.broadcast_to(rstd, (256, 128))
        hl[rows, :] = (n * gain1 + shift1).astype(BF16)
        return 0

    lax.fori_loop(0, full // 256, norm_one, 0)
    for c in loads[4:]:
        c.wait()

    def ffn(b, pooled):
        rows = pl.ds(pl.multiple_of(b * 512, 512), 512)
        for j in range(n_ch):
            h, o = j // per_half, (j % per_half) * CH
            pre = dot_nn(hl[rows, :], wuv[h, :, o : o + CH])
            a, da = gelu_pair(pre)
            ab = a.astype(BF16)
            act[rows, j * CH : (j + 1) * CH] = ab
            dg[rows, j * CH : (j + 1) * CH] = da.astype(BF16)
            term = dot_nn(ab, wdv[j * CH : (j + 1) * CH, :])
            if j == 0:
                facc[...] = term
            else:
                facc[...] += term
        for s in range(2):
            sub = pl.ds(pl.multiple_of(b * 512 + s * 256, 256), 256)
            r = n1[sub, :] * gain1 + shift1 + facc[s * 256 : (s + 1) * 256, :] * (
                mfv[sub, :].astype(F32) * INV_KEEP
            )
            cen = r - jnp.mean(r, axis=1, keepdims=True)
            rstd = lax.rsqrt(jnp.mean(cen * cen, axis=1, keepdims=True) + EPSILON)
            n = cen * rstd
            n2[sub, :] = n
            rs2[sub, :] = jnp.broadcast_to(rstd, (256, 128))
            y = n * gain2 + shift2
            yb[sub, :] = y.astype(BF16)
            pos = lax.broadcasted_iota(jnp.int32, (256, width), 0) + (b * 512 + s * 256)
            pooled = pooled + jnp.sum(jnp.where(pos < length, y, 0.0), axis=0, keepdims=True)
        return pooled

    pooled = lax.fori_loop(0, full // 512, ffn, jnp.zeros((1, width), F32))

    for g in range(groups):
        sbuf[g : g + 1, :] = pooled[:, g * 128 : (g + 1) * 128]
    sbuf[groups:, :] = jnp.zeros((8 - groups, 128), F32)
    slot = t * n_dp + d
    pl.semaphore_wait(barrier, n_dev - 1)

    def push(k, start):
        lin = lax.rem(me + k, n_dev)
        pd, pt = lin // 2, lax.rem(lin, 2)
        c = pltpu.make_async_remote_copy(
            src_ref=sbuf, dst_ref=pool_all.at[slot], send_sem=send_sem.at[k],
            recv_sem=recv_sem.at[slot], device_id=(pd, pt), device_id_type=MESH,
        )
        if start:
            c.start()
        else:
            c.wait_send()
        return 0

    lax.fori_loop(1, n_dev, lambda k, _: push(k, True), 0)
    own_rows = pl.ds(pl.multiple_of(t * loc, loc), loc)
    oth_rows = pl.ds(pl.multiple_of(other * loc, loc), loc)
    lay_local = pltpu.make_async_copy(yb.at[own_rows], lay_o.at[t], lay_sem.at[0])
    lay_local.start()
    lay_send = pltpu.make_async_remote_copy(
        src_ref=yb.at[oth_rows], dst_ref=lay_o.at[t], send_sem=lay_sem.at[1],
        recv_sem=lay_sem.at[2], device_id=peer, device_id_type=MESH,
    )
    lay_send.start()
    pool_all[slot] = sbuf[...]

    def arrive(k, _):
        lin = lax.rem(me + k, n_dev)
        s = lax.rem(lin, 2) * n_dp + lin // 2
        pltpu.make_async_remote_copy(
            src_ref=sbuf, dst_ref=pool_all.at[s], send_sem=send_sem.at[k],
            recv_sem=recv_sem.at[s], device_id=(lin // 2, lax.rem(lin, 2)), device_id_type=MESH,
        ).wait_recv()
        return 0

    lax.fori_loop(1, n_dev, arrive, 0)

    len_col = lens_b[...][:, :1]
    units = []
    scales = []
    for v in range(2):
        raw = jnp.concatenate(
            [pool_all[v * n_dp : (v + 1) * n_dp, g, :] for g in range(groups)], axis=1
        )
        pv = raw / len_col
        scale = lax.rsqrt(jnp.sum(pv * pv, axis=1, keepdims=True) + EPSILON)
        units.append(pv * scale)
        scales.append(scale)
    u0, u1 = units
    nt = (((1,), (1,)), ((), ()))
    row_i = lax.broadcasted_iota(jnp.int32, (n_dp, n_dp), 0)
    col_i = lax.broadcasted_iota(jnp.int32, (n_dp, n_dp), 1)
    diag = row_i == col_i
    sim = lax.dot_general(u0, u1, nt, precision=HIGHEST, preferred_element_type=F32) / SOFTMAX_WARMTH
    top = jnp.max(sim, axis=1, keepdims=True)
    raw = jnp.exp(sim - top)
    total = jnp.sum(raw, axis=1, keepdims=True)
    ce = top + jnp.log(total) - jnp.sum(jnp.where(diag, sim, 0.0), axis=1, keepdims=True)
    loss = jnp.sum(ce, axis=0, keepdims=True) / n_dp
    gap = u0 - u1
    align = jnp.sum(jnp.sum(gap * gap, axis=1, keepdims=True), axis=0, keepdims=True) / n_dp
    sq = jnp.sum(u0 * u0, axis=1, keepdims=True)
    sq_row = lax.dot_general(
        jnp.ones((n_dp, width), F32), u0 * u0, nt, precision=HIGHEST, preferred_element_type=F32
    )
    inner = lax.dot_general(u0, u0, nt, precision=HIGHEST, preferred_element_type=F32)
    pot = jnp.where(diag, 0.0, jnp.exp(-2.0 * (sq + sq_row - 2.0 * inner)))
    uni = jnp.log(
        jnp.sum(jnp.sum(pot, axis=1, keepdims=True), axis=0, keepdims=True) / (n_dp * (n_dp - 1))
    )
    stat_i = lax.broadcasted_iota(jnp.int32, (8, 128), 0)
    loss_o[...] = jnp.where(stat_i == 0, loss, jnp.where(stat_i == 1, align, uni))
    d_sim = (raw / total - jnp.where(diag, 1.0, 0.0)) / SOFTMAX_WARMTH
    d_u0 = jnp.dot(d_sim, u1, precision=HIGHEST, preferred_element_type=F32)
    d_u1 = lax.dot_general(
        d_sim, u0, (((0,), (0,)), ((), ())), precision=HIGHEST, preferred_element_type=F32
    )
    first_view = t == 0
    du = jnp.where(first_view, d_u0, d_u1)
    u = jnp.where(first_view, u0, u1)
    scale = jnp.where(first_view, scales[0], scales[1])
    d_pool = (du - u * jnp.sum(u * du, axis=1, keepdims=True)) * scale / len_col
    mine = lax.broadcasted_iota(jnp.int32, (n_dp, width), 0) == d
    pool_grad = jnp.sum(jnp.where(mine, d_pool, 0.0), axis=0, keepdims=True)

    def norm_two_back(b, sums):
        rows = pl.ds(pl.multiple_of(b * 256, 256), 256)
        pos = lax.broadcasted_iota(jnp.int32, (256, width), 0) + b * 256
        dy = cotv[rows, :].astype(F32) + jnp.where(pos < length, pool_grad, 0.0)
        n = n2[rows, :]
        g = dy * gain2
        dr = (g - jnp.mean(g, axis=1, keepdims=True) - n * jnp.mean(g * n, axis=1, keepdims=True)) * rs2[rows, :1]
        dr2[rows, :] = dr
        g2[rows, :] = (dr * (mfv[rows, :].astype(F32) * INV_KEEP)).astype(BF16)
        return (
            sums[0] + jnp.sum(dy * n, axis=0, keepdims=True),
            sums[1] + jnp.sum(dy, axis=0, keepdims=True),
        )

    zero = jnp.zeros((1, width), F32)
    gg2, gs2 = lax.fori_loop(0, full // 256, norm_two_back, (zero, zero))

    def down_copy(j, s):
        return pltpu.make_async_copy(
            gch.at[s], gd_o.at[pl.ds(pl.multiple_of(j * CH, CH), CH)], ch_sem.at[s]
        )

    for j in range(n_ch):
        s = j % 2
        if j >= 2:
            down_copy(j - 2, s).wait()
        gch[s] = dot_tn(act[:, j * CH : (j + 1) * CH], g2[...]).astype(BF16)
        down_copy(j, s).start()
    for j in range(n_ch - 2, n_ch):
        down_copy(j, j % 2).wait()

    def ffn_back(b, _):
        rows = pl.ds(pl.multiple_of(b * 512, 512), 512)
        for j in range(n_ch):
            h, o = j // per_half, (j % per_half) * CH
            cols = slice(j * CH, (j + 1) * CH)
            da = dot_nt(g2[rows, :], wdv[cols, :])
            dp = (da * dg[rows, cols].astype(F32)).astype(BF16)
            dg[rows, cols] = dp
            dr2[rows, :] += dot_nt(dp, wuv[h, :, o : o + CH])
        return 0

    lax.fori_loop(0, full // 512, ffn_back, 0)

    def up_copy(j):
        h, o = j // per_half, (j % per_half) * CH
        return pltpu.make_async_copy(
            uch.at[j % 2], gu_o.at[h, :, pl.ds(o, CH)], ch_sem.at[2 + j % 2]
        )

    for j in range(n_ch):
        if j >= 2:
            up_copy(j - 2).wait()
        uch[j % 2] = dot_tn(hl[...], dg[:, j * CH : (j + 1) * CH]).astype(BF16)
        up_copy(j).start()
    for j in range(n_ch - 2, n_ch):
        up_copy(j).wait()

    def norm_one_back(b, sums):
        rows = pl.ds(pl.multiple_of(b * 256, 256), 256)
        dh = dr2[rows, :]
        n = n1[rows, :]
        g = dh * gain1
        dr = (g - jnp.mean(g, axis=1, keepdims=True) - n * jnp.mean(g * n, axis=1, keepdims=True)) * rs1[rows, :1]
        dr2[rows, :] = dr
        g2[rows, :] = (dr * (mav[rows, :].astype(F32) * INV_KEEP)).astype(BF16)
        return (
            sums[0] + jnp.sum(dh * n, axis=0, keepdims=True),
            sums[1] + jnp.sum(dh, axis=0, keepdims=True),
        )

    gg1, gs1 = lax.fori_loop(0, full // 256, norm_one_back, (zero, zero))
    save_dr = pltpu.make_async_copy(dr2, dr1_o, out_sem.at[0])
    save_dr.start()
    ng_o[...] = jnp.concatenate([gg1, gs1, gg2, gs2, zero, zero, zero, zero], axis=0)

    lane = lax.broadcasted_iota(jnp.int32, (full, 128), 1)
    seg = (
        (lax.broadcasted_iota(jnp.int32, (128, 128), 0) < 64)
        != (lax.broadcasted_iota(jnp.int32, (128, 128), 1) < 64)
    ).astype(F32).astype(BF16)

    def go_copy(g):
        rows = pl.ds(g * 128, 128)
        return pltpu.make_async_copy(x0v.at[rows], go_o.at[rows], out_sem.at[1 + g])

    def dob_copy(g):
        return pltpu.make_async_copy(
            dov.at[pl.ds(2 * g, 2)], dob_o.at[pl.ds(2 * g, 2)], out_sem.at[1 + groups + g]
        )

    for g in range(groups):
        cf = ctxv[g]
        x0v[g * 128 : (g + 1) * 128, :] = dot_tn(cf.astype(BF16), g2[...]).astype(BF16)
        go_copy(g).start()
        dc = dot_nt(g2[...], wov[g * 128 : (g + 1) * 128, :]).astype(BF16).astype(F32)
        hi, mid, lo = split_three(dc * cf)
        delta = dot_nn(hi.astype(BF16), seg) + dot_nn(mid.astype(BF16), seg) + dot_nn(lo.astype(BF16), seg)
        hi, mid, lo = split_three(delta)
        for a in range(2):
            own = (lane < 64) if a == 0 else (lane >= 64)
            first = 64 if a == 0 else 0
            extra = jnp.where(
                lane == first, hi, jnp.where(lane == first + 1, mid, jnp.where(lane == first + 2, lo, 0.0))
            )
            dov[2 * g + a] = jnp.where(own, dc, extra).astype(BF16)
        dob_copy(g).start()
    for g in range(groups):
        go_copy(g).wait()
        dob_copy(g).wait()
    save_dr.wait()
    lax.fori_loop(1, n_dev, lambda k, _: push(k, False), 0)
    lay_local.wait()
    lay_send.wait()


def middle(lengths, lens_b, vecs, ctx, x0, ma, mf, cot, wo, wu, wd, n_dp):
    full, width = x0.shape
    loc = full // 2
    groups = width // 128
    ff = wd.shape[0]
    n_dev = 2 * n_dp
    sds = jax.ShapeDtypeStruct
    anyspec = pl.BlockSpec(memory_space=pl.ANY)
    vspec = pl.BlockSpec(memory_space=pltpu.VMEM)
    outs = [
        sds((2, loc, width), BF16), sds((8, 128), F32), sds((ff, width), BF16), sds(wu.shape, BF16),
        sds((width, width), BF16), sds((8, width), F32), sds((full, width), F32),
        sds((2 * groups, full, 128), BF16),
    ]
    vm = pltpu.VMEM
    dma = pltpu.SemaphoreType.DMA
    return pl.pallas_call(
        middle_kernel,
        out_shape=outs,
        in_specs=[pl.BlockSpec(memory_space=pltpu.SMEM), vspec, vspec] + [anyspec] * 8,
        out_specs=[anyspec, vspec, anyspec, anyspec, anyspec, vspec, anyspec, anyspec],
        scratch_shapes=[
            vm(ctx.shape, F32), vm((full, width), BF16), vm((full, width), BF16),
            vm((full, width), BF16), vm((full, width), BF16), vm(wo.shape, BF16),
            vm(wu.shape, BF16), vm(wd.shape, BF16),
            vm((full, width), F32), vm((full, width), F32), vm((full, 128), F32), vm((full, 128), F32),
            vm((full, width), BF16), vm((full, ff), BF16), vm((full, ff), BF16),
            vm((full, width), BF16), vm((full, width), F32), vm((full, width), BF16),
            vm((8, 128), F32), vm((n_dev, 8, 128), F32), vm((2, CH, width), BF16),
            vm((2, width, CH), BF16), vm((2 * groups, full, 128), BF16), vm((512, width), F32),
            dma((8,)), dma((3,)), dma((n_dev,)), dma((n_dev,)), dma((4,)), dma((1 + 2 * groups,)),
        ],
        compiler_params=pltpu.CompilerParams(
            collective_id=1, has_side_effects=True, vmem_limit_bytes=VMEM_LIMIT
        ),
        name="middle",
    )(lengths, lens_b, vecs, ctx, x0, ma, mf, cot, wo, wu, wd)


def back_kernel(
    lens, qb, dob, qkv, wq, x0, dr1, d_in,
    gq_o, gt_o,
    qbv, dobv, qkvv, wqv, xv, xt, drv, dinv, dq3, acc, gch, stage, got, gtv,
    in_sem, ch_sem, send_sem,
):
    d = lax.axis_index("dp")
    t = lax.axis_index("tensor")
    other = 1 - t
    peer = (d, other)
    full, width = xv.shape
    loc = full // 2
    half_w = qkvv.shape[2]
    hw = half_w // 3
    pairs = hw // 128

    barrier = pltpu.get_barrier_semaphore()
    pl.semaphore_signal(barrier, inc=1, device_id=peer, device_id_type=MESH)
    srcs = (qb, dob, qkv, x0, wq, dr1, d_in)
    dsts = (qbv, dobv, qkvv, xv, wqv, drv, dinv)
    loads = [pltpu.make_async_copy(s, v, in_sem.at[i]) for i, (s, v) in enumerate(zip(srcs, dsts))]
    for c in loads:
        c.start()
    length = lens[d]
    lane = lax.broadcasted_iota(jnp.int32, (full, 128), 1)
    bias = jnp.where(
        lax.broadcasted_iota(jnp.int32, (full, 128), 0) < length, 0.0, MASKED_SCORE
    )
    for c in loads[:3]:
        c.wait()
    kb = 512

    def head_pair(i, _):
        h = i // pairs
        off = (i - h * pairs) * 128

        def part(c):
            return qkvv[h, :, pl.ds(pl.multiple_of(c * hw + off, 128), 128)]

        k2 = part(1)
        k2f = k2.astype(F32)
        k2t = k2f.T.astype(BF16)
        v2f = part(2).astype(F32)
        dks, dvs, dqs = [], [], []
        for a in range(2):
            own = (lane < 64) if a == 0 else (lane >= 64)
            first = 64 if a == 0 else 0
            lane3 = jnp.logical_and(lane >= first, lane < first + 3)
            minus = jnp.where(lane3, -1.0, 0.0)
            ka = jnp.where(own, k2f, jnp.where(lane == first + 3, bias, minus)).astype(BF16)
            va = jnp.where(own, v2f, minus).astype(BF16)
            qa = qbv[2 * i + a]
            da = dobv[2 * i + a]
            dk, dv = [], []
            dqt = None
            for b in range(full // kb):
                rows = slice(b * kb, (b + 1) * kb)
                p = jnp.exp(dot_nt(ka[rows], qa))
                ds = (p * dot_nt(va[rows], da)).astype(BF16)
                dv.append(dot_nn(p.astype(BF16), da))
                dk.append(dot_nn(ds, qa))
                term = dot_nn(k2t[a * 64 : (a + 1) * 64, rows], ds)
                dqt = term if dqt is None else dqt + term
            dks.append(dk)
            dvs.append(dv)
            dqs.append(dqt)
        low_half = lax.broadcasted_iota(jnp.int32, (kb, 128), 1) < 64
        for b in range(full // kb):
            rows = slice(b * kb, (b + 1) * kb)
            dq3[h, rows, pl.ds(pl.multiple_of(hw + off, 128), 128)] = jnp.where(
                low_half, dks[0][b], dks[1][b]
            ).astype(BF16)
            dq3[h, rows, pl.ds(pl.multiple_of(2 * hw + off, 128), 128)] = jnp.where(
                low_half, dvs[0][b], dvs[1][b]
            ).astype(BF16)
        dq = jnp.concatenate(dqs, axis=0) * HEAD_DIM**-0.5
        dq3[h, :, pl.ds(pl.multiple_of(off, 128), 128)] = dq.T.astype(BF16)
        return 0

    lax.fori_loop(0, 2 * pairs, head_pair, 0)
    for c in loads[3:]:
        c.wait()

    pl.semaphore_wait(barrier, 1)
    own_rows = pl.ds(pl.multiple_of(t * loc, loc), loc)
    oth_rows = pl.ds(pl.multiple_of(other * loc, loc), loc)

    def d_input(rows):
        return dot_nt(dq3[0, rows, :], wqv[0]) + dot_nt(dq3[1, rows, :], wqv[1]) + drv[rows, :]

    for s in range(loc // 256):
        stage[s * 256 : (s + 1) * 256, :] = d_input(
            pl.ds(pl.multiple_of(other * loc + s * 256, 256), 256)
        ).astype(BF16)
    send = pltpu.make_async_remote_copy(
        src_ref=stage, dst_ref=got, send_sem=send_sem.at[0], recv_sem=send_sem.at[1],
        device_id=peer, device_id_type=MESH,
    )
    send.start()
    for s in range(loc // 256):
        acc[s * 256 : (s + 1) * 256, :] = d_input(
            pl.ds(pl.multiple_of(t * loc + s * 256, 256), 256)
        )
    for c in range(width // 256):
        cols = slice(c * 256, (c + 1) * 256)
        xt[cols, :] = (xv[:, cols].astype(F32) * INV_KEEP).T.astype(BF16)

    def q_copy(j):
        h, o = j // 3, (j % 3) * hw
        return pltpu.make_async_copy(gch.at[j % 2], gq_o.at[h, :, pl.ds(o, hw)], ch_sem.at[j % 2])

    for j in range(6):
        h, o = j // 3, (j % 3) * hw
        if j >= 2:
            q_copy(j - 2).wait()
        gch[j % 2] = dot_nn(xt[...], dq3[h, :, o : o + hw]).astype(BF16)
        q_copy(j).start()
    send.wait()
    for s in range(loc // 256):
        rows = slice(s * 256, (s + 1) * 256)
        gtv[rows, :] = (
            jnp.where(dinv[t, rows, :] != 0, acc[rows, :], 0.0)
            + jnp.where(dinv[other, rows, :] != 0, got[rows, :].astype(F32), 0.0)
        ) * INV_KEEP
    out = pltpu.make_async_copy(gtv, gt_o, ch_sem.at[2])
    out.start()
    for j in range(4, 6):
        q_copy(j).wait()
    out.wait()


def back(lengths, qb, dob, qkv, wq, x0, dr1, d_in):
    full, width = x0.shape
    loc = full // 2
    half_w = qkv.shape[2]
    sds = jax.ShapeDtypeStruct
    anyspec = pl.BlockSpec(memory_space=pl.ANY)
    vm = pltpu.VMEM
    dma = pltpu.SemaphoreType.DMA
    return pl.pallas_call(
        back_kernel,
        out_shape=[sds(wq.shape, BF16), sds((loc, width), F32)],
        in_specs=[pl.BlockSpec(memory_space=pltpu.SMEM)] + [anyspec] * 7,
        out_specs=[anyspec, anyspec],
        scratch_shapes=[
            vm(qb.shape, BF16), vm(dob.shape, BF16), vm(qkv.shape, BF16), vm(wq.shape, BF16),
            vm(x0.shape, BF16), vm((width, full), BF16), vm(dr1.shape, F32), vm(d_in.shape, jnp.int32),
            vm(qkv.shape, BF16), vm((loc, width), F32), vm((2, width, half_w // 3), BF16),
            vm((loc, width), BF16), vm((loc, width), BF16), vm((loc, width), F32),
            dma((7,)), dma((3,)), dma((2,)),
        ],
        compiler_params=pltpu.CompilerParams(
            collective_id=2, has_side_effects=True, vmem_limit_bytes=VMEM_LIMIT
        ),
        name="back",
    )(lengths, qb, dob, qkv, wq, x0, dr1, d_in)


def per_device(
    tokens, lengths, drop_in, drop_attn, drop_ffn, qkv_weight, out_weight, up_weight, down_weight,
    gain_first, shift_first, gain_second, shift_second, cotangent,
):
    n_dp = lax.axis_size("dp")
    width = tokens.shape[2]
    wq = qkv_weight.reshape(width, -1)
    x0, ma, mf, cot, wqf, wof, wuf, wdf, qkv, qb, ctx = front(
        lengths, tokens[0], drop_in[0], drop_attn[0], drop_ffn[0], cotangent[0],
        wq, out_weight, up_weight, down_weight,
    )
    lens_b = jnp.broadcast_to(lengths.astype(F32)[:, None], (n_dp, 128))
    vecs = jnp.stack([gain_first, shift_first, gain_second, shift_second] * 2)
    lay, stats, gd, gu, go, ng, dr1, dob = middle(
        lengths, lens_b, vecs, ctx, x0, ma, mf, cot,
        wof.reshape(width, width), wuf, wdf.reshape(-1, width), n_dp,
    )
    gq, gt = back(lengths, qb, dob, qkv, wqf, x0, dr1, drop_in[0])
    halves = [
        gq, go.reshape(2, -1, width), gu, gd.reshape(2, -1, width),
    ]
    summed = []
    for g in halves:
        g = lax.psum_scatter(g, "tensor", scatter_dimension=0, tiled=False)
        summed.append(lax.psum(g, "dp").astype(F32))
    norms = lax.psum(ng, ("dp", "tensor"))
    return (
        lay[None], gt[None],
        summed[0].reshape(qkv_weight.shape), summed[1], summed[2], summed[3],
        norms[0], norms[1], norms[2], norms[3],
        stats[0, 0], stats[1, 0], stats[2, 0],
    )


def solution(mesh):
    act = P("dp", None, "tensor", None)
    in_specs = (
        P("dp", "tensor", None), P(), act, act, act,
        P(None, None, "tensor"), P("tensor", None), P(None, "tensor"), P("tensor", None),
        P(), P(), P(), P(), act,
    )
    out_specs = (
        act, P("dp", "tensor", None),
        P(None, None, "tensor"), P("tensor", None), P(None, "tensor"), P("tensor", None),
        P(), P(), P(), P(), P(), P(), P(),
    )
    return jax.shard_map(
        per_device, mesh=mesh, in_specs=in_specs, out_specs=out_specs, check_vma=False
    )
```

```python
import functools
import math

import jax
import jax.numpy as jnp
from jax import lax
from jax.experimental import pallas as pl
from jax.experimental.pallas import tpu as pltpu
from jax.sharding import PartitionSpec as P

HEAD_DIM = 64
INV_KEEP = 1.0 / 0.9
SOFTMAX_WARMTH = 0.05
EPSILON = 1e-06
MASKED_SCORE = -1e30
MESH = pl.DeviceIdType.MESH
F32 = jnp.float32
BF16 = jnp.bfloat16
VMEM_LIMIT = 60 * 2**20
HIGHEST = lax.Precision.HIGHEST

TAIL_P = 0.3
TAIL = (
    0.11962929778234735,
    0.12075397394392673,
    0.09991336806236217,
    0.1285620774207718,
    -0.05368457414666341,
    0.20635459819946347,
    -0.15720376083821283,
    0.03567494667807555,
)


def dot_nn(a, b):
    return jnp.dot(a, b, preferred_element_type=F32)


def dot_nt(a, b):
    return lax.dot_general(a, b, (((1,), (1,)), ((), ())), preferred_element_type=F32)


def dot_tn(a, b):
    return lax.dot_general(a, b, (((0,), (0,)), ((), ())), preferred_element_type=F32)


def gelu_pair(x):
    z = jnp.abs(x)
    bell = jnp.exp(x * x * -0.5)
    t = 1.0 / (1.0 + TAIL_P * z)
    acc = jnp.full_like(t, TAIL[-1])
    for c in TAIL[-2::-1]:
        acc = acc * t + c
    tail = acc * t * bell
    cdf = jnp.where(x < 0.0, tail, 1.0 - tail)
    return x * cdf, cdf + x * (bell * (1.0 / math.sqrt(2.0 * math.pi)))


def split_three(v):
    hi = v.astype(BF16).astype(F32)
    rest = v - hi
    mid = rest.astype(BF16).astype(F32)
    return hi, mid, rest - mid


def front_kernel(
    lens, tok, d_in, d_at, d_ff, cot, wq, wo, wu, wd,
    x0_o, ma_o, mf_o, cot_o, wq_o, wo_o, wu_o, wd_o, qkv_o, qb_o, ctx_o,
    xv, xl, wv, qs, ms, tokv, st, qbv, ctxv, in_sem, loc_sem, send_sem, recv_sem, out_sem,
):
    d = lax.axis_index("dp")
    t = lax.axis_index("tensor")
    other = 1 - t
    peer = (d, other)
    loc = tok.shape[0]
    full = 2 * loc
    half_w = wq.shape[1]
    hw = half_w // 3
    pairs = hw // 128

    barrier = pltpu.get_barrier_semaphore()
    pl.semaphore_signal(barrier, inc=1, device_id=peer, device_id_type=MESH)

    loads = [
        pltpu.make_async_copy(tok, tokv, in_sem.at[0]),
        pltpu.make_async_copy(d_in, ms.at[0], in_sem.at[1]),
        pltpu.make_async_copy(wq, wv.at[t], in_sem.at[2]),
        pltpu.make_async_copy(d_at, ms.at[1], in_sem.at[3]),
        pltpu.make_async_copy(d_ff, ms.at[2], in_sem.at[4]),
    ]
    for c in loads:
        c.start()
    own_rows = pl.ds(pl.multiple_of(t * loc, loc), loc)

    def remote(i, src, dst):
        return pltpu.make_async_remote_copy(
            src_ref=src, dst_ref=dst, send_sem=send_sem.at[i], recv_sem=recv_sem.at[i],
            device_id=peer, device_id_type=MESH,
        )

    pl.semaphore_wait(barrier, 1)
    send_wq = remote(0, wq, wv.at[t])
    send_wq.start()
    loads[0].wait()
    loads[1].wait()
    st[0] = jnp.where(ms[0, other] != 0, tokv[...].astype(F32), 0.0).astype(BF16)
    send_x = remote(1, st.at[0], xv.at[own_rows])
    send_x.start()
    own_x = jnp.where(ms[0, t] != 0, tokv[...].astype(F32), 0.0)
    xv[own_rows, :] = own_x.astype(BF16)
    xl[own_rows, :] = (own_x * INV_KEEP).astype(BF16)
    loads[3].wait()
    st[1] = ms[1, other].astype(F32).astype(BF16)
    st[2] = ms[1, t].astype(F32).astype(BF16)
    loads[4].wait()
    st[3] = ms[2, other].astype(F32).astype(BF16)
    st[4] = ms[2, t].astype(F32).astype(BF16)
    sends = [
        remote(2, wo, wo_o),
        remote(3, st.at[1], ma_o.at[own_rows]),
        remote(4, wu, wu_o),
        remote(5, wd, wd_o),
        remote(6, st.at[3], mf_o.at[own_rows]),
        remote(7, cot.at[other], cot_o),
    ]
    for c in sends:
        c.start()
    more = [
        pltpu.make_async_copy(st.at[2], ma_o.at[own_rows], loc_sem.at[0]),
        pltpu.make_async_copy(st.at[4], mf_o.at[own_rows], loc_sem.at[1]),
    ]
    for c in more:
        c.start()

    loads[2].wait()
    send_wq.wait_recv()
    send_x.wait_recv()
    oth_rows = pl.ds(pl.multiple_of(other * loc, loc), loc)
    xl[oth_rows, :] = (xv[oth_rows, :].astype(F32) * INV_KEEP).astype(BF16)
    save_x = pltpu.make_async_copy(xv, x0_o, loc_sem.at[2])
    save_x.start()
    save_w = pltpu.make_async_copy(wv, wq_o, loc_sem.at[3])
    save_w.start()

    for h in range(2):
        for c in range(3):
            def project(b, _, h=h, c=c):
                rows = pl.ds(pl.multiple_of(b * 512, 512), 512)
                qs[h, rows, c * hw : (c + 1) * hw] = dot_nn(
                    xl[rows, :], wv[h, :, c * hw : (c + 1) * hw]
                ).astype(BF16)
                return 0

            lax.fori_loop(0, full // 512, project, 0)
    save_qkv = pltpu.make_async_copy(qs, qkv_o, loc_sem.at[4])
    save_qkv.start()

    length = lens[d]
    bias = jnp.where(
        lax.broadcasted_iota(jnp.int32, (full, 128), 0) < length, 0.0, MASKED_SCORE
    )
    lane = lax.broadcasted_iota(jnp.int32, (full, 128), 1)
    lane_q = lax.broadcasted_iota(jnp.int32, (512, 128), 1)

    def out_copies(i):
        return [
            pltpu.make_async_copy(qbv.at[pl.ds(2 * i, 2)], qb_o.at[pl.ds(2 * i, 2)], out_sem.at[0, i]),
            pltpu.make_async_copy(ctxv.at[i], ctx_o.at[i], out_sem.at[1, i]),
        ]

    def head_pair(i, _):
        h = i // pairs
        off = (i - h * pairs) * 128

        def part(c):
            return qs[h, :, pl.ds(pl.multiple_of(c * hw + off, 128), 128)].astype(F32)

        q2 = part(0) * HEAD_DIM**-0.5
        k2 = part(1)
        v2 = part(2)
        keys, vals, ques = [], [], []
        for a in range(2):
            own = (lane < 64) if a == 0 else (lane >= 64)
            first = 64 if a == 0 else 0
            keys.append(jnp.where(own, k2, jnp.where(lane == first, bias, 0.0)).astype(BF16))
            ques.append(jnp.where(own, q2, jnp.where(lane == first, 1.0, 0.0)).astype(BF16))
            vals.append(jnp.where(own, v2, 1.0).astype(BF16))
        for b in range(full // 512):
            rows = slice(b * 512, (b + 1) * 512)
            tops, outs = [], []
            for a in range(2):
                s = dot_nt(ques[a][rows], keys[a])
                top = jnp.max(s, axis=1, keepdims=True)
                p = jnp.exp(s - top).astype(BF16)
                outs.append(dot_nn(p, vals[a]))
                tops.append(top)
            low_half = lane_q < 64
            num = jnp.where(low_half, outs[0], outs[1])
            den = pltpu.roll(jnp.where(low_half, outs[1], outs[0]), 64, 1)
            ctxv[i, rows, :] = num / den
            for a in range(2):
                hi, mid, lo = split_three(tops[a] + jnp.log(outs[a]))
                own = low_half if a == 0 else jnp.logical_not(low_half)
                first = 64 if a == 0 else 0
                extra = jnp.where(
                    lane_q == first, hi,
                    jnp.where(lane_q == first + 1, mid,
                              jnp.where(lane_q == first + 2, lo,
                                        jnp.where(lane_q == first + 3, 1.0, 0.0))),
                )
                qbv[2 * i + a, rows, :] = jnp.where(own, q2[rows], extra).astype(BF16)
        for c in out_copies(i):
            c.start()
        return 0

    lax.fori_loop(0, 2 * pairs, head_pair, 0)

    def drain(i, _):
        for c in out_copies(i):
            c.wait()
        return 0

    lax.fori_loop(0, 2 * pairs, drain, 0)
    send_wq.wait_send()
    send_x.wait_send()
    for c in sends:
        c.wait()
    for c in more + [save_x, save_w, save_qkv]:
        c.wait()


def front(lengths, tok, d_in, d_at, d_ff, cot, wq, wo, wu, wd):
    loc, width = tok.shape
    full = 2 * loc
    half_w = wq.shape[1]
    groups = width // 128
    sds = jax.ShapeDtypeStruct
    anyspec = pl.BlockSpec(memory_space=pl.ANY)
    outs = [
        sds((full, width), BF16), sds((full, width), BF16), sds((full, width), BF16),
        sds((loc, width), BF16),
        sds((2,) + wq.shape, BF16), sds(wo.shape, BF16), sds(wu.shape, BF16), sds(wd.shape, BF16),
        sds((2, full, half_w), BF16), sds((2 * groups, full, 128), BF16),
        sds((groups, full, 128), F32),
    ]
    return pl.pallas_call(
        front_kernel,
        out_shape=outs,
        in_specs=[pl.BlockSpec(memory_space=pltpu.SMEM)] + [anyspec] * 9,
        out_specs=[anyspec] * len(outs),
        scratch_shapes=[
            pltpu.VMEM((full, width), BF16), pltpu.VMEM((full, width), BF16),
            pltpu.VMEM((2,) + wq.shape, BF16), pltpu.VMEM((2, full, half_w), BF16),
            pltpu.VMEM((3, 2, loc, width), jnp.int32), pltpu.VMEM((loc, width), BF16),
            pltpu.VMEM((5, loc, width), BF16),
            pltpu.VMEM((2 * groups, full, 128), BF16), pltpu.VMEM((groups, full, 128), F32),
            pltpu.SemaphoreType.DMA((5,)), pltpu.SemaphoreType.DMA((5,)),
            pltpu.SemaphoreType.DMA((8,)), pltpu.SemaphoreType.DMA((8,)),
            pltpu.SemaphoreType.DMA((2, groups)),
        ],
        compiler_params=pltpu.CompilerParams(
            collective_id=0, has_side_effects=True, vmem_limit_bytes=VMEM_LIMIT
        ),
        name="front",
    )(lengths, tok, d_in, d_at, d_ff, cot, wq, wo, wu, wd)


CH = 512


def middle_kernel(
    lens, lens_b, vecs, ctx, x0, ma, mf, cot, cot_p, wo, wo_p, wu, wu_p, wd, wd_p,
    lay_o, loss_o, act_o, dg_o, hl_o, n1_o, rs1_o, g2_o, dr2_o, ng_o,
    ctxv, x0v, mav, mfv, cotv, wov, wuv, wdv,
    n1, n2, rs1, rs2, hl, act, dg, g2, dr2, yb, sbuf, pool_all, facc,
    in_sem, lay_sem, send_sem, recv_sem, row_sem, out_sem,
):
    d = lax.axis_index("dp")
    t = lax.axis_index("tensor")
    other = 1 - t
    peer = (d, other)
    n_dp = lax.axis_size("dp")
    n_dev = 2 * n_dp
    full, width = x0v.shape
    loc = full // 2
    groups = width // 128
    ff_half = wuv.shape[2]
    n_ch = 2 * ff_half // CH
    per_half = ff_half // CH
    me = d * 2 + t

    barrier = pltpu.get_barrier_semaphore()

    def greet(k, _):
        lin = lax.rem(me + k, n_dev)
        pl.semaphore_signal(
            barrier, inc=1, device_id=(lin // 2, lax.rem(lin, 2)), device_id_type=MESH
        )
        return 0

    lax.fori_loop(1, n_dev, greet, 0)

    own_rows = pl.ds(pl.multiple_of(t * loc, loc), loc)
    oth_rows = pl.ds(pl.multiple_of(other * loc, loc), loc)
    srcs = (ctx, wo, wo_p, x0, ma, wu, wu_p, wd, wd_p, mf, cot.at[t], cot_p)
    dsts = (
        ctxv, wov.at[t], wov.at[other], x0v, mav, wuv.at[t], wuv.at[other], wdv.at[t],
        wdv.at[other], mfv, cotv.at[own_rows], cotv.at[oth_rows],
    )
    loads = [pltpu.make_async_copy(s, v, in_sem.at[i]) for i, (s, v) in enumerate(zip(srcs, dsts))]
    for c in loads:
        c.start()
    gain1, shift1, gain2, shift2 = (vecs[i : i + 1, :] for i in range(4))
    length = lens[d]

    for c in loads[:5]:
        c.wait()

    def norm_one(b, _):
        rows = pl.ds(pl.multiple_of(b * 256, 256), 256)
        c2 = jnp.concatenate([ctxv[g, rows, :].astype(BF16) for g in range(groups)], axis=1)
        branch = dot_nn(c2, wov[...].reshape(width, width))
        r = (x0v[rows, :].astype(F32) + branch * mav[rows, :].astype(F32)) * INV_KEEP
        cen = r - jnp.mean(r, axis=1, keepdims=True)
        rstd = lax.rsqrt(jnp.mean(cen * cen, axis=1, keepdims=True) + EPSILON)
        n = cen * rstd
        n1[rows, :] = n
        rs1[rows, :] = jnp.broadcast_to(rstd, (256, 128))
        hl[rows, :] = (n * gain1 + shift1).astype(BF16)
        return 0

    lax.fori_loop(0, full // 256, norm_one, 0)
    saves = [
        pltpu.make_async_copy(s, o, out_sem.at[i])
        for i, (s, o) in enumerate(((hl, hl_o), (n1, n1_o), (rs1, rs1_o)))
    ]
    for c in saves:
        c.start()
    for c in loads[5:]:
        c.wait()

    def row_copies(b):
        rows = pl.ds(pl.multiple_of(b * 512, 512), 512)
        return [
            pltpu.make_async_copy(act.at[rows], act_o.at[rows], row_sem.at[b, 0]),
            pltpu.make_async_copy(dg.at[rows], dg_o.at[rows], row_sem.at[b, 1]),
        ]

    def ffn(b, pooled):
        rows = pl.ds(pl.multiple_of(b * 512, 512), 512)
        for j in range(n_ch):
            h, o = j // per_half, (j % per_half) * CH
            pre = dot_nn(hl[rows, :], wuv[h, :, o : o + CH])
            a, da = gelu_pair(pre)
            ab = a.astype(BF16)
            act[rows, j * CH : (j + 1) * CH] = ab
            dg[rows, j * CH : (j + 1) * CH] = da.astype(BF16)
            term = dot_nn(ab, wdv[h, o : o + CH, :])
            if j == 0:
                facc[...] = term
            else:
                facc[...] += term
        for c in row_copies(b):
            c.start()
        for s in range(2):
            sub = pl.ds(pl.multiple_of(b * 512 + s * 256, 256), 256)
            r = n1[sub, :] * gain1 + shift1 + facc[s * 256 : (s + 1) * 256, :] * (
                mfv[sub, :].astype(F32) * INV_KEEP
            )
            cen = r - jnp.mean(r, axis=1, keepdims=True)
            rstd = lax.rsqrt(jnp.mean(cen * cen, axis=1, keepdims=True) + EPSILON)
            n = cen * rstd
            n2[sub, :] = n
            rs2[sub, :] = jnp.broadcast_to(rstd, (256, 128))
            y = n * gain2 + shift2
            yb[sub, :] = y.astype(BF16)
            pos = lax.broadcasted_iota(jnp.int32, (256, width), 0) + (b * 512 + s * 256)
            pooled = pooled + jnp.sum(jnp.where(pos < length, y, 0.0), axis=0, keepdims=True)
        return pooled

    pooled = lax.fori_loop(0, full // 512, ffn, jnp.zeros((1, width), F32))

    for g in range(groups):
        sbuf[g : g + 1, :] = pooled[:, g * 128 : (g + 1) * 128]
    sbuf[groups:, :] = jnp.zeros((8 - groups, 128), F32)
    slot = t * n_dp + d
    pl.semaphore_wait(barrier, n_dev - 1)

    def push(k, start):
        lin = lax.rem(me + k, n_dev)
        pd, pt = lin // 2, lax.rem(lin, 2)
        c = pltpu.make_async_remote_copy(
            src_ref=sbuf, dst_ref=pool_all.at[slot], send_sem=send_sem.at[k],
            recv_sem=recv_sem.at[slot], device_id=(pd, pt), device_id_type=MESH,
        )
        if start:
            c.start()
        else:
            c.wait_send()
        return 0

    lax.fori_loop(1, n_dev, lambda k, _: push(k, True), 0)
    lay_local = pltpu.make_async_copy(yb.at[own_rows], lay_o.at[t], lay_sem.at[0])
    lay_local.start()
    lay_send = pltpu.make_async_remote_copy(
        src_ref=yb.at[oth_rows], dst_ref=lay_o.at[t], send_sem=lay_sem.at[1],
        recv_sem=lay_sem.at[2], device_id=peer, device_id_type=MESH,
    )
    lay_send.start()
    pool_all[slot] = sbuf[...]

    def arrive(k, _):
        lin = lax.rem(me + k, n_dev)
        s = lax.rem(lin, 2) * n_dp + lin // 2
        pltpu.make_async_remote_copy(
            src_ref=sbuf, dst_ref=pool_all.at[s], send_sem=send_sem.at[k],
            recv_sem=recv_sem.at[s], device_id=(lin // 2, lax.rem(lin, 2)), device_id_type=MESH,
        ).wait_recv()
        return 0

    lax.fori_loop(1, n_dev, arrive, 0)

    len_col = lens_b[...][:, :1]
    units = []
    scales = []
    for v in range(2):
        raw = jnp.concatenate(
            [pool_all[v * n_dp : (v + 1) * n_dp, g, :] for g in range(groups)], axis=1
        )
        pv = raw / len_col
        scale = lax.rsqrt(jnp.sum(pv * pv, axis=1, keepdims=True) + EPSILON)
        units.append(pv * scale)
        scales.append(scale)
    u0, u1 = units
    nt = (((1,), (1,)), ((), ()))
    row_i = lax.broadcasted_iota(jnp.int32, (n_dp, n_dp), 0)
    col_i = lax.broadcasted_iota(jnp.int32, (n_dp, n_dp), 1)
    diag = row_i == col_i
    sim = lax.dot_general(u0, u1, nt, precision=HIGHEST, preferred_element_type=F32) / SOFTMAX_WARMTH
    top = jnp.max(sim, axis=1, keepdims=True)
    raw = jnp.exp(sim - top)
    total = jnp.sum(raw, axis=1, keepdims=True)
    ce = top + jnp.log(total) - jnp.sum(jnp.where(diag, sim, 0.0), axis=1, keepdims=True)
    loss = jnp.sum(ce, axis=0, keepdims=True) / n_dp
    gap = u0 - u1
    align = jnp.sum(jnp.sum(gap * gap, axis=1, keepdims=True), axis=0, keepdims=True) / n_dp
    sq = jnp.sum(u0 * u0, axis=1, keepdims=True)
    sq_row = lax.dot_general(
        jnp.ones((n_dp, width), F32), u0 * u0, nt, precision=HIGHEST, preferred_element_type=F32
    )
    inner = lax.dot_general(u0, u0, nt, precision=HIGHEST, preferred_element_type=F32)
    pot = jnp.where(diag, 0.0, jnp.exp(-2.0 * (sq + sq_row - 2.0 * inner)))
    uni = jnp.log(
        jnp.sum(jnp.sum(pot, axis=1, keepdims=True), axis=0, keepdims=True) / (n_dp * (n_dp - 1))
    )
    stat_i = lax.broadcasted_iota(jnp.int32, (8, 128), 0)
    loss_o[...] = jnp.where(stat_i == 0, loss, jnp.where(stat_i == 1, align, uni))
    d_sim = (raw / total - jnp.where(diag, 1.0, 0.0)) / SOFTMAX_WARMTH
    d_u0 = jnp.dot(d_sim, u1, precision=HIGHEST, preferred_element_type=F32)
    d_u1 = lax.dot_general(
        d_sim, u0, (((0,), (0,)), ((), ())), precision=HIGHEST, preferred_element_type=F32
    )
    first_view = t == 0
    du = jnp.where(first_view, d_u0, d_u1)
    u = jnp.where(first_view, u0, u1)
    scale = jnp.where(first_view, scales[0], scales[1])
    d_pool = (du - u * jnp.sum(u * du, axis=1, keepdims=True)) * scale / len_col
    mine = lax.broadcasted_iota(jnp.int32, (n_dp, width), 0) == d
    pool_grad = jnp.sum(jnp.where(mine, d_pool, 0.0), axis=0, keepdims=True)

    def norm_two_back(b, sums):
        rows = pl.ds(pl.multiple_of(b * 256, 256), 256)
        pos = lax.broadcasted_iota(jnp.int32, (256, width), 0) + b * 256
        dy = cotv[rows, :].astype(F32) + jnp.where(pos < length, pool_grad, 0.0)
        n = n2[rows, :]
        g = dy * gain2
        dr = (g - jnp.mean(g, axis=1, keepdims=True) - n * jnp.mean(g * n, axis=1, keepdims=True)) * rs2[rows, :1]
        dr2[rows, :] = dr
        g2[rows, :] = (dr * (mfv[rows, :].astype(F32) * INV_KEEP)).astype(BF16)
        return (
            sums[0] + jnp.sum(dy * n, axis=0, keepdims=True),
            sums[1] + jnp.sum(dy, axis=0, keepdims=True),
        )

    zero = jnp.zeros((1, width), F32)
    gg2, gs2 = lax.fori_loop(0, full // 256, norm_two_back, (zero, zero))

    ng_o[...] = jnp.concatenate([gg2, gs2, zero, zero, zero, zero, zero, zero], axis=0)
    more = [
        pltpu.make_async_copy(g2, g2_o, out_sem.at[3]),
        pltpu.make_async_copy(dr2, dr2_o, out_sem.at[4]),
    ]
    for c in more:
        c.start()
    for b in range(full // 512):
        for c in row_copies(b):
            c.wait()
    lax.fori_loop(1, n_dev, lambda k, _: push(k, False), 0)
    lay_local.wait()
    lay_send.wait()
    for c in saves + more:
        c.wait()


def middle(lengths, lens_b, vecs, ctx, x0, ma, mf, cot, cot_p, wo, wo_p, wu, wu_p, wd, wd_p, n_dp):
    full, width = x0.shape
    loc = full // 2
    ff = 2 * wd.shape[0]
    n_dev = 2 * n_dp
    sds = jax.ShapeDtypeStruct
    anyspec = pl.BlockSpec(memory_space=pl.ANY)
    vspec = pl.BlockSpec(memory_space=pltpu.VMEM)
    outs = [
        sds((2, loc, width), BF16), sds((8, 128), F32), sds((full, ff), BF16), sds((full, ff), BF16),
        sds((full, width), BF16), sds((full, width), F32), sds((full, 128), F32),
        sds((full, width), BF16), sds((full, width), F32), sds((8, width), F32),
    ]
    vm = pltpu.VMEM
    dma = pltpu.SemaphoreType.DMA
    return pl.pallas_call(
        middle_kernel,
        out_shape=outs,
        in_specs=[pl.BlockSpec(memory_space=pltpu.SMEM), vspec, vspec] + [anyspec] * 12,
        out_specs=[anyspec, vspec] + [anyspec] * 7 + [vspec],
        scratch_shapes=[
            vm(ctx.shape, F32), vm((full, width), BF16), vm((full, width), BF16),
            vm((full, width), BF16), vm((full, width), BF16), vm((2,) + wo.shape, BF16),
            vm((2,) + wu.shape, BF16), vm((2,) + wd.shape, BF16),
            vm((full, width), F32), vm((full, width), F32), vm((full, 128), F32), vm((full, 128), F32),
            vm((full, width), BF16), vm((full, ff), BF16), vm((full, ff), BF16),
            vm((full, width), BF16), vm((full, width), F32), vm((full, width), BF16),
            vm((8, 128), F32), vm((n_dev, 8, 128), F32), vm((512, width), F32),
            dma((12,)), dma((3,)), dma((n_dev,)), dma((n_dev,)), dma((full // 512, 2)), dma((5,)),
        ],
        compiler_params=pltpu.CompilerParams(
            collective_id=1, has_side_effects=True, vmem_limit_bytes=VMEM_LIMIT
        ),
        name="middle",
    )(lengths, lens_b, vecs, ctx, x0, ma, mf, cot, cot_p, wo, wo_p, wu, wu_p, wd, wd_p)


def sum_orders(n_dp):
    bits = n_dp.bit_length() - 1
    if bits == 4:
        return {"xy": ((0, 1, 2, 3), (1, 0, 2, 3)), "z": ((2, 3, 0, 1), (2, 3, 1, 0))}
    plain = tuple(range(bits))

    def turn(k):
        return plain[k % bits :] + plain[: k % bits] if bits else plain

    return {"xy": (turn(0), turn(2)), "z": (turn(4), turn(3))}


def back_kernel(
    lens, vecs, ng2, g2_i, dr2_i, act_i, dg_i, hl_i, n1_i, rs1_i, ctx_i, ma_i, wo, wo_p, wu, wu_p,
    wd, wd_p, qb_i, qkv_i, x0_i, wq_i, din_i,
    gq_o, go_o, gu_o, gd_o, gt_o, ng_o,
    mine, core_in, ring_in, stage, g2, dr, dobv, gin, gout, nsend, nall,
    in_sem, core_send, core_recv, ring_send, ring_recv, out_sem, nsend_sem, nrecv_sem, gt_sem,
):
    d = lax.axis_index("dp")
    t = lax.axis_index("tensor")
    other = 1 - t
    peer = (d, other)
    n_dp = lax.axis_size("dp")
    n_dev = 2 * n_dp
    me = d * 2 + t
    full, width = g2.shape
    loc = full // 2
    ff_half = wu.shape[1]
    half_w = qkv_i.shape[2]
    hw = half_w // 3
    pairs = hw // 128
    groups = width // 128
    n_cols = ff_half // CH
    rows_c = mine.shape[1]
    bits = n_dp.bit_length() - 1
    orders = sum_orders(n_dp)
    n_chunks = mine.shape[0]
    kinds = ["xy"] * n_chunks
    kinds[1] = kinds[4] = "z"

    barrier = pltpu.get_barrier_semaphore()

    def greet(k, _):
        lin = lax.rem(me + k, n_dev)
        pl.semaphore_signal(
            barrier, inc=1, device_id=(lin // 2, lax.rem(lin, 2)), device_id_type=MESH
        )
        return 0

    lax.fori_loop(1, n_dev, greet, 0)

    def load(pairs_of, first):
        copies = [
            pltpu.make_async_copy(s, v, in_sem.at[first + i]) for i, (s, v) in enumerate(pairs_of)
        ]
        for c in copies:
            c.start()
        return copies

    def core_copy(c):
        return pltpu.make_async_remote_copy(
            src_ref=stage.at[c % 3], dst_ref=core_in.at[c], send_sem=core_send.at[c],
            recv_sem=core_recv.at[c], device_id=peer, device_id_type=MESH,
        )

    def plan(c):
        steps = []
        off = 0
        size = rows_c
        place = 0
        o0, o1 = orders[kinds[c]]
        for b0, b1 in zip(o0, o1):
            size //= 2
            beta = lax.rem(d // 2**b0, 2) * other + lax.rem(d // 2**b1, 2) * t
            hop = 2**b0 * other + 2**b1 * t
            partner = d + (1 - 2 * beta) * hop
            keep = pl.multiple_of(off + beta * size, 16)
            sent = pl.multiple_of(off + (1 - beta) * size, 16)
            steps.append((partner, keep, sent, size, place))
            off = off + beta * size
            place += size
        return steps

    def ring_copy(c, s):
        if s < bits:
            partner, keep, sent, size, place = plan(c)[s]
            src, dst = mine.at[c, pl.ds(sent, size)], ring_in.at[c, pl.ds(place, size)]
        else:
            partner, keep, sent, size, place = plan(c)[2 * bits - 1 - s]
            src, dst = core_in.at[c, pl.ds(keep, size)], core_in.at[c, pl.ds(keep, size)]
        return pltpu.make_async_remote_copy(
            src_ref=src, dst_ref=dst, send_sem=ring_send.at[c, s], recv_sem=ring_recv.at[c, s],
            device_id=(partner, t), device_id_type=MESH,
        )

    def add_in(c, dst, dst_off, size, src, src_off):
        step = math.gcd(size, 384)

        def body(i, _):
            a = pl.ds(pl.multiple_of(dst_off + i * step, 16), step)
            b = pl.ds(pl.multiple_of(src_off + i * step, 16), step)
            dst[c, a, :] = (mine[c, a, :].astype(F32) + src[c, b, :].astype(F32)).astype(BF16)
            return 0

        lax.fori_loop(0, size // step, body, 0)

    def out_copies(c):
        dst = []
        if c < n_cols:
            for g in range(groups):
                dst.append((g * CH, CH, gd_o.at[pl.ds(c * CH, CH), pl.ds(g * 128, 128)]))
        elif c < 2 * n_cols:
            for g in range(CH // 128):
                col = (c - n_cols) * CH + g * 128
                dst.append((g * width, width, gu_o.at[:, pl.ds(col, 128)]))
        else:
            j = c - 2 * n_cols
            for g in range(3):
                dst.append((g * width, width, gq_o.at[:, pl.ds(g * hw + j * 128, 128)]))
            for g in range(groups):
                dst.append(
                    (3 * width + g * 128, 128, go_o.at[pl.ds(j * 128, 128), pl.ds(g * 128, 128)])
                )
        return [
            pltpu.make_async_copy(core_in.at[c, pl.ds(o, n)], r, out_sem.at[c, i])
            for i, (o, n, r) in enumerate(dst)
        ]

    last = 2 * bits + 1
    begun = {}
    now = [0]

    def advance(c, a):
        if a == 0:
            core_copy(c).wait()
            add_in(c, mine, 0, rows_c, core_in, 0)
        else:
            ring_copy(c, a - 1).wait()
            if a <= bits:
                _, keep, _, size, place = plan(c)[a - 1]
                add_in(c, core_in if a == bits else mine, keep, size, ring_in, place)
        if a < 2 * bits:
            ring_copy(c, a).start()
        else:
            for cp in out_copies(c):
                cp.start()

    def tick():
        now[0] += 1
        for c in sorted(begun):
            a = begun[c]
            if a <= 2 * bits:
                advance(c, a)
                begun[c] = a + 1

    def begin(c):
        core_copy(c).start()

    def put(ref, at, val):
        n = val.shape[0]
        for g in range(val.shape[1] // 128):
            ref[at + g * n : at + (g + 1) * n, :] = val[:, g * 128 : (g + 1) * 128].astype(BF16)

    gain1 = vecs[0:1, :]
    met = [False]

    def meet():
        if not met[0]:
            pl.semaphore_wait(barrier, n_dev - 1)
            met[0] = True

    def feed_forward(act, dg, hl, hlt, wuv, wdv):
        first = load(
            [(g2_i, g2), (act_i, act), (dr2_i, dr), (hl_i, hl), (dg_i, dg), (wd, wdv.at[t]),
             (wd_p, wdv.at[other]), (wu, wuv.at[t]), (wu_p, wuv.at[other])], 0,
        )
        first[0].wait()
        first[1].wait()
        for c in range(n_cols):
            for h, ref in ((other, stage.at[c % 3]), (t, mine.at[c])):
                col = pl.ds(pl.multiple_of(h * ff_half + c * CH, CH), CH)
                put(ref, 0, dot_tn(act[:, col], g2[...]))
                if ref is not None and h is other:
                    meet()
                    begin(c)
            tick()
            begun[c] = 0
        for cp in first[2:]:
            cp.wait()
        for k in range(groups):
            cols = slice(k * 128, (k + 1) * 128)
            hlt[cols, :] = hl[:, cols].astype(F32).T.astype(BF16)
        for k in range(n_cols):
            c = n_cols + k
            for h, ref in ((other, stage.at[c % 3]), (t, mine.at[c])):
                col = pl.ds(pl.multiple_of(h * ff_half + k * CH, CH), CH)
                for b in range(full // 512):
                    rows = slice(b * 512, (b + 1) * 512)
                    da = dot_nt(g2[rows, :], wdv[h, k * CH : (k + 1) * CH, :])
                    dp = (da * dg[rows, col].astype(F32)).astype(BF16)
                    dg[rows, col] = dp
                    dr[rows, :] += dot_nt(dp, wuv[h, :, k * CH : (k + 1) * CH])
                put(ref, 0, dot_nn(hlt[...], dg[:, col]))
                if h is other:
                    begin(c)
            tick()
            begun[c] = 0

    vm = pltpu.VMEM
    ff = 2 * ff_half
    pl.run_scoped(
        feed_forward, vm((full, ff), BF16), vm((full, ff), BF16), vm((full, width), BF16),
        vm((width, full), BF16), vm((2,) + wu.shape, BF16), vm((2,) + wd.shape, BF16),
    )

    def norm_and_out(n1, rs1, ctxv, mav, wov, gov):
        first = load(
            [(n1_i, n1), (rs1_i, rs1), (ma_i, mav), (wo, wov.at[t]), (wo_p, wov.at[other]),
             (ctx_i, ctxv)], 9,
        )
        for cp in first[:3]:
            cp.wait()

        def norm_one_back(b, sums):
            rows = pl.ds(pl.multiple_of(b * 256, 256), 256)
            dh = dr[rows, :]
            n = n1[rows, :]
            g = dh * gain1
            r = (
                g - jnp.mean(g, axis=1, keepdims=True) - n * jnp.mean(g * n, axis=1, keepdims=True)
            ) * rs1[rows, :1]
            dr[rows, :] = r
            g2[rows, :] = (r * (mav[rows, :].astype(F32) * INV_KEEP)).astype(BF16)
            return (
                sums[0] + jnp.sum(dh * n, axis=0, keepdims=True),
                sums[1] + jnp.sum(dh, axis=0, keepdims=True),
            )

        zero = jnp.zeros((1, width), F32)
        gg1, gs1 = lax.fori_loop(0, full // 256, norm_one_back, (zero, zero))
        for i, row in enumerate((gg1, gs1, ng2[0:1, :], ng2[1:2, :])):
            for g in range(groups):
                nsend[i * groups + g : i * groups + g + 1, :] = row[:, g * 128 : (g + 1) * 128]
        nall[me] = nsend[...]
        lax.fori_loop(1, n_dev, lambda k, _: push(k, 0), 0)
        for cp in first[3:]:
            cp.wait()
        lane = lax.broadcasted_iota(jnp.int32, (full, 128), 1)
        seg = (
            (lax.broadcasted_iota(jnp.int32, (128, 128), 0) < 64)
            != (lax.broadcasted_iota(jnp.int32, (128, 128), 1) < 64)
        ).astype(F32).astype(BF16)
        for g in range(groups):
            h, j = g // pairs, g % pairs
            cf = ctxv[g]
            gov[g * 128 : (g + 1) * 128, :] = dot_tn(cf.astype(BF16), g2[...]).astype(BF16)
            dc = dot_nt(g2[...], wov[h, j * 128 : (j + 1) * 128, :]).astype(BF16).astype(F32)
            hi, mid, lo = split_three(dc * cf)
            delta = (
                dot_nn(hi.astype(BF16), seg) + dot_nn(mid.astype(BF16), seg)
                + dot_nn(lo.astype(BF16), seg)
            )
            hi, mid, lo = split_three(delta)
            for a in range(2):
                own = (lane < 64) if a == 0 else (lane >= 64)
                z = 64 if a == 0 else 0
                extra = jnp.where(
                    lane == z, hi,
                    jnp.where(lane == z + 1, mid, jnp.where(lane == z + 2, lo, 0.0)),
                )
                dobv[2 * g + a] = jnp.where(own, dc, extra).astype(BF16)
            if g == pairs - 1:
                tick()
        for j in range(pairs):
            c = 2 * n_cols + j
            for h, ref in ((other, stage.at[c % 3]), (t, mine.at[c])):
                row = pl.ds(pl.multiple_of((h * pairs + j) * 128, 128), 128)
                for g in range(groups):
                    ref[3 * width + g * 128 : 3 * width + (g + 1) * 128, :] = gov[
                        row, g * 128 : (g + 1) * 128
                    ]
        tick()

    def push(k, what):
        lin = lax.rem(me + k, n_dev)
        c = pltpu.make_async_remote_copy(
            src_ref=nsend, dst_ref=nall.at[me], send_sem=nsend_sem.at[k], recv_sem=nrecv_sem.at[me],
            device_id=(lin // 2, lax.rem(lin, 2)), device_id_type=MESH,
        )
        if what == 0:
            c.start()
        else:
            c.wait_send()
        return 0

    def arrive(k, _):
        lin = lax.rem(me + k, n_dev)
        pltpu.make_async_remote_copy(
            src_ref=nsend, dst_ref=nall.at[lin], send_sem=nsend_sem.at[k],
            recv_sem=nrecv_sem.at[lin], device_id=(lin // 2, lax.rem(lin, 2)), device_id_type=MESH,
        ).wait_recv()
        return 0

    pl.run_scoped(
        norm_and_out, vm((full, width), F32), vm((full, 128), F32), vm((groups, full, 128), F32),
        vm((full, width), BF16), vm((2,) + wo.shape, BF16), vm((width, width), BF16),
    )

    def attention(dq3, qbv, qkvv, xv, xt):
        first = load([(qkv_i, qkvv), (qb_i, qbv), (x0_i, xv)], 15)
        length = lens[d]
        lane = lax.broadcasted_iota(jnp.int32, (full, 128), 1)
        bias = jnp.where(
            lax.broadcasted_iota(jnp.int32, (full, 128), 0) < length, 0.0, MASKED_SCORE
        )
        kb = 512
        low_half = lax.broadcasted_iota(jnp.int32, (kb, 128), 1) < 64
        for cp in first:
            cp.wait()
        for g in range(groups):
            cols = slice(g * 128, (g + 1) * 128)
            xt[cols, :] = (xv[:, cols].astype(F32) * INV_KEEP).T.astype(BF16)

        def head_pair(h, j):
            i = h * pairs + j

            def part(c):
                return qkvv[h, :, c * hw + j * 128 : c * hw + (j + 1) * 128]

            k2f = part(1).astype(F32)
            k2t = k2f.T.astype(BF16)
            v2f = part(2).astype(F32)
            dks, dvs, dqs = [], [], []
            for a in range(2):
                own = (lane < 64) if a == 0 else (lane >= 64)
                z = 64 if a == 0 else 0
                minus = jnp.where(jnp.logical_and(lane >= z, lane < z + 3), -1.0, 0.0)
                ka = jnp.where(own, k2f, jnp.where(lane == z + 3, bias, minus)).astype(BF16)
                va = jnp.where(own, v2f, minus).astype(BF16)
                qa = qbv[2 * i + a]
                da = dobv[2 * i + a]
                dk, dv = [], []
                dqt = None
                for b in range(full // kb):
                    rows = slice(b * kb, (b + 1) * kb)
                    p = jnp.exp(dot_nt(ka[rows], qa))
                    ds = (p * dot_nt(va[rows], da)).astype(BF16)
                    dv.append(dot_nn(p.astype(BF16), da))
                    dk.append(dot_nn(ds, qa))
                    term = dot_nn(k2t[a * 64 : (a + 1) * 64, rows], ds)
                    dqt = term if dqt is None else dqt + term
                dks.append(dk)
                dvs.append(dv)
                dqs.append(dqt)
            for b in range(full // kb):
                rows = slice(b * kb, (b + 1) * kb)
                dq3[i, rows, 128:256] = jnp.where(low_half, dks[0][b], dks[1][b]).astype(BF16)
                dq3[i, rows, 256:384] = jnp.where(low_half, dvs[0][b], dvs[1][b]).astype(BF16)
            dq = jnp.concatenate(dqs, axis=0) * HEAD_DIM**-0.5
            dq3[i, :, 0:128] = dq.T.astype(BF16)

        for j in range(pairs):
            c = 2 * n_cols + j
            for h, ref in ((other, stage.at[c % 3]), (t, mine.at[c])):
                head_pair(h, j)
                put(ref, 0, dot_nn(xt[...], dq3[h * pairs + j]))
                if h is other:
                    begin(c)
                tick()
            begun[c] = 0

    def to_input(dq3, wqv, dinv, acc, gtv):
        first = load([(wq_i, wqv), (din_i, dinv)], 18)
        for cp in first:
            cp.wait()

        def d_input(start):
            rows = pl.ds(pl.multiple_of(start, 256), 256)
            total = dr[rows, :]
            for h in range(2):
                lhs = jnp.concatenate(
                    [dq3[h * pairs + j, rows, c * 128 : (c + 1) * 128] for c in range(3) for j in range(pairs)],
                    axis=1,
                )
                total = total + dot_nt(lhs, wqv[h])
            return total

        for s in range(loc // 256):
            gout[s * 256 : (s + 1) * 256, :] = d_input(other * loc + s * 256).astype(BF16)
        send = pltpu.make_async_remote_copy(
            src_ref=gout, dst_ref=gin, send_sem=gt_sem.at[0], recv_sem=gt_sem.at[1],
            device_id=peer, device_id_type=MESH,
        )
        send.start()
        tick()
        for s in range(loc // 256):
            acc[s * 256 : (s + 1) * 256, :] = d_input(t * loc + s * 256)
        tick()
        send.wait()
        for s in range(loc // 256):
            rows = slice(s * 256, (s + 1) * 256)
            gtv[rows, :] = (
                jnp.where(dinv[t, rows, :] != 0, acc[rows, :], 0.0)
                + jnp.where(dinv[other, rows, :] != 0, gin[rows, :].astype(F32), 0.0)
            ) * INV_KEEP
        out = pltpu.make_async_copy(gtv, gt_o, gt_sem.at[2])
        out.start()
        tick()
        lax.fori_loop(1, n_dev, arrive, 0)
        total = nall[0]
        for k in range(1, n_dev):
            total = total + nall[k]
        ng_o[...] = total
        tick()
        while any(a <= 2 * bits for a in begun.values()):
            tick()
        out.wait()

    def projections(dq3):
        pl.run_scoped(
            functools.partial(attention, dq3), vm((2 * groups, full, 128), BF16),
            vm(qkv_i.shape, BF16), vm((full, width), BF16), vm((width, full), BF16),
        )
        pl.run_scoped(
            functools.partial(to_input, dq3), vm(wq_i.shape, BF16), vm(din_i.shape, jnp.int32),
            vm((loc, width), F32), vm((loc, width), F32),
        )

    pl.run_scoped(projections, vm((groups, full, 384), BF16))
    for c in range(n_chunks):
        for cp in out_copies(c):
            cp.wait()
    lax.fori_loop(1, n_dev, lambda k, _: push(k, 1), 0)


def back(
    lengths, vecs, ng2, g2, dr2, act, dg, hl, n1, rs1, ctx, ma, wo, wo_p, wu, wu_p, wd, wd_p, qb,
    qkv, x0, wq, d_in, n_dp,
):
    full, width = x0.shape
    loc = full // 2
    groups = width // 128
    bits = n_dp.bit_length() - 1
    n_dev = 2 * n_dp
    n_chunks = 2 * (wu.shape[1] // CH) + groups // 2
    rows_c = CH * width // 128
    sds = jax.ShapeDtypeStruct
    anyspec = pl.BlockSpec(memory_space=pl.ANY)
    vspec = pl.BlockSpec(memory_space=pltpu.VMEM)
    vm = pltpu.VMEM
    dma = pltpu.SemaphoreType.DMA
    return pl.pallas_call(
        back_kernel,
        out_shape=[
            sds(wq.shape[1:], BF16), sds(wo.shape, BF16), sds(wu.shape, BF16), sds(wd.shape, BF16),
            sds((loc, width), F32), sds((4 * groups, 128), F32),
        ],
        in_specs=[pl.BlockSpec(memory_space=pltpu.SMEM), vspec, vspec] + [anyspec] * 20,
        out_specs=[anyspec] * 5 + [vspec],
        scratch_shapes=[
            vm((n_chunks, rows_c, 128), BF16), vm((n_chunks, rows_c, 128), BF16),
            vm((n_chunks, rows_c, 128), BF16), vm((3, rows_c, 128), BF16),
            vm((full, width), BF16), vm((full, width), F32), vm(qb.shape, BF16),
            vm((loc, width), BF16), vm((loc, width), BF16),
            vm((4 * groups, 128), F32), vm((n_dev, 4 * groups, 128), F32),
            dma((20,)), dma((n_chunks,)), dma((n_chunks,)), dma((n_chunks, 2 * bits)),
            dma((n_chunks, 2 * bits)), dma((n_chunks, 9)), dma((n_dev,)), dma((n_dev,)), dma((3,)),
        ],
        compiler_params=pltpu.CompilerParams(
            collective_id=2, has_side_effects=True, vmem_limit_bytes=VMEM_LIMIT
        ),
        name="back",
    )(
        lengths, vecs, ng2, g2, dr2, act, dg, hl, n1, rs1, ctx, ma, wo, wo_p, wu, wu_p, wd, wd_p,
        qb, qkv, x0, wq, d_in,
    )


def per_device(
    tokens, lengths, drop_in, drop_attn, drop_ffn, qkv_weight, out_weight, up_weight, down_weight,
    gain_first, shift_first, gain_second, shift_second, cotangent,
):
    n_dp = lax.axis_size("dp")
    width = tokens.shape[2]
    wq = qkv_weight.reshape(width, -1)
    x0, ma, mf, cot_p, wqf, wo_p, wu_p, wd_p, qkv, qb, ctx = front(
        lengths, tokens[0], drop_in[0], drop_attn[0], drop_ffn[0], cotangent[0],
        wq, out_weight, up_weight, down_weight,
    )
    lens_b = jnp.broadcast_to(lengths.astype(F32)[:, None], (n_dp, 128))
    vecs = jnp.stack([gain_first, shift_first, gain_second, shift_second] * 2)
    lay, stats, act, dg, hl, n1, rs1, g2, dr2, ng2 = middle(
        lengths, lens_b, vecs, ctx, x0, ma, mf, cotangent[0], cot_p, out_weight, wo_p,
        up_weight, wu_p, down_weight, wd_p, n_dp,
    )
    gq, go, gu, gd, gt, norms = back(
        lengths, vecs, ng2, g2, dr2, act, dg, hl, n1, rs1, ctx, ma, out_weight, wo_p,
        up_weight, wu_p, down_weight, wd_p, qb, qkv, x0, wqf, drop_in[0], n_dp,
    )
    norms = norms.reshape(4, width)
    return (
        lay[None], gt[None], gq.reshape(qkv_weight.shape).astype(F32), go.astype(F32),
        gu.astype(F32), gd.astype(F32),
        norms[0], norms[1], norms[2], norms[3],
        stats[0, 0], stats[1, 0], stats[2, 0],
    )


def solution(mesh):
    act = P("dp", None, "tensor", None)
    in_specs = (
        P("dp", "tensor", None), P(), act, act, act,
        P(None, None, "tensor"), P("tensor", None), P(None, "tensor"), P("tensor", None),
        P(), P(), P(), P(), act,
    )
    out_specs = (
        act, P("dp", "tensor", None),
        P(None, None, "tensor"), P("tensor", None), P(None, "tensor"), P("tensor", None),
        P(), P(), P(), P(), P(), P(), P(),
    )
    return jax.shard_map(
        per_device, mesh=mesh, in_specs=in_specs, out_specs=out_specs, check_vma=False
    )
```

```python
import functools
import math

import jax
import jax.numpy as jnp
from jax import lax
from jax.experimental import pallas as pl
from jax.experimental.pallas import tpu as pltpu
from jax.sharding import PartitionSpec as P

HEAD_DIM = 64
INV_KEEP = 1.0 / 0.9
SOFTMAX_WARMTH = 0.05
EPSILON = 1e-06
MASKED_SCORE = -1e30
MESH = pl.DeviceIdType.MESH
F32 = jnp.float32
BF16 = jnp.bfloat16
VMEM_LIMIT = 60 * 2**20
HIGHEST = lax.Precision.HIGHEST

TAIL_P = 0.3
TAIL = (
    0.11962929778234735,
    0.12075397394392673,
    0.09991336806236217,
    0.1285620774207718,
    -0.05368457414666341,
    0.20635459819946347,
    -0.15720376083821283,
    0.03567494667807555,
)


def dot_nn(a, b):
    return jnp.dot(a, b, preferred_element_type=F32)


def dot_nt(a, b):
    return lax.dot_general(a, b, (((1,), (1,)), ((), ())), preferred_element_type=F32)


def dot_tn(a, b):
    return lax.dot_general(a, b, (((0,), (0,)), ((), ())), preferred_element_type=F32)


def gelu_pair(x):
    z = jnp.abs(x)
    bell = jnp.exp(x * x * -0.5)
    t = 1.0 / (1.0 + TAIL_P * z)
    acc = jnp.full_like(t, TAIL[-1])
    for c in TAIL[-2::-1]:
        acc = acc * t + c
    tail = acc * t * bell
    cdf = jnp.where(x < 0.0, tail, 1.0 - tail)
    return x * cdf, cdf + x * (bell * (1.0 / math.sqrt(2.0 * math.pi)))


def split_three(v):
    hi = v.astype(BF16).astype(F32)
    rest = v - hi
    mid = rest.astype(BF16).astype(F32)
    return hi, mid, rest - mid


def front_kernel(
    lens, tok, d_in, d_at, d_ff, cot, wq, wo, wu, wd,
    x0_o, ma_o, mf_o, cot_o, wq_o, wo_o, wu_o, wd_o, qkv_o, qb_o, ctx_o,
    xv, xl, wv, qs, ms, tokv, st, qbv, ctxv, in_sem, loc_sem, send_sem, recv_sem, out_sem,
):
    d = lax.axis_index("dp")
    t = lax.axis_index("tensor")
    other = 1 - t
    peer = (d, other)
    loc = tok.shape[0]
    full = 2 * loc
    hw = wq.shape[2]
    pairs = hw // 128

    barrier = pltpu.get_barrier_semaphore()
    pl.semaphore_signal(barrier, inc=1, device_id=peer, device_id_type=MESH)

    loads = [
        pltpu.make_async_copy(tok, tokv, in_sem.at[0]),
        pltpu.make_async_copy(d_in, ms.at[0], in_sem.at[1]),
        pltpu.make_async_copy(wq, wv.at[t], in_sem.at[2]),
        pltpu.make_async_copy(d_at, ms.at[1], in_sem.at[3]),
        pltpu.make_async_copy(d_ff, ms.at[2], in_sem.at[4]),
    ]
    for c in loads:
        c.start()
    own_rows = pl.ds(pl.multiple_of(t * loc, loc), loc)

    def remote(i, src, dst):
        return pltpu.make_async_remote_copy(
            src_ref=src, dst_ref=dst, send_sem=send_sem.at[i], recv_sem=recv_sem.at[i],
            device_id=peer, device_id_type=MESH,
        )

    pl.semaphore_wait(barrier, 1)
    send_wq = remote(0, wq, wv.at[t])
    send_wq.start()
    loads[0].wait()
    loads[1].wait()
    st[0] = jnp.where(ms[0, other] != 0, tokv[...].astype(F32), 0.0).astype(BF16)
    send_x = remote(1, st.at[0], xv.at[own_rows])
    send_x.start()
    own_x = jnp.where(ms[0, t] != 0, tokv[...].astype(F32), 0.0)
    xv[own_rows, :] = own_x.astype(BF16)
    xl[own_rows, :] = (own_x * INV_KEEP).astype(BF16)
    loads[3].wait()
    st[1] = ms[1, other].astype(F32).astype(BF16)
    st[2] = ms[1, t].astype(F32).astype(BF16)
    loads[4].wait()
    st[3] = ms[2, other].astype(F32).astype(BF16)
    st[4] = ms[2, t].astype(F32).astype(BF16)
    sends = [
        remote(2, wo, wo_o),
        remote(3, st.at[1], ma_o.at[own_rows]),
        remote(4, wu, wu_o),
        remote(5, wd, wd_o),
        remote(6, st.at[3], mf_o.at[own_rows]),
        remote(7, cot.at[other], cot_o),
    ]
    for c in sends:
        c.start()
    more = [
        pltpu.make_async_copy(st.at[2], ma_o.at[own_rows], loc_sem.at[0]),
        pltpu.make_async_copy(st.at[4], mf_o.at[own_rows], loc_sem.at[1]),
    ]
    for c in more:
        c.start()

    loads[2].wait()
    send_wq.wait_recv()
    send_x.wait_recv()
    oth_rows = pl.ds(pl.multiple_of(other * loc, loc), loc)
    xl[oth_rows, :] = (xv[oth_rows, :].astype(F32) * INV_KEEP).astype(BF16)
    save_x = pltpu.make_async_copy(xv, x0_o, loc_sem.at[2])
    save_x.start()
    save_w = pltpu.make_async_copy(wv, wq_o, loc_sem.at[3])
    save_w.start()

    for h in range(2):
        for c in range(3):
            def project(b, _, h=h, c=c):
                rows = pl.ds(pl.multiple_of(b * 512, 512), 512)
                qs[h, rows, c * hw : (c + 1) * hw] = dot_nn(
                    xl[rows, :], wv[h, c]
                ).astype(BF16)
                return 0

            lax.fori_loop(0, full // 512, project, 0)
    save_qkv = pltpu.make_async_copy(qs, qkv_o, loc_sem.at[4])
    save_qkv.start()

    length = lens[d]
    bias = jnp.where(
        lax.broadcasted_iota(jnp.int32, (full, 128), 0) < length, 0.0, MASKED_SCORE
    )
    lane = lax.broadcasted_iota(jnp.int32, (full, 128), 1)
    lane_q = lax.broadcasted_iota(jnp.int32, (512, 128), 1)

    def out_copies(i):
        return [
            pltpu.make_async_copy(qbv.at[pl.ds(2 * i, 2)], qb_o.at[pl.ds(2 * i, 2)], out_sem.at[0, i]),
            pltpu.make_async_copy(ctxv.at[i], ctx_o.at[i], out_sem.at[1, i]),
        ]

    def head_pair(i, _):
        h = i // pairs
        off = (i - h * pairs) * 128

        def part(c):
            return qs[h, :, pl.ds(pl.multiple_of(c * hw + off, 128), 128)].astype(F32)

        q2 = part(0) * HEAD_DIM**-0.5
        k2 = part(1)
        v2 = part(2)
        keys, vals, ques = [], [], []
        for a in range(2):
            own = (lane < 64) if a == 0 else (lane >= 64)
            first = 64 if a == 0 else 0
            keys.append(jnp.where(own, k2, jnp.where(lane == first, bias, 0.0)).astype(BF16))
            ques.append(jnp.where(own, q2, jnp.where(lane == first, 1.0, 0.0)).astype(BF16))
            vals.append(jnp.where(own, v2, 1.0).astype(BF16))
        for b in range(full // 512):
            rows = slice(b * 512, (b + 1) * 512)
            tops, outs = [], []
            for a in range(2):
                s = dot_nt(ques[a][rows], keys[a])
                top = jnp.max(s, axis=1, keepdims=True)
                p = jnp.exp(s - top).astype(BF16)
                outs.append(dot_nn(p, vals[a]))
                tops.append(top)
            low_half = lane_q < 64
            num = jnp.where(low_half, outs[0], outs[1])
            den = pltpu.roll(jnp.where(low_half, outs[1], outs[0]), 64, 1)
            ctxv[i, rows, :] = num / den
            for a in range(2):
                hi, mid, lo = split_three(tops[a] + jnp.log(outs[a]))
                own = low_half if a == 0 else jnp.logical_not(low_half)
                first = 64 if a == 0 else 0
                extra = jnp.where(
                    lane_q == first, hi,
                    jnp.where(lane_q == first + 1, mid,
                              jnp.where(lane_q == first + 2, lo,
                                        jnp.where(lane_q == first + 3, 1.0, 0.0))),
                )
                qbv[2 * i + a, rows, :] = jnp.where(own, q2[rows], extra).astype(BF16)
        for c in out_copies(i):
            c.start()
        return 0

    lax.fori_loop(0, 2 * pairs, head_pair, 0)

    def drain(i, _):
        for c in out_copies(i):
            c.wait()
        return 0

    lax.fori_loop(0, 2 * pairs, drain, 0)
    send_wq.wait_send()
    send_x.wait_send()
    for c in sends:
        c.wait()
    for c in more + [save_x, save_w, save_qkv]:
        c.wait()


def front(lengths, tok, d_in, d_at, d_ff, cot, wq, wo, wu, wd):
    loc, width = tok.shape
    full = 2 * loc
    half_w = 3 * wq.shape[2]
    groups = width // 128
    sds = jax.ShapeDtypeStruct
    anyspec = pl.BlockSpec(memory_space=pl.ANY)
    outs = [
        sds((full, width), BF16), sds((full, width), BF16), sds((full, width), BF16),
        sds((loc, width), BF16),
        sds((2,) + wq.shape, BF16), sds(wo.shape, BF16), sds(wu.shape, BF16), sds(wd.shape, BF16),
        sds((2, full, half_w), BF16), sds((2 * groups, full, 128), BF16),
        sds((groups, full, 128), F32),
    ]
    return pl.pallas_call(
        front_kernel,
        out_shape=outs,
        in_specs=[pl.BlockSpec(memory_space=pltpu.SMEM)] + [anyspec] * 9,
        out_specs=[anyspec] * len(outs),
        scratch_shapes=[
            pltpu.VMEM((full, width), BF16), pltpu.VMEM((full, width), BF16),
            pltpu.VMEM((2,) + wq.shape, BF16), pltpu.VMEM((2, full, half_w), BF16),
            pltpu.VMEM((3, 2, loc, width), jnp.int32), pltpu.VMEM((loc, width), BF16),
            pltpu.VMEM((5, loc, width), BF16),
            pltpu.VMEM((2 * groups, full, 128), BF16), pltpu.VMEM((groups, full, 128), F32),
            pltpu.SemaphoreType.DMA((5,)), pltpu.SemaphoreType.DMA((5,)),
            pltpu.SemaphoreType.DMA((8,)), pltpu.SemaphoreType.DMA((8,)),
            pltpu.SemaphoreType.DMA((2, groups)),
        ],
        compiler_params=pltpu.CompilerParams(
            collective_id=0, has_side_effects=True, vmem_limit_bytes=VMEM_LIMIT
        ),
        name="front",
    )(lengths, tok, d_in, d_at, d_ff, cot, wq, wo, wu, wd)


CH = 512


def middle_kernel(
    lens, lens_b, vecs, ctx, x0, ma, mf, cot, cot_p, wo, wo_p, wu, wu_p, wd, wd_p,
    lay_o, loss_o, act_o, dg_o, hl_o, n1_o, rs1_o, g2_o, dr2_o, ng_o,
    ctxv, x0v, mav, mfv, cotv, wov, wuv, wdv,
    n1, n2, rs1, rs2, hl, act, dg, g2, dr2, yb, sbuf, pool_all, facc,
    in_sem, lay_sem, send_sem, recv_sem, row_sem, out_sem,
):
    d = lax.axis_index("dp")
    t = lax.axis_index("tensor")
    other = 1 - t
    peer = (d, other)
    n_dp = lax.axis_size("dp")
    n_dev = 2 * n_dp
    full, width = x0v.shape
    loc = full // 2
    groups = width // 128
    ff_half = wuv.shape[2]
    n_ch = 2 * ff_half // CH
    per_half = ff_half // CH
    me = d * 2 + t

    barrier = pltpu.get_barrier_semaphore()

    def greet(k, _):
        lin = lax.rem(me + k, n_dev)
        pl.semaphore_signal(
            barrier, inc=1, device_id=(lin // 2, lax.rem(lin, 2)), device_id_type=MESH
        )
        return 0

    lax.fori_loop(1, n_dev, greet, 0)

    own_rows = pl.ds(pl.multiple_of(t * loc, loc), loc)
    oth_rows = pl.ds(pl.multiple_of(other * loc, loc), loc)
    srcs = (ctx, wo, wo_p, x0, ma, wu, wu_p, wd, wd_p, mf, cot.at[t], cot_p)
    dsts = (
        ctxv, wov.at[t], wov.at[other], x0v, mav, wuv.at[t], wuv.at[other], wdv.at[t],
        wdv.at[other], mfv, cotv.at[own_rows], cotv.at[oth_rows],
    )
    loads = [pltpu.make_async_copy(s, v, in_sem.at[i]) for i, (s, v) in enumerate(zip(srcs, dsts))]
    for c in loads:
        c.start()
    gain1, shift1, gain2, shift2 = (vecs[i : i + 1, :] for i in range(4))
    length = lens[d]

    for c in loads[:5]:
        c.wait()

    def norm_one(b, _):
        rows = pl.ds(pl.multiple_of(b * 256, 256), 256)
        c2 = jnp.concatenate([ctxv[g, rows, :].astype(BF16) for g in range(groups)], axis=1)
        branch = dot_nn(c2, wov[...].reshape(width, width))
        r = (x0v[rows, :].astype(F32) + branch * mav[rows, :].astype(F32)) * INV_KEEP
        cen = r - jnp.mean(r, axis=1, keepdims=True)
        rstd = lax.rsqrt(jnp.mean(cen * cen, axis=1, keepdims=True) + EPSILON)
        n = cen * rstd
        n1[rows, :] = n
        rs1[rows, :] = jnp.broadcast_to(rstd, (256, 128))
        hl[rows, :] = (n * gain1 + shift1).astype(BF16)
        return 0

    lax.fori_loop(0, full // 256, norm_one, 0)
    saves = [
        pltpu.make_async_copy(s, o, out_sem.at[i])
        for i, (s, o) in enumerate(((hl, hl_o), (n1, n1_o), (rs1, rs1_o)))
    ]
    for c in saves:
        c.start()
    for c in loads[5:]:
        c.wait()

    def row_copies(b):
        rows = pl.ds(pl.multiple_of(b * 512, 512), 512)
        return [
            pltpu.make_async_copy(act.at[rows], act_o.at[rows], row_sem.at[b, 0]),
            pltpu.make_async_copy(dg.at[rows], dg_o.at[rows], row_sem.at[b, 1]),
        ]

    def ffn(b, pooled):
        rows = pl.ds(pl.multiple_of(b * 512, 512), 512)
        for j in range(n_ch):
            h, o = j // per_half, (j % per_half) * CH
            pre = dot_nn(hl[rows, :], wuv[h, :, o : o + CH])
            a, da = gelu_pair(pre)
            ab = a.astype(BF16)
            act[rows, j * CH : (j + 1) * CH] = ab
            dg[rows, j * CH : (j + 1) * CH] = da.astype(BF16)
            term = dot_nn(ab, wdv[h, o : o + CH, :])
            if j == 0:
                facc[...] = term
            else:
                facc[...] += term
        for c in row_copies(b):
            c.start()
        for s in range(2):
            sub = pl.ds(pl.multiple_of(b * 512 + s * 256, 256), 256)
            r = n1[sub, :] * gain1 + shift1 + facc[s * 256 : (s + 1) * 256, :] * (
                mfv[sub, :].astype(F32) * INV_KEEP
            )
            cen = r - jnp.mean(r, axis=1, keepdims=True)
            rstd = lax.rsqrt(jnp.mean(cen * cen, axis=1, keepdims=True) + EPSILON)
            n = cen * rstd
            n2[sub, :] = n
            rs2[sub, :] = jnp.broadcast_to(rstd, (256, 128))
            y = n * gain2 + shift2
            yb[sub, :] = y.astype(BF16)
            pos = lax.broadcasted_iota(jnp.int32, (256, width), 0) + (b * 512 + s * 256)
            pooled = pooled + jnp.sum(jnp.where(pos < length, y, 0.0), axis=0, keepdims=True)
        return pooled

    pooled = lax.fori_loop(0, full // 512, ffn, jnp.zeros((1, width), F32))

    for g in range(groups):
        sbuf[g : g + 1, :] = pooled[:, g * 128 : (g + 1) * 128]
    sbuf[groups:, :] = jnp.zeros((8 - groups, 128), F32)
    slot = t * n_dp + d
    pl.semaphore_wait(barrier, n_dev - 1)

    def push(k, start):
        lin = lax.rem(me + k, n_dev)
        pd, pt = lin // 2, lax.rem(lin, 2)
        c = pltpu.make_async_remote_copy(
            src_ref=sbuf, dst_ref=pool_all.at[slot], send_sem=send_sem.at[k],
            recv_sem=recv_sem.at[slot], device_id=(pd, pt), device_id_type=MESH,
        )
        if start:
            c.start()
        else:
            c.wait_send()
        return 0

    lax.fori_loop(1, n_dev, lambda k, _: push(k, True), 0)
    lay_local = pltpu.make_async_copy(yb.at[own_rows], lay_o.at[t], lay_sem.at[0])
    lay_local.start()
    lay_send = pltpu.make_async_remote_copy(
        src_ref=yb.at[oth_rows], dst_ref=lay_o.at[t], send_sem=lay_sem.at[1],
        recv_sem=lay_sem.at[2], device_id=peer, device_id_type=MESH,
    )
    lay_send.start()
    pool_all[slot] = sbuf[...]

    def arrive(k, _):
        lin = lax.rem(me + k, n_dev)
        s = lax.rem(lin, 2) * n_dp + lin // 2
        pltpu.make_async_remote_copy(
            src_ref=sbuf, dst_ref=pool_all.at[s], send_sem=send_sem.at[k],
            recv_sem=recv_sem.at[s], device_id=(lin // 2, lax.rem(lin, 2)), device_id_type=MESH,
        ).wait_recv()
        return 0

    lax.fori_loop(1, n_dev, arrive, 0)

    len_col = lens_b[...][:, :1]
    units = []
    scales = []
    for v in range(2):
        raw = jnp.concatenate(
            [pool_all[v * n_dp : (v + 1) * n_dp, g, :] for g in range(groups)], axis=1
        )
        pv = raw / len_col
        scale = lax.rsqrt(jnp.sum(pv * pv, axis=1, keepdims=True) + EPSILON)
        units.append(pv * scale)
        scales.append(scale)
    u0, u1 = units
    nt = (((1,), (1,)), ((), ()))
    row_i = lax.broadcasted_iota(jnp.int32, (n_dp, n_dp), 0)
    col_i = lax.broadcasted_iota(jnp.int32, (n_dp, n_dp), 1)
    diag = row_i == col_i
    sim = lax.dot_general(u0, u1, nt, precision=HIGHEST, preferred_element_type=F32) / SOFTMAX_WARMTH
    top = jnp.max(sim, axis=1, keepdims=True)
    raw = jnp.exp(sim - top)
    total = jnp.sum(raw, axis=1, keepdims=True)
    ce = top + jnp.log(total) - jnp.sum(jnp.where(diag, sim, 0.0), axis=1, keepdims=True)
    loss = jnp.sum(ce, axis=0, keepdims=True) / n_dp
    gap = u0 - u1
    align = jnp.sum(jnp.sum(gap * gap, axis=1, keepdims=True), axis=0, keepdims=True) / n_dp
    sq = jnp.sum(u0 * u0, axis=1, keepdims=True)
    sq_row = lax.dot_general(
        jnp.ones((n_dp, width), F32), u0 * u0, nt, precision=HIGHEST, preferred_element_type=F32
    )
    inner = lax.dot_general(u0, u0, nt, precision=HIGHEST, preferred_element_type=F32)
    pot = jnp.where(diag, 0.0, jnp.exp(-2.0 * (sq + sq_row - 2.0 * inner)))
    uni = jnp.log(
        jnp.sum(jnp.sum(pot, axis=1, keepdims=True), axis=0, keepdims=True) / (n_dp * (n_dp - 1))
    )
    stat_i = lax.broadcasted_iota(jnp.int32, (8, 128), 0)
    loss_o[...] = jnp.where(stat_i == 0, loss, jnp.where(stat_i == 1, align, uni))
    d_sim = (raw / total - jnp.where(diag, 1.0, 0.0)) / SOFTMAX_WARMTH
    d_u0 = jnp.dot(d_sim, u1, precision=HIGHEST, preferred_element_type=F32)
    d_u1 = lax.dot_general(
        d_sim, u0, (((0,), (0,)), ((), ())), precision=HIGHEST, preferred_element_type=F32
    )
    first_view = t == 0
    du = jnp.where(first_view, d_u0, d_u1)
    u = jnp.where(first_view, u0, u1)
    scale = jnp.where(first_view, scales[0], scales[1])
    d_pool = (du - u * jnp.sum(u * du, axis=1, keepdims=True)) * scale / len_col
    mine = lax.broadcasted_iota(jnp.int32, (n_dp, width), 0) == d
    pool_grad = jnp.sum(jnp.where(mine, d_pool, 0.0), axis=0, keepdims=True)

    def norm_two_back(b, sums):
        rows = pl.ds(pl.multiple_of(b * 256, 256), 256)
        pos = lax.broadcasted_iota(jnp.int32, (256, width), 0) + b * 256
        dy = cotv[rows, :].astype(F32) + jnp.where(pos < length, pool_grad, 0.0)
        n = n2[rows, :]
        g = dy * gain2
        dr = (g - jnp.mean(g, axis=1, keepdims=True) - n * jnp.mean(g * n, axis=1, keepdims=True)) * rs2[rows, :1]
        dr2[rows, :] = dr
        g2[rows, :] = (dr * (mfv[rows, :].astype(F32) * INV_KEEP)).astype(BF16)
        return (
            sums[0] + jnp.sum(dy * n, axis=0, keepdims=True),
            sums[1] + jnp.sum(dy, axis=0, keepdims=True),
        )

    zero = jnp.zeros((1, width), F32)
    gg2, gs2 = lax.fori_loop(0, full // 256, norm_two_back, (zero, zero))

    ng_o[...] = jnp.concatenate([gg2, gs2, zero, zero, zero, zero, zero, zero], axis=0)
    more = [
        pltpu.make_async_copy(g2, g2_o, out_sem.at[3]),
        pltpu.make_async_copy(dr2, dr2_o, out_sem.at[4]),
    ]
    for c in more:
        c.start()
    for b in range(full // 512):
        for c in row_copies(b):
            c.wait()
    lax.fori_loop(1, n_dev, lambda k, _: push(k, False), 0)
    lay_local.wait()
    lay_send.wait()
    for c in saves + more:
        c.wait()


def middle(lengths, lens_b, vecs, ctx, x0, ma, mf, cot, cot_p, wo, wo_p, wu, wu_p, wd, wd_p, n_dp):
    full, width = x0.shape
    loc = full // 2
    ff = 2 * wd.shape[0]
    n_dev = 2 * n_dp
    sds = jax.ShapeDtypeStruct
    anyspec = pl.BlockSpec(memory_space=pl.ANY)
    vspec = pl.BlockSpec(memory_space=pltpu.VMEM)
    outs = [
        sds((2, loc, width), BF16), sds((8, 128), F32), sds((full, ff), BF16), sds((full, ff), BF16),
        sds((full, width), BF16), sds((full, width), F32), sds((full, 128), F32),
        sds((full, width), BF16), sds((full, width), F32), sds((8, width), F32),
    ]
    vm = pltpu.VMEM
    dma = pltpu.SemaphoreType.DMA
    return pl.pallas_call(
        middle_kernel,
        out_shape=outs,
        in_specs=[pl.BlockSpec(memory_space=pltpu.SMEM), vspec, vspec] + [anyspec] * 12,
        out_specs=[anyspec, vspec] + [anyspec] * 7 + [vspec],
        scratch_shapes=[
            vm(ctx.shape, F32), vm((full, width), BF16), vm((full, width), BF16),
            vm((full, width), BF16), vm((full, width), BF16), vm((2,) + wo.shape, BF16),
            vm((2,) + wu.shape, BF16), vm((2,) + wd.shape, BF16),
            vm((full, width), F32), vm((full, width), F32), vm((full, 128), F32), vm((full, 128), F32),
            vm((full, width), BF16), vm((full, ff), BF16), vm((full, ff), BF16),
            vm((full, width), BF16), vm((full, width), F32), vm((full, width), BF16),
            vm((8, 128), F32), vm((n_dev, 8, 128), F32), vm((512, width), F32),
            dma((12,)), dma((3,)), dma((n_dev,)), dma((n_dev,)), dma((full // 512, 2)), dma((5,)),
        ],
        compiler_params=pltpu.CompilerParams(
            collective_id=1, has_side_effects=True, vmem_limit_bytes=VMEM_LIMIT
        ),
        name="middle",
    )(lengths, lens_b, vecs, ctx, x0, ma, mf, cot, cot_p, wo, wo_p, wu, wu_p, wd, wd_p)


XY = ((0, 1, 2, 3), (1, 0, 2, 3))
ORDERS_16 = (
    XY, ((2, 3, 1, 0), (1, 0, 2, 3)), ((2, 3, 0, 1), (0, 1, 2, 3)), XY,
    ((0, 2, 3, 1), (1, 2, 3, 0)), XY, XY, ((2, 0, 1, 3), (2, 1, 0, 3)), XY,
)
TABLE_16 = (
    (), (), (), (), (0,), (), (1,), (), (2, 0), (), (), (1,), (3, 2), (0,), (1,), (), (4, 0, 3),
    (2, 1), (), (0,), (5, 4, 3, 2, 0, 1), (), (), (), (), (5, 4), (3, 2), (0, 1, 5), (4,),
    (3, 0, 2, 1, 5, 4), (), (3,), (6, 0, 2), (1, 4, 3, 5), (), (6, 2), (7, 4), (1, 5, 3), (6, 2), (),
    (8, 3), (), (7,), (), (), (4, 8), (),
    (5, 7, 6, 4, 6, 8, 5, 6, 7, 8, 6, 7, 5, 8, 6, 7, 8, 6, 7, 8, 7, 8, 8, 7),
)


def sum_plan(n_dp, n_chunks):
    bits = n_dp.bit_length() - 1
    if bits == 4 and n_chunks == len(ORDERS_16):
        return ORDERS_16, TABLE_16
    plain = tuple(range(bits))

    def turn(k):
        return plain[k % bits :] + plain[: k % bits] if bits else plain

    return tuple((turn(2 * c), turn(2 * c + 2)) for c in range(n_chunks)), None


def back_kernel(
    lens, vecs, ng2, g2_i, dr2_i, act_i, dg_i, hl_i, n1_i, rs1_i, ctx_i, ma_i, wo, wo_p, wu, wu_p,
    wd, wd_p, qb_i, qkv_i, x0_i, wq_i, din_i,
    gq_o, go_o, gu_o, gd_o, gt_o, ng_o,
    mine, core_in, ring_in, stage, g2, dr, dobv, gin, gout, nsend, nall,
    in_sem, core_send, core_recv, ring_send, ring_recv, out_sem, nsend_sem, nrecv_sem, gt_sem,
):
    d = lax.axis_index("dp")
    t = lax.axis_index("tensor")
    other = 1 - t
    peer = (d, other)
    n_dp = lax.axis_size("dp")
    n_dev = 2 * n_dp
    me = d * 2 + t
    full, width = g2.shape
    loc = full // 2
    ff_half = wu.shape[1]
    half_w = qkv_i.shape[2]
    hw = half_w // 3
    pairs = hw // 128
    groups = width // 128
    n_cols = ff_half // CH
    rows_c = mine.shape[1]
    bits = n_dp.bit_length() - 1
    n_chunks = mine.shape[0]
    orders, table = sum_plan(n_dp, n_chunks)

    barrier = pltpu.get_barrier_semaphore()

    def greet(k, _):
        lin = lax.rem(me + k, n_dev)
        pl.semaphore_signal(
            barrier, inc=1, device_id=(lin // 2, lax.rem(lin, 2)), device_id_type=MESH
        )
        return 0

    lax.fori_loop(1, n_dev, greet, 0)

    def load(pairs_of, first):
        copies = [
            pltpu.make_async_copy(s, v, in_sem.at[first + i]) for i, (s, v) in enumerate(pairs_of)
        ]
        for c in copies:
            c.start()
        return copies

    def core_copy(c):
        return pltpu.make_async_remote_copy(
            src_ref=stage.at[c % 3], dst_ref=core_in.at[c], send_sem=core_send.at[c],
            recv_sem=core_recv.at[c], device_id=peer, device_id_type=MESH,
        )

    def plan(c):
        steps = []
        off = 0
        size = rows_c
        place = 0
        o0, o1 = orders[c]
        for b0, b1 in zip(o0, o1):
            size //= 2
            beta = lax.rem(d // 2**b0, 2) * other + lax.rem(d // 2**b1, 2) * t
            hop = 2**b0 * other + 2**b1 * t
            partner = d + (1 - 2 * beta) * hop
            keep = pl.multiple_of(off + beta * size, 16)
            sent = pl.multiple_of(off + (1 - beta) * size, 16)
            steps.append((partner, keep, sent, size, place))
            off = off + beta * size
            place += size
        return steps

    def ring_copy(c, s):
        if s < bits:
            partner, keep, sent, size, place = plan(c)[s]
            src, dst = mine.at[c, pl.ds(sent, size)], ring_in.at[c, pl.ds(place, size)]
        else:
            partner, keep, sent, size, place = plan(c)[2 * bits - 1 - s]
            src, dst = core_in.at[c, pl.ds(keep, size)], core_in.at[c, pl.ds(keep, size)]
        return pltpu.make_async_remote_copy(
            src_ref=src, dst_ref=dst, send_sem=ring_send.at[c, s], recv_sem=ring_recv.at[c, s],
            device_id=(partner, t), device_id_type=MESH,
        )

    def add_in(c, dst, dst_off, size, src, src_off):
        step = math.gcd(size, 384)

        def body(i, _):
            a = pl.ds(pl.multiple_of(dst_off + i * step, 16), step)
            b = pl.ds(pl.multiple_of(src_off + i * step, 16), step)
            dst[c, a, :] = (mine[c, a, :].astype(F32) + src[c, b, :].astype(F32)).astype(BF16)
            return 0

        lax.fori_loop(0, size // step, body, 0)

    def out_copies(c):
        dst = []
        if c < n_cols:
            for g in range(groups):
                dst.append((g * CH, CH, gd_o.at[pl.ds(c * CH, CH), pl.ds(g * 128, 128)]))
        elif c < 2 * n_cols:
            for g in range(CH // 128):
                col = (c - n_cols) * CH + g * 128
                dst.append((g * width, width, gu_o.at[:, pl.ds(col, 128)]))
        else:
            j = c - 2 * n_cols
            for g in range(3):
                dst.append((g * width, width, gq_o.at[g, :, pl.ds(j * 128, 128)]))
            for g in range(groups):
                dst.append(
                    (3 * width + g * 128, 128, go_o.at[pl.ds(j * 128, 128), pl.ds(g * 128, 128)])
                )
        return [
            pltpu.make_async_copy(core_in.at[c, pl.ds(o, n)], r, out_sem.at[c, i])
            for i, (o, n, r) in enumerate(dst)
        ]

    begun = {}
    now = [0]

    def advance(c, a):
        if a == 0:
            core_copy(c).wait()
            add_in(c, mine, 0, rows_c, core_in, 0)
        else:
            ring_copy(c, a - 1).wait()
            if a <= bits:
                _, keep, _, size, place = plan(c)[a - 1]
                add_in(c, core_in if a == bits else mine, keep, size, ring_in, place)
        if a < 2 * bits:
            ring_copy(c, a).start()
        else:
            for cp in out_copies(c):
                cp.start()

    def step(c):
        a = begun[c]
        assert a <= 2 * bits
        advance(c, a)
        begun[c] = a + 1

    def mark():
        at = now[0]
        now[0] += 1
        if table is not None:
            todo = table[at]
        elif at % 2 == 0:
            todo = [c for c in sorted(begun) if begun[c] <= 2 * bits]
        else:
            todo = ()
        for c in todo:
            step(c)

    def finish_all():
        for c in table[now[0]] if table is not None else ():
            step(c)
        while any(a <= 2 * bits for a in begun.values()):
            for c in sorted(begun):
                if begun[c] <= 2 * bits:
                    step(c)

    def begin(c):
        core_copy(c).start()

    def put(ref, at, val):
        n = val.shape[0]
        for g in range(val.shape[1] // 128):
            ref[at + g * n : at + (g + 1) * n, :] = val[:, g * 128 : (g + 1) * 128].astype(BF16)

    gain1 = vecs[0:1, :]
    met = [False]

    def meet():
        if not met[0]:
            pl.semaphore_wait(barrier, n_dev - 1)
            met[0] = True

    def feed_forward(act, dg, hl, hlt, wuv, wdv):
        first = load(
            [(g2_i, g2), (act_i, act), (dr2_i, dr), (hl_i, hl), (dg_i, dg), (wd, wdv.at[t]),
             (wd_p, wdv.at[other]), (wu, wuv.at[t]), (wu_p, wuv.at[other])], 0,
        )
        first[0].wait()
        first[1].wait()
        mark()
        for c in range(n_cols):
            for h, ref in ((other, stage.at[c % 3]), (t, mine.at[c])):
                col = pl.ds(pl.multiple_of(h * ff_half + c * CH, CH), CH)
                put(ref, 0, dot_tn(act[:, col], g2[...]))
                if h is other:
                    meet()
                    begin(c)
                else:
                    begun[c] = 0
                mark()
        for cp in first[2:]:
            cp.wait()
        for k in range(groups):
            cols = slice(k * 128, (k + 1) * 128)
            hlt[cols, :] = hl[:, cols].astype(F32).T.astype(BF16)
        mark()
        for k in range(n_cols):
            c = n_cols + k
            for h, ref in ((other, stage.at[c % 3]), (t, mine.at[c])):
                col = pl.ds(pl.multiple_of(h * ff_half + k * CH, CH), CH)
                for b in range(full // 512):
                    rows = slice(b * 512, (b + 1) * 512)
                    da = dot_nt(g2[rows, :], wdv[h, k * CH : (k + 1) * CH, :])
                    dp = (da * dg[rows, col].astype(F32)).astype(BF16)
                    dg[rows, col] = dp
                    dr[rows, :] += dot_nt(dp, wuv[h, :, k * CH : (k + 1) * CH])
                mark()
                put(ref, 0, dot_nn(hlt[...], dg[:, col]))
                if h is other:
                    begin(c)
                else:
                    begun[c] = 0
                mark()

    vm = pltpu.VMEM
    ff = 2 * ff_half
    pl.run_scoped(
        feed_forward, vm((full, ff), BF16), vm((full, ff), BF16), vm((full, width), BF16),
        vm((width, full), BF16), vm((2,) + wu.shape, BF16), vm((2,) + wd.shape, BF16),
    )

    def norm_and_out(n1, rs1, ctxv, mav, wov, gov):
        first = load(
            [(n1_i, n1), (rs1_i, rs1), (ma_i, mav), (wo, wov.at[t]), (wo_p, wov.at[other]),
             (ctx_i, ctxv)], 9,
        )
        for cp in first[:3]:
            cp.wait()

        def norm_one_back(b, sums):
            rows = pl.ds(pl.multiple_of(b * 256, 256), 256)
            dh = dr[rows, :]
            n = n1[rows, :]
            g = dh * gain1
            r = (
                g - jnp.mean(g, axis=1, keepdims=True) - n * jnp.mean(g * n, axis=1, keepdims=True)
            ) * rs1[rows, :1]
            dr[rows, :] = r
            g2[rows, :] = (r * (mav[rows, :].astype(F32) * INV_KEEP)).astype(BF16)
            return (
                sums[0] + jnp.sum(dh * n, axis=0, keepdims=True),
                sums[1] + jnp.sum(dh, axis=0, keepdims=True),
            )

        zero = jnp.zeros((1, width), F32)
        gg1, gs1 = lax.fori_loop(0, full // 256, norm_one_back, (zero, zero))
        for i, row in enumerate((gg1, gs1, ng2[0:1, :], ng2[1:2, :])):
            for g in range(groups):
                nsend[i * groups + g : i * groups + g + 1, :] = row[:, g * 128 : (g + 1) * 128]
        nall[me] = nsend[...]
        lax.fori_loop(1, n_dev, lambda k, _: push(k, 0), 0)
        for cp in first[3:]:
            cp.wait()
        mark()
        lane = lax.broadcasted_iota(jnp.int32, (full, 128), 1)
        seg = (
            (lax.broadcasted_iota(jnp.int32, (128, 128), 0) < 64)
            != (lax.broadcasted_iota(jnp.int32, (128, 128), 1) < 64)
        ).astype(F32).astype(BF16)
        for g in range(groups):
            h, j = g // pairs, g % pairs
            cf = ctxv[g]
            gov[g * 128 : (g + 1) * 128, :] = dot_tn(cf.astype(BF16), g2[...]).astype(BF16)
            dc = dot_nt(g2[...], wov[h, j * 128 : (j + 1) * 128, :]).astype(BF16).astype(F32)
            hi, mid, lo = split_three(dc * cf)
            delta = (
                dot_nn(hi.astype(BF16), seg) + dot_nn(mid.astype(BF16), seg)
                + dot_nn(lo.astype(BF16), seg)
            )
            hi, mid, lo = split_three(delta)
            for a in range(2):
                own = (lane < 64) if a == 0 else (lane >= 64)
                z = 64 if a == 0 else 0
                extra = jnp.where(
                    lane == z, hi,
                    jnp.where(lane == z + 1, mid, jnp.where(lane == z + 2, lo, 0.0)),
                )
                dobv[2 * g + a] = jnp.where(own, dc, extra).astype(BF16)
            if g < groups - 1:
                mark()
        for j in range(pairs):
            c = 2 * n_cols + j
            for h, ref in ((other, stage.at[c % 3]), (t, mine.at[c])):
                row = pl.ds(pl.multiple_of((h * pairs + j) * 128, 128), 128)
                for g in range(groups):
                    ref[3 * width + g * 128 : 3 * width + (g + 1) * 128, :] = gov[
                        row, g * 128 : (g + 1) * 128
                    ]
        mark()

    def push(k, what):
        lin = lax.rem(me + k, n_dev)
        c = pltpu.make_async_remote_copy(
            src_ref=nsend, dst_ref=nall.at[me], send_sem=nsend_sem.at[k], recv_sem=nrecv_sem.at[me],
            device_id=(lin // 2, lax.rem(lin, 2)), device_id_type=MESH,
        )
        if what == 0:
            c.start()
        else:
            c.wait_send()
        return 0

    def arrive(k, _):
        lin = lax.rem(me + k, n_dev)
        pltpu.make_async_remote_copy(
            src_ref=nsend, dst_ref=nall.at[lin], send_sem=nsend_sem.at[k],
            recv_sem=nrecv_sem.at[lin], device_id=(lin // 2, lax.rem(lin, 2)), device_id_type=MESH,
        ).wait_recv()
        return 0

    pl.run_scoped(
        norm_and_out, vm((full, width), F32), vm((full, 128), F32), vm((groups, full, 128), F32),
        vm((full, width), BF16), vm((2,) + wo.shape, BF16), vm((width, width), BF16),
    )

    def attention(dq3, qbv, qkvv, xv, xt):
        first = load([(qkv_i, qkvv), (qb_i, qbv), (x0_i, xv)], 15)
        length = lens[d]
        lane = lax.broadcasted_iota(jnp.int32, (full, 128), 1)
        bias = jnp.where(
            lax.broadcasted_iota(jnp.int32, (full, 128), 0) < length, 0.0, MASKED_SCORE
        )
        kb = 512
        low_half = lax.broadcasted_iota(jnp.int32, (kb, 128), 1) < 64
        for cp in first:
            cp.wait()
        for g in range(groups):
            cols = slice(g * 128, (g + 1) * 128)
            xt[cols, :] = (xv[:, cols].astype(F32) * INV_KEEP).T.astype(BF16)
        mark()

        def head_pair(h, j):
            i = h * pairs + j

            def part(c):
                return qkvv[h, :, c * hw + j * 128 : c * hw + (j + 1) * 128]

            k2f = part(1).astype(F32)
            k2t = k2f.T.astype(BF16)
            v2f = part(2).astype(F32)
            dks, dvs, dqs = [], [], []
            for a in range(2):
                own = (lane < 64) if a == 0 else (lane >= 64)
                z = 64 if a == 0 else 0
                minus = jnp.where(jnp.logical_and(lane >= z, lane < z + 3), -1.0, 0.0)
                ka = jnp.where(own, k2f, jnp.where(lane == z + 3, bias, minus)).astype(BF16)
                va = jnp.where(own, v2f, minus).astype(BF16)
                qa = qbv[2 * i + a]
                da = dobv[2 * i + a]
                dk, dv = [], []
                dqt = None
                for b in range(full // kb):
                    rows = slice(b * kb, (b + 1) * kb)
                    p = jnp.exp(dot_nt(ka[rows], qa))
                    ds = (p * dot_nt(va[rows], da)).astype(BF16)
                    dv.append(dot_nn(p.astype(BF16), da))
                    dk.append(dot_nn(ds, qa))
                    term = dot_nn(k2t[a * 64 : (a + 1) * 64, rows], ds)
                    dqt = term if dqt is None else dqt + term
                dks.append(dk)
                dvs.append(dv)
                dqs.append(dqt)
                if a == 0:
                    mark()
            for b in range(full // kb):
                rows = slice(b * kb, (b + 1) * kb)
                dq3[i, rows, 128:256] = jnp.where(low_half, dks[0][b], dks[1][b]).astype(BF16)
                dq3[i, rows, 256:384] = jnp.where(low_half, dvs[0][b], dvs[1][b]).astype(BF16)
            dq = jnp.concatenate(dqs, axis=0) * HEAD_DIM**-0.5
            dq3[i, :, 0:128] = dq.T.astype(BF16)

        for j in range(pairs):
            c = 2 * n_cols + j
            for h, ref in ((other, stage.at[c % 3]), (t, mine.at[c])):
                head_pair(h, j)
                put(ref, 0, dot_nn(xt[...], dq3[h * pairs + j]))
                if h is other:
                    begin(c)
                else:
                    begun[c] = 0
                mark()

    def to_input(dq3, wqv, dinv, acc, gtv):
        first = load([(wq_i, wqv), (din_i, dinv)], 18)
        for cp in first:
            cp.wait()
        mark()

        def d_input(start):
            rows = pl.ds(pl.multiple_of(start, 256), 256)
            total = dr[rows, :]
            for h in range(2):
                lhs = jnp.concatenate(
                    [dq3[h * pairs + j, rows, c * 128 : (c + 1) * 128] for c in range(3) for j in range(pairs)],
                    axis=1,
                )
                total = total + dot_nt(
                    lhs, jnp.concatenate([wqv[h, c] for c in range(3)], axis=1)
                )
            return total

        for s in range(loc // 256):
            gout[s * 256 : (s + 1) * 256, :] = d_input(other * loc + s * 256).astype(BF16)
            if s < loc // 256 - 1:
                mark()
        send = pltpu.make_async_remote_copy(
            src_ref=gout, dst_ref=gin, send_sem=gt_sem.at[0], recv_sem=gt_sem.at[1],
            device_id=peer, device_id_type=MESH,
        )
        send.start()
        mark()
        for s in range(loc // 256):
            acc[s * 256 : (s + 1) * 256, :] = d_input(t * loc + s * 256)
            mark()
        send.wait()
        for s in range(loc // 256):
            rows = slice(s * 256, (s + 1) * 256)
            gtv[rows, :] = (
                jnp.where(dinv[t, rows, :] != 0, acc[rows, :], 0.0)
                + jnp.where(dinv[other, rows, :] != 0, gin[rows, :].astype(F32), 0.0)
            ) * INV_KEEP
        out = pltpu.make_async_copy(gtv, gt_o, gt_sem.at[2])
        out.start()
        mark()
        lax.fori_loop(1, n_dev, arrive, 0)
        total = nall[0]
        for k in range(1, n_dev):
            total = total + nall[k]
        ng_o[...] = total
        finish_all()
        out.wait()

    def projections(dq3):
        pl.run_scoped(
            functools.partial(attention, dq3), vm((2 * groups, full, 128), BF16),
            vm(qkv_i.shape, BF16), vm((full, width), BF16), vm((width, full), BF16),
        )
        pl.run_scoped(
            functools.partial(to_input, dq3), vm(wq_i.shape, BF16), vm(din_i.shape, jnp.int32),
            vm((loc, width), F32), vm((loc, width), F32),
        )

    pl.run_scoped(projections, vm((groups, full, 384), BF16))
    for c in range(n_chunks):
        for cp in out_copies(c):
            cp.wait()
    lax.fori_loop(1, n_dev, lambda k, _: push(k, 1), 0)


def back(
    lengths, vecs, ng2, g2, dr2, act, dg, hl, n1, rs1, ctx, ma, wo, wo_p, wu, wu_p, wd, wd_p, qb,
    qkv, x0, wq, d_in, n_dp,
):
    full, width = x0.shape
    loc = full // 2
    groups = width // 128
    bits = n_dp.bit_length() - 1
    n_dev = 2 * n_dp
    n_chunks = 2 * (wu.shape[1] // CH) + groups // 2
    rows_c = CH * width // 128
    sds = jax.ShapeDtypeStruct
    anyspec = pl.BlockSpec(memory_space=pl.ANY)
    vspec = pl.BlockSpec(memory_space=pltpu.VMEM)
    vm = pltpu.VMEM
    dma = pltpu.SemaphoreType.DMA
    return pl.pallas_call(
        back_kernel,
        out_shape=[
            sds(wq.shape[1:], BF16), sds(wo.shape, BF16), sds(wu.shape, BF16), sds(wd.shape, BF16),
            sds((loc, width), F32), sds((4 * groups, 128), F32),
        ],
        in_specs=[pl.BlockSpec(memory_space=pltpu.SMEM), vspec, vspec] + [anyspec] * 20,
        out_specs=[anyspec] * 5 + [vspec],
        scratch_shapes=[
            vm((n_chunks, rows_c, 128), BF16), vm((n_chunks, rows_c, 128), BF16),
            vm((n_chunks, rows_c, 128), BF16), vm((3, rows_c, 128), BF16),
            vm((full, width), BF16), vm((full, width), F32), vm(qb.shape, BF16),
            vm((loc, width), BF16), vm((loc, width), BF16),
            vm((4 * groups, 128), F32), vm((n_dev, 4 * groups, 128), F32),
            dma((20,)), dma((n_chunks,)), dma((n_chunks,)), dma((n_chunks, 2 * bits)),
            dma((n_chunks, 2 * bits)), dma((n_chunks, 9)), dma((n_dev,)), dma((n_dev,)), dma((3,)),
        ],
        compiler_params=pltpu.CompilerParams(
            collective_id=2, has_side_effects=True, vmem_limit_bytes=VMEM_LIMIT
        ),
        name="back",
    )(
        lengths, vecs, ng2, g2, dr2, act, dg, hl, n1, rs1, ctx, ma, wo, wo_p, wu, wu_p, wd, wd_p,
        qb, qkv, x0, wq, d_in,
    )


def finish_kernel(n_parts, *refs):
    n = len(n_parts)
    srcs, dsts = refs[:n], refs[n : 2 * n]
    narrow, wide = refs[2 * n : 3 * n], refs[3 * n : 4 * n]
    in_sem, out_sem = refs[4 * n :]

    def piece(i, k):
        rows = srcs[i].shape[0] // n_parts[i]
        return pl.ds(k * rows, rows)

    todo = [(i, k) for i in range(n) for k in range(n_parts[i])]
    loads = []
    for m, (i, k) in enumerate(todo):
        r = piece(i, k)
        loads.append(pltpu.make_async_copy(srcs[i].at[r], narrow[i].at[r], in_sem.at[m]))
        loads[-1].start()
    saves = []
    for m, (i, k) in enumerate(todo):
        r = piece(i, k)
        loads[m].wait()
        from_ref = narrow[i]
        if srcs[i].dtype != dsts[i].dtype:
            wide[i][r] = narrow[i][r].astype(F32)
            from_ref = wide[i]
        saves.append(pltpu.make_async_copy(from_ref.at[r], dsts[i].at[r], out_sem.at[m]))
        saves[-1].start()
    for c in saves:
        c.wait()


def finish(arrays, kinds, n_parts):
    sds = jax.ShapeDtypeStruct
    anyspec = pl.BlockSpec(memory_space=pl.ANY)
    vm = pltpu.VMEM
    dma = pltpu.SemaphoreType.DMA
    n = len(arrays)
    wide = [
        vm(a.shape if a.dtype != k else (8, 128), F32) for a, k in zip(arrays, kinds)
    ]
    return pl.pallas_call(
        functools.partial(finish_kernel, n_parts),
        out_shape=[sds(a.shape, k) for a, k in zip(arrays, kinds)],
        in_specs=[anyspec] * n,
        out_specs=[anyspec] * n,
        scratch_shapes=[vm(a.shape, a.dtype) for a in arrays] + wide
        + [dma((sum(n_parts),)), dma((sum(n_parts),))],
        compiler_params=pltpu.CompilerParams(vmem_limit_bytes=VMEM_LIMIT),
        name="finish",
    )(*arrays)


def per_device(
    tokens, lengths, drop_in, drop_attn, drop_ffn, qkv_weight, out_weight, up_weight, down_weight,
    gain_first, shift_first, gain_second, shift_second, cotangent,
):
    n_dp = lax.axis_size("dp")
    width = tokens.shape[2]
    wq = jnp.transpose(qkv_weight, (1, 0, 2))
    x0, ma, mf, cot_p, wqf, wo_p, wu_p, wd_p, qkv, qb, ctx = front(
        lengths, tokens[0], drop_in[0], drop_attn[0], drop_ffn[0], cotangent[0],
        wq, out_weight, up_weight, down_weight,
    )
    lens_b = jnp.broadcast_to(lengths.astype(F32)[:, None], (n_dp, 128))
    vecs = jnp.stack([gain_first, shift_first, gain_second, shift_second] * 2)
    lay, stats, act, dg, hl, n1, rs1, g2, dr2, ng2 = middle(
        lengths, lens_b, vecs, ctx, x0, ma, mf, cotangent[0], cot_p, out_weight, wo_p,
        up_weight, wu_p, down_weight, wd_p, n_dp,
    )
    gq, go, gu, gd, gt, norms = back(
        lengths, vecs, ng2, g2, dr2, act, dg, hl, n1, rs1, ctx, ma, out_weight, wo_p,
        up_weight, wu_p, down_weight, wd_p, qb, qkv, x0, wqf, drop_in[0], n_dp,
    )
    norms = norms.reshape(4, width)
    lay, gt, gq, go, gu, gd = finish(
        [lay, gt, gq, go, gu, gd], [BF16, F32, F32, F32, F32, F32], [2, 2, 3, 1, 3, 3]
    )
    return (
        lay[None], gt[None], jnp.transpose(gq, (1, 0, 2)), go, gu, gd,
        norms[0], norms[1], norms[2], norms[3],
        stats[0, 0], stats[1, 0], stats[2, 0],
    )


def solution(mesh):
    act = P("dp", None, "tensor", None)
    in_specs = (
        P("dp", "tensor", None), P(), act, act, act,
        P(None, None, "tensor"), P("tensor", None), P(None, "tensor"), P("tensor", None),
        P(), P(), P(), P(), act,
    )
    out_specs = (
        act, P("dp", "tensor", None),
        P(None, None, "tensor"), P("tensor", None), P(None, "tensor"), P("tensor", None),
        P(), P(), P(), P(), P(), P(), P(),
    )
    return jax.shard_map(
        per_device, mesh=mesh, in_specs=in_specs, out_specs=out_specs, check_vma=False
    )
```

```python
import functools
import math

import jax
import jax.numpy as jnp
from jax import lax
from jax.experimental import pallas as pl
from jax.experimental.pallas import tpu as pltpu
from jax.sharding import PartitionSpec as P

HEAD_DIM = 64
INV_KEEP = 1.0 / 0.9
SOFTMAX_WARMTH = 0.05
EPSILON = 1e-06
MASKED_SCORE = -1e30
MESH = pl.DeviceIdType.MESH
F32 = jnp.float32
BF16 = jnp.bfloat16
VMEM_LIMIT = 60 * 2**20
HIGHEST = lax.Precision.HIGHEST

TAIL_P = 0.3
TAIL = (
    0.11962929778234735,
    0.12075397394392673,
    0.09991336806236217,
    0.1285620774207718,
    -0.05368457414666341,
    0.20635459819946347,
    -0.15720376083821283,
    0.03567494667807555,
)


def dot_nn(a, b):
    return jnp.dot(a, b, preferred_element_type=F32)


def dot_nt(a, b):
    return lax.dot_general(a, b, (((1,), (1,)), ((), ())), preferred_element_type=F32)


def dot_tn(a, b):
    return lax.dot_general(a, b, (((0,), (0,)), ((), ())), preferred_element_type=F32)


def gelu_pair(x):
    z = jnp.abs(x)
    bell = jnp.exp2(x * x * (-0.5 * math.log2(math.e)))
    t = pl.reciprocal(1.0 + TAIL_P * z, approx=True)
    acc = jnp.full_like(t, TAIL[-1])
    for c in TAIL[-2::-1]:
        acc = acc * t + c
    tail = acc * t * bell
    cdf = jnp.where(x < 0.0, tail, 1.0 - tail)
    return x * cdf, cdf + x * (bell * (1.0 / math.sqrt(2.0 * math.pi)))


def split_three(v):
    hi = v.astype(BF16).astype(F32)
    rest = v - hi
    mid = rest.astype(BF16).astype(F32)
    return hi, mid, rest - mid


def front_kernel(
    lens, tok, d_in, d_at, d_ff, cot, wq, wo, wu, wd,
    x0_o, ma_o, mf_o, cot_o, wq_o, wo_o, wu_o, wd_o, qkv_o, qb_o, ctx_o,
    xv, xl, wv, qs, ms, tokv, st, qbv, ctxv, in_sem, loc_sem, send_sem, recv_sem, out_sem,
):
    d = lax.axis_index("dp")
    t = lax.axis_index("tensor")
    other = 1 - t
    peer = (d, other)
    loc = tok.shape[0]
    full = 2 * loc
    hw = wq.shape[2]
    pairs = hw // 128

    barrier = pltpu.get_barrier_semaphore()
    pl.semaphore_signal(barrier, inc=1, device_id=peer, device_id_type=MESH)

    loads = [
        pltpu.make_async_copy(tok, tokv, in_sem.at[0]),
        pltpu.make_async_copy(d_in, ms.at[0], in_sem.at[1]),
        pltpu.make_async_copy(wq, wv.at[t], in_sem.at[2]),
        pltpu.make_async_copy(d_at, ms.at[1], in_sem.at[3]),
        pltpu.make_async_copy(d_ff, ms.at[2], in_sem.at[4]),
    ]
    for c in loads:
        c.start()
    own_rows = pl.ds(pl.multiple_of(t * loc, loc), loc)

    def remote(i, src, dst):
        return pltpu.make_async_remote_copy(
            src_ref=src, dst_ref=dst, send_sem=send_sem.at[i], recv_sem=recv_sem.at[i],
            device_id=peer, device_id_type=MESH,
        )

    pl.semaphore_wait(barrier, 1)
    send_wq = remote(0, wq, wv.at[t])
    send_wq.start()
    loads[0].wait()
    loads[1].wait()
    st[0] = jnp.where(ms[0, other] != 0, tokv[...].astype(F32), 0.0).astype(BF16)
    send_x = remote(1, st.at[0], xv.at[own_rows])
    send_x.start()
    own_x = jnp.where(ms[0, t] != 0, tokv[...].astype(F32), 0.0)
    xv[own_rows, :] = own_x.astype(BF16)
    xl[own_rows, :] = (own_x * INV_KEEP).astype(BF16)
    loads[3].wait()
    st[1] = ms[1, other].astype(F32).astype(BF16)
    st[2] = ms[1, t].astype(F32).astype(BF16)
    loads[4].wait()
    st[3] = ms[2, other].astype(F32).astype(BF16)
    st[4] = ms[2, t].astype(F32).astype(BF16)
    sends = [
        remote(2, wo, wo_o),
        remote(3, st.at[1], ma_o.at[own_rows]),
        remote(4, wu, wu_o),
        remote(5, wd, wd_o),
        remote(6, st.at[3], mf_o.at[own_rows]),
        remote(7, cot.at[other], cot_o),
    ]
    for c in sends:
        c.start()
    more = [
        pltpu.make_async_copy(st.at[2], ma_o.at[own_rows], loc_sem.at[0]),
        pltpu.make_async_copy(st.at[4], mf_o.at[own_rows], loc_sem.at[1]),
    ]
    for c in more:
        c.start()

    loads[2].wait()
    send_wq.wait_recv()
    send_x.wait_recv()
    oth_rows = pl.ds(pl.multiple_of(other * loc, loc), loc)
    xl[oth_rows, :] = (xv[oth_rows, :].astype(F32) * INV_KEEP).astype(BF16)
    save_x = pltpu.make_async_copy(xv, x0_o, loc_sem.at[2])
    save_x.start()
    save_w = pltpu.make_async_copy(wv, wq_o, loc_sem.at[3])
    save_w.start()

    for h in range(2):
        for c in range(3):
            def project(b, _, h=h, c=c):
                rows = pl.ds(pl.multiple_of(b * 512, 512), 512)
                qs[h, rows, c * hw : (c + 1) * hw] = dot_nn(
                    xl[rows, :], wv[h, c]
                ).astype(BF16)
                return 0

            lax.fori_loop(0, full // 512, project, 0)
    save_qkv = pltpu.make_async_copy(qs, qkv_o, loc_sem.at[4])
    save_qkv.start()

    length = lens[d]
    bias = jnp.where(
        lax.broadcasted_iota(jnp.int32, (full, 128), 0) < length, 0.0, MASKED_SCORE
    )
    lane = lax.broadcasted_iota(jnp.int32, (full, 128), 1)
    lane_q = lax.broadcasted_iota(jnp.int32, (512, 128), 1)

    def out_copies(i):
        return [
            pltpu.make_async_copy(qbv.at[pl.ds(2 * i, 2)], qb_o.at[pl.ds(2 * i, 2)], out_sem.at[0, i]),
            pltpu.make_async_copy(ctxv.at[i], ctx_o.at[i], out_sem.at[1, i]),
        ]

    def head_pair(i, _):
        h = i // pairs
        off = (i - h * pairs) * 128

        def part(c):
            return qs[h, :, pl.ds(pl.multiple_of(c * hw + off, 128), 128)].astype(F32)

        q2 = part(0) * HEAD_DIM**-0.5
        k2 = part(1)
        v2 = part(2)
        keys, vals, ques = [], [], []
        for a in range(2):
            own = (lane < 64) if a == 0 else (lane >= 64)
            first = 64 if a == 0 else 0
            keys.append(jnp.where(own, k2, jnp.where(lane == first, bias, 0.0)).astype(BF16))
            ques.append(jnp.where(own, q2, jnp.where(lane == first, 1.0, 0.0)).astype(BF16))
            vals.append(jnp.where(own, v2, 1.0).astype(BF16))
        for b in range(full // 512):
            rows = slice(b * 512, (b + 1) * 512)
            tops, outs = [], []
            for a in range(2):
                s = dot_nt(ques[a][rows], keys[a])
                top = jnp.max(s, axis=1, keepdims=True)
                p = jnp.exp(s - top).astype(BF16)
                outs.append(dot_nn(p, vals[a]))
                tops.append(top)
            low_half = lane_q < 64
            num = jnp.where(low_half, outs[0], outs[1])
            den = pltpu.roll(jnp.where(low_half, outs[1], outs[0]), 64, 1)
            ctxv[i, rows, :] = num / den
            for a in range(2):
                hi, mid, lo = split_three(tops[a] + jnp.log(outs[a]))
                own = low_half if a == 0 else jnp.logical_not(low_half)
                first = 64 if a == 0 else 0
                extra = jnp.where(
                    lane_q == first, hi,
                    jnp.where(lane_q == first + 1, mid,
                              jnp.where(lane_q == first + 2, lo,
                                        jnp.where(lane_q == first + 3, 1.0, 0.0))),
                )
                qbv[2 * i + a, rows, :] = jnp.where(own, q2[rows], extra).astype(BF16)
        for c in out_copies(i):
            c.start()
        return 0

    lax.fori_loop(0, 2 * pairs, head_pair, 0)

    def drain(i, _):
        for c in out_copies(i):
            c.wait()
        return 0

    lax.fori_loop(0, 2 * pairs, drain, 0)
    send_wq.wait_send()
    send_x.wait_send()
    for c in sends:
        c.wait()
    for c in more + [save_x, save_w, save_qkv]:
        c.wait()


def front(lengths, tok, d_in, d_at, d_ff, cot, wq, wo, wu, wd):
    loc, width = tok.shape
    full = 2 * loc
    half_w = 3 * wq.shape[2]
    groups = width // 128
    sds = jax.ShapeDtypeStruct
    anyspec = pl.BlockSpec(memory_space=pl.ANY)
    outs = [
        sds((full, width), BF16), sds((full, width), BF16), sds((full, width), BF16),
        sds((loc, width), BF16),
        sds((2,) + wq.shape, BF16), sds(wo.shape, BF16), sds(wu.shape, BF16), sds(wd.shape, BF16),
        sds((2, full, half_w), BF16), sds((2 * groups, full, 128), BF16),
        sds((groups, full, 128), F32),
    ]
    return pl.pallas_call(
        front_kernel,
        out_shape=outs,
        in_specs=[pl.BlockSpec(memory_space=pltpu.SMEM)] + [anyspec] * 9,
        out_specs=[anyspec] * len(outs),
        scratch_shapes=[
            pltpu.VMEM((full, width), BF16), pltpu.VMEM((full, width), BF16),
            pltpu.VMEM((2,) + wq.shape, BF16), pltpu.VMEM((2, full, half_w), BF16),
            pltpu.VMEM((3, 2, loc, width), jnp.int32), pltpu.VMEM((loc, width), BF16),
            pltpu.VMEM((5, loc, width), BF16),
            pltpu.VMEM((2 * groups, full, 128), BF16), pltpu.VMEM((groups, full, 128), F32),
            pltpu.SemaphoreType.DMA((5,)), pltpu.SemaphoreType.DMA((5,)),
            pltpu.SemaphoreType.DMA((8,)), pltpu.SemaphoreType.DMA((8,)),
            pltpu.SemaphoreType.DMA((2, groups)),
        ],
        compiler_params=pltpu.CompilerParams(
            collective_id=0, has_side_effects=True, vmem_limit_bytes=VMEM_LIMIT
        ),
        name="front",
    )(lengths, tok, d_in, d_at, d_ff, cot, wq, wo, wu, wd)


CH = 512


def middle_kernel(
    lens, ga1, sh1, ga2, sh2, ctx, x0, ma, mf, cot, cot_p, wo, wo_p, wu, wu_p, wd, wd_p,
    lay_o, loss_o, act_o, dg_o, hl_o, n1_o, rs1_o, g2_o, dr2_o, ng_o,
    ctxv, x0v, mav, mfv, cotv, wov, wuv, wdv,
    n1, n2, rs1, rs2, hl, act, dg, g2, dr2, yb, sbuf, pool_all, facc,
    in_sem, lay_sem, send_sem, recv_sem, row_sem, out_sem,
):
    d = lax.axis_index("dp")
    t = lax.axis_index("tensor")
    other = 1 - t
    peer = (d, other)
    n_dp = lax.axis_size("dp")
    n_dev = 2 * n_dp
    full, width = x0v.shape
    loc = full // 2
    groups = width // 128
    ff_half = wuv.shape[2]
    n_ch = 2 * ff_half // CH
    per_half = ff_half // CH
    me = d * 2 + t

    barrier = pltpu.get_barrier_semaphore()

    def greet(k, _):
        lin = lax.rem(me + k, n_dev)
        pl.semaphore_signal(
            barrier, inc=1, device_id=(lin // 2, lax.rem(lin, 2)), device_id_type=MESH
        )
        return 0

    lax.fori_loop(1, n_dev, greet, 0)

    own_rows = pl.ds(pl.multiple_of(t * loc, loc), loc)
    oth_rows = pl.ds(pl.multiple_of(other * loc, loc), loc)
    srcs = (ctx, wo, wo_p, x0, ma, wu, wu_p, wd, wd_p, mf, cot.at[t], cot_p)
    dsts = (
        ctxv, wov.at[t], wov.at[other], x0v, mav, wuv.at[t], wuv.at[other], wdv.at[t],
        wdv.at[other], mfv, cotv.at[own_rows], cotv.at[oth_rows],
    )
    loads = [pltpu.make_async_copy(s, v, in_sem.at[i]) for i, (s, v) in enumerate(zip(srcs, dsts))]
    for c in loads:
        c.start()
    gain1, shift1, gain2, shift2 = (r[...].reshape(1, width) for r in (ga1, sh1, ga2, sh2))
    length = lens[d]

    for c in loads[:5]:
        c.wait()

    def norm_one(b, _):
        rows = pl.ds(pl.multiple_of(b * 256, 256), 256)
        c2 = jnp.concatenate([ctxv[g, rows, :].astype(BF16) for g in range(groups)], axis=1)
        branch = dot_nn(c2, wov[...].reshape(width, width))
        r = (x0v[rows, :].astype(F32) + branch * mav[rows, :].astype(F32)) * INV_KEEP
        cen = r - jnp.mean(r, axis=1, keepdims=True)
        rstd = lax.rsqrt(jnp.mean(cen * cen, axis=1, keepdims=True) + EPSILON)
        n = cen * rstd
        n1[rows, :] = n
        rs1[rows, :] = jnp.broadcast_to(rstd, (256, 128))
        hl[rows, :] = (n * gain1 + shift1).astype(BF16)
        return 0

    lax.fori_loop(0, full // 256, norm_one, 0)
    saves = [
        pltpu.make_async_copy(s, o, out_sem.at[i])
        for i, (s, o) in enumerate(((hl, hl_o), (n1, n1_o), (rs1, rs1_o)))
    ]
    for c in saves:
        c.start()
    for c in loads[5:]:
        c.wait()

    def row_copies(b):
        rows = pl.ds(pl.multiple_of(b * 512, 512), 512)
        return [
            pltpu.make_async_copy(act.at[rows], act_o.at[rows], row_sem.at[b, 0]),
            pltpu.make_async_copy(dg.at[rows], dg_o.at[rows], row_sem.at[b, 1]),
        ]

    def ffn(b, pooled):
        rows = pl.ds(pl.multiple_of(b * 512, 512), 512)
        def up(j):
            h, o = j // per_half, (j % per_half) * CH
            return dot_nn(hl[rows, :], wuv[h, :, o : o + CH])

        ahead = up(0)
        for j in range(n_ch):
            h, o = j // per_half, (j % per_half) * CH
            pre = ahead
            if j + 1 < n_ch:
                ahead = up(j + 1)
            a, da = gelu_pair(pre)
            ab = a.astype(BF16)
            act[rows, j * CH : (j + 1) * CH] = ab
            dg[rows, j * CH : (j + 1) * CH] = da.astype(BF16)
            term = dot_nn(ab, wdv[h, o : o + CH, :])
            if j == 0:
                facc[...] = term
            else:
                facc[...] += term
        for c in row_copies(b):
            c.start()
        for s in range(2):
            sub = pl.ds(pl.multiple_of(b * 512 + s * 256, 256), 256)
            r = n1[sub, :] * gain1 + shift1 + facc[s * 256 : (s + 1) * 256, :] * (
                mfv[sub, :].astype(F32) * INV_KEEP
            )
            cen = r - jnp.mean(r, axis=1, keepdims=True)
            rstd = lax.rsqrt(jnp.mean(cen * cen, axis=1, keepdims=True) + EPSILON)
            n = cen * rstd
            n2[sub, :] = n
            rs2[sub, :] = jnp.broadcast_to(rstd, (256, 128))
            y = n * gain2 + shift2
            yb[sub, :] = y.astype(BF16)
            pos = lax.broadcasted_iota(jnp.int32, (256, width), 0) + (b * 512 + s * 256)
            pooled = pooled + jnp.sum(jnp.where(pos < length, y, 0.0), axis=0, keepdims=True)
        return pooled

    pooled = lax.fori_loop(0, full // 512, ffn, jnp.zeros((1, width), F32))

    for g in range(groups):
        sbuf[g : g + 1, :] = pooled[:, g * 128 : (g + 1) * 128]
    sbuf[groups:, :] = jnp.zeros((8 - groups, 128), F32)
    slot = t * n_dp + d
    pl.semaphore_wait(barrier, n_dev - 1)

    def push(k, start):
        lin = lax.rem(me + k, n_dev)
        pd, pt = lin // 2, lax.rem(lin, 2)
        c = pltpu.make_async_remote_copy(
            src_ref=sbuf, dst_ref=pool_all.at[slot], send_sem=send_sem.at[k],
            recv_sem=recv_sem.at[slot], device_id=(pd, pt), device_id_type=MESH,
        )
        if start:
            c.start()
        else:
            c.wait_send()
        return 0

    lax.fori_loop(1, n_dev, lambda k, _: push(k, True), 0)
    lay_local = pltpu.make_async_copy(yb.at[own_rows], lay_o.at[t], lay_sem.at[0])
    lay_local.start()
    lay_send = pltpu.make_async_remote_copy(
        src_ref=yb.at[oth_rows], dst_ref=lay_o.at[t], send_sem=lay_sem.at[1],
        recv_sem=lay_sem.at[2], device_id=peer, device_id_type=MESH,
    )
    lay_send.start()
    pool_all[slot] = sbuf[...]

    def arrive(k, _):
        lin = lax.rem(me + k, n_dev)
        s = lax.rem(lin, 2) * n_dp + lin // 2
        pltpu.make_async_remote_copy(
            src_ref=sbuf, dst_ref=pool_all.at[s], send_sem=send_sem.at[k],
            recv_sem=recv_sem.at[s], device_id=(lin // 2, lax.rem(lin, 2)), device_id_type=MESH,
        ).wait_recv()
        return 0

    lax.fori_loop(1, n_dev, arrive, 0)

    pair_i = lax.broadcasted_iota(jnp.int32, (n_dp, 1), 0)
    len_col = jnp.zeros((n_dp, 1), F32)
    for k in range(n_dp):
        len_col = jnp.where(pair_i == k, lens[k].astype(F32), len_col)
    units = []
    scales = []
    for v in range(2):
        raw = jnp.concatenate(
            [pool_all[v * n_dp : (v + 1) * n_dp, g, :] for g in range(groups)], axis=1
        )
        pv = raw / len_col
        scale = lax.rsqrt(jnp.sum(pv * pv, axis=1, keepdims=True) + EPSILON)
        units.append(pv * scale)
        scales.append(scale)
    u0, u1 = units
    nt = (((1,), (1,)), ((), ()))
    row_i = lax.broadcasted_iota(jnp.int32, (n_dp, n_dp), 0)
    col_i = lax.broadcasted_iota(jnp.int32, (n_dp, n_dp), 1)
    diag = row_i == col_i
    sim = lax.dot_general(u0, u1, nt, precision=HIGHEST, preferred_element_type=F32) / SOFTMAX_WARMTH
    top = jnp.max(sim, axis=1, keepdims=True)
    raw = jnp.exp(sim - top)
    total = jnp.sum(raw, axis=1, keepdims=True)
    ce = top + jnp.log(total) - jnp.sum(jnp.where(diag, sim, 0.0), axis=1, keepdims=True)
    loss = jnp.sum(ce, axis=0, keepdims=True) / n_dp
    gap = u0 - u1
    align = jnp.sum(jnp.sum(gap * gap, axis=1, keepdims=True), axis=0, keepdims=True) / n_dp
    sq = jnp.sum(u0 * u0, axis=1, keepdims=True)
    sq_row = lax.dot_general(
        jnp.ones((n_dp, width), F32), u0 * u0, nt, precision=HIGHEST, preferred_element_type=F32
    )
    inner = lax.dot_general(u0, u0, nt, precision=HIGHEST, preferred_element_type=F32)
    pot = jnp.where(diag, 0.0, jnp.exp(-2.0 * (sq + sq_row - 2.0 * inner)))
    uni = jnp.log(
        jnp.sum(jnp.sum(pot, axis=1, keepdims=True), axis=0, keepdims=True) / (n_dp * (n_dp - 1))
    )
    stat_i = lax.broadcasted_iota(jnp.int32, (8, 128), 0)
    loss_o[...] = jnp.where(stat_i == 0, loss, jnp.where(stat_i == 1, align, uni))
    d_sim = (raw / total - jnp.where(diag, 1.0, 0.0)) / SOFTMAX_WARMTH
    d_u0 = jnp.dot(d_sim, u1, precision=HIGHEST, preferred_element_type=F32)
    d_u1 = lax.dot_general(
        d_sim, u0, (((0,), (0,)), ((), ())), precision=HIGHEST, preferred_element_type=F32
    )
    first_view = t == 0
    du = jnp.where(first_view, d_u0, d_u1)
    u = jnp.where(first_view, u0, u1)
    scale = jnp.where(first_view, scales[0], scales[1])
    d_pool = (du - u * jnp.sum(u * du, axis=1, keepdims=True)) * scale / len_col
    mine = lax.broadcasted_iota(jnp.int32, (n_dp, width), 0) == d
    pool_grad = jnp.sum(jnp.where(mine, d_pool, 0.0), axis=0, keepdims=True)

    def norm_two_back(b, sums):
        rows = pl.ds(pl.multiple_of(b * 256, 256), 256)
        pos = lax.broadcasted_iota(jnp.int32, (256, width), 0) + b * 256
        dy = cotv[rows, :].astype(F32) + jnp.where(pos < length, pool_grad, 0.0)
        n = n2[rows, :]
        g = dy * gain2
        dr = (g - jnp.mean(g, axis=1, keepdims=True) - n * jnp.mean(g * n, axis=1, keepdims=True)) * rs2[rows, :1]
        dr2[rows, :] = dr
        g2[rows, :] = (dr * (mfv[rows, :].astype(F32) * INV_KEEP)).astype(BF16)
        return (
            sums[0] + jnp.sum(dy * n, axis=0, keepdims=True),
            sums[1] + jnp.sum(dy, axis=0, keepdims=True),
        )

    zero = jnp.zeros((1, width), F32)
    gg2, gs2 = lax.fori_loop(0, full // 256, norm_two_back, (zero, zero))

    ng_o[...] = jnp.concatenate([gg2, gs2, zero, zero, zero, zero, zero, zero], axis=0)
    more = [
        pltpu.make_async_copy(g2, g2_o, out_sem.at[3]),
        pltpu.make_async_copy(dr2, dr2_o, out_sem.at[4]),
    ]
    for c in more:
        c.start()
    for b in range(full // 512):
        for c in row_copies(b):
            c.wait()
    lax.fori_loop(1, n_dev, lambda k, _: push(k, False), 0)
    lay_local.wait()
    lay_send.wait()
    for c in saves + more:
        c.wait()


def middle(
    lengths, gains, ctx, x0, ma, mf, cot, cot_p, wo, wo_p, wu, wu_p, wd, wd_p, n_dp
):
    full, width = x0.shape
    loc = full // 2
    ff = 2 * wd.shape[0]
    n_dev = 2 * n_dp
    sds = jax.ShapeDtypeStruct
    anyspec = pl.BlockSpec(memory_space=pl.ANY)
    vspec = pl.BlockSpec(memory_space=pltpu.VMEM)
    outs = [
        sds((2, loc, width), BF16), sds((8, 128), F32), sds((full, ff), BF16), sds((full, ff), BF16),
        sds((full, width), BF16), sds((full, width), F32), sds((full, 128), F32),
        sds((full, width), BF16), sds((full, width), F32), sds((8, width), F32),
    ]
    vm = pltpu.VMEM
    dma = pltpu.SemaphoreType.DMA
    return pl.pallas_call(
        middle_kernel,
        out_shape=outs,
        in_specs=[pl.BlockSpec(memory_space=pltpu.SMEM)] + [vspec] * 4 + [anyspec] * 12,
        out_specs=[anyspec, vspec] + [anyspec] * 7 + [vspec],
        scratch_shapes=[
            vm(ctx.shape, F32), vm((full, width), BF16), vm((full, width), BF16),
            vm((full, width), BF16), vm((full, width), BF16), vm((2,) + wo.shape, BF16),
            vm((2,) + wu.shape, BF16), vm((2,) + wd.shape, BF16),
            vm((full, width), F32), vm((full, width), F32), vm((full, 128), F32), vm((full, 128), F32),
            vm((full, width), BF16), vm((full, ff), BF16), vm((full, ff), BF16),
            vm((full, width), BF16), vm((full, width), F32), vm((full, width), BF16),
            vm((8, 128), F32), vm((n_dev, 8, 128), F32), vm((512, width), F32),
            dma((12,)), dma((3,)), dma((n_dev,)), dma((n_dev,)), dma((full // 512, 2)), dma((5,)),
        ],
        compiler_params=pltpu.CompilerParams(
            collective_id=1, has_side_effects=True, vmem_limit_bytes=VMEM_LIMIT
        ),
        name="middle",
    )(lengths, *gains, ctx, x0, ma, mf, cot, cot_p, wo, wo_p, wu, wu_p, wd, wd_p)


ORDERS_16 = (
    ((0, 1, 2, 3), (1, 0, 2, 3)), ((2, 0, 1, 3), (2, 1, 0, 3)),
    ((0, 1, 2, 3), (1, 0, 2, 3)), ((0, 1, 2, 3), (1, 0, 2, 3)),
    ((0, 2, 3, 1), (1, 2, 3, 0)), ((0, 1, 2, 3), (1, 0, 2, 3)),
    ((0, 1, 2, 3), (1, 0, 2, 3)), ((0, 2, 1, 3), (1, 2, 0, 3)),
    ((2, 0, 1, 3), (2, 1, 0, 3)), ((0, 2, 1, 3), (1, 2, 0, 3)),
)
TABLE_16 = (
    (), (), (), (), (), (0,),
    (), (1,), (2,), (), (0,), (),
    (3,), (2,), (1, 0), (), (4, 3), (),
    (0, 2), (1,), (5, 4, 0), (2, 3), (1,), (),
    (), (5, 4, 0), (2,), (3,), (1, 5), (4, 0, 2),
    (3, 5, 1, 4), (2, 0, 1, 4, 3), (6, 5), (2, 3, 4), (0, 5, 1), (6, 4),
    (7, 5, 2), (3, 6), (1, 4), (6, 7), (), (8, 9, 5),
    (6,), (3,), (9, 7), (), (), (5, 8, 7, 6, 9, 8, 7, 9, 8, 6, 7, 9, 6, 8, 7, 9, 8, 6, 9, 8, 7, 8, 9, 7, 8, 9),
)
LAST_PARTS = 2


def sum_plan(n_dp, n_chunks, rows):
    bits = n_dp.bit_length() - 1
    if bits == 4 and n_chunks + LAST_PARTS - 1 == len(ORDERS_16):
        part = rows // LAST_PARTS
        places = [(c, 0, rows) for c in range(n_chunks - 1)]
        places += [(n_chunks - 1, k * part, part) for k in range(LAST_PARTS)]
        return [p + o for p, o in zip(places, ORDERS_16)], TABLE_16
    plain = tuple(range(bits))

    def turn(k):
        return plain[k % bits :] + plain[: k % bits] if bits else plain

    return [(c, 0, rows, turn(2 * c), turn(2 * c + 2)) for c in range(n_chunks)], None


def back_kernel(
    lens, ga1, ng2, g2_i, dr2_i, act_i, dg_i, hl_i, n1_i, rs1_i, ctx_i, ma_i, wo, wo_p, wu, wu_p,
    wd, wd_p, qb_i, qkv_i, x0_i, wq_i, din_i,
    gq_o, go_o, gu_o, gd_o, gt_o, ng_o,
    mine, core_in, ring_in, stage, g2, dr, dobv, gin, nsend, nall,
    in_sem, core_send, core_recv, ring_send, ring_recv, out_sem, nsend_sem, nrecv_sem, gt_sem,
):
    d = lax.axis_index("dp")
    t = lax.axis_index("tensor")
    other = 1 - t
    peer = (d, other)
    n_dp = lax.axis_size("dp")
    n_dev = 2 * n_dp
    me = d * 2 + t
    full, width = g2.shape
    loc = full // 2
    ff_half = wu.shape[1]
    half_w = qkv_i.shape[2]
    hw = half_w // 3
    pairs = hw // 128
    groups = width // 128
    n_cols = ff_half // CH
    rows_c = mine.shape[1]
    bits = n_dp.bit_length() - 1
    n_chunks = mine.shape[0]
    items, table = sum_plan(n_dp, n_chunks, rows_c)

    barrier = pltpu.get_barrier_semaphore()

    def greet(k, _):
        lin = lax.rem(me + k, n_dev)
        pl.semaphore_signal(
            barrier, inc=1, device_id=(lin // 2, lax.rem(lin, 2)), device_id_type=MESH
        )
        return 0

    lax.fori_loop(1, n_dev, greet, 0)

    def load(pairs_of, first):
        copies = [
            pltpu.make_async_copy(s, v, in_sem.at[first + i]) for i, (s, v) in enumerate(pairs_of)
        ]
        for c in copies:
            c.start()
        return copies

    def core_copy(c):
        return pltpu.make_async_remote_copy(
            src_ref=stage.at[c % 3], dst_ref=core_in.at[c], send_sem=core_send.at[c],
            recv_sem=core_recv.at[c], device_id=peer, device_id_type=MESH,
        )

    def plan(i):
        steps = []
        _, off, size, o0, o1 = items[i]
        place = off
        for b0, b1 in zip(o0, o1):
            size //= 2
            beta = lax.rem(d // 2**b0, 2) * other + lax.rem(d // 2**b1, 2) * t
            hop = 2**b0 * other + 2**b1 * t
            partner = d + (1 - 2 * beta) * hop
            keep = pl.multiple_of(off + beta * size, 16)
            sent = pl.multiple_of(off + (1 - beta) * size, 16)
            steps.append((partner, keep, sent, size, place))
            off = off + beta * size
            place += size
        return steps

    def ring_copy(i, s):
        c = items[i][0]
        if s < bits:
            partner, keep, sent, size, place = plan(i)[s]
            src, dst = mine.at[c, pl.ds(sent, size)], ring_in.at[c, pl.ds(place, size)]
        else:
            partner, keep, sent, size, place = plan(i)[2 * bits - 1 - s]
            src, dst = core_in.at[c, pl.ds(keep, size)], core_in.at[c, pl.ds(keep, size)]
        return pltpu.make_async_remote_copy(
            src_ref=src, dst_ref=dst, send_sem=ring_send.at[i, s], recv_sem=ring_recv.at[i, s],
            device_id=(partner, t), device_id_type=MESH,
        )

    def add_in(c, dst, dst_off, size, src, src_off):
        step = math.gcd(size, 384)

        def body(i, _):
            a = pl.ds(pl.multiple_of(dst_off + i * step, 16), step)
            b = pl.ds(pl.multiple_of(src_off + i * step, 16), step)
            dst[c, a, :] = (mine[c, a, :].astype(F32) + src[c, b, :].astype(F32)).astype(BF16)
            return 0

        lax.fori_loop(0, size // step, body, 0)

    def out_copies(c):
        dst = []
        if c < n_cols:
            for g in range(groups):
                dst.append((g * CH, CH, gd_o.at[pl.ds(c * CH, CH), pl.ds(g * 128, 128)]))
        elif c < 2 * n_cols:
            for g in range(CH // 128):
                col = (c - n_cols) * CH + g * 128
                dst.append((g * width, width, gu_o.at[:, pl.ds(col, 128)]))
        else:
            j = c - 2 * n_cols
            for g in range(3):
                dst.append((g * width, width, gq_o.at[g, :, pl.ds(j * 128, 128)]))
            for g in range(groups):
                dst.append(
                    (3 * width + g * 128, 128, go_o.at[pl.ds(j * 128, 128), pl.ds(g * 128, 128)])
                )
        return [
            pltpu.make_async_copy(core_in.at[c, pl.ds(o, n)], r, out_sem.at[c, i])
            for i, (o, n, r) in enumerate(dst)
        ]

    begun = {}
    made = set()
    left = [sum(1 for it in items if it[0] == c) for c in range(n_chunks)]
    now = [0]

    def step(i):
        c, first, count = items[i][:3]
        a = begun.get(i, 0)
        assert c in made and a <= 2 * bits
        begun[i] = a + 1
        if a == 0:
            if first == 0:
                core_copy(c).wait()
            add_in(c, mine, first, count, core_in, first)
        else:
            ring_copy(i, a - 1).wait()
            if a <= bits:
                _, keep, _, size, place = plan(i)[a - 1]
                add_in(c, core_in if a == bits else mine, keep, size, ring_in, place)
        if a < 2 * bits:
            ring_copy(i, a).start()
        else:
            left[c] -= 1
            if left[c] == 0:
                for cp in out_copies(c):
                    cp.start()

    def mark():
        at = now[0]
        now[0] += 1
        if table is not None:
            todo = table[at]
        elif at % 2 == 0:
            todo = unfinished()
        else:
            todo = ()
        for i in todo:
            step(i)

    def unfinished():
        return [
            i for i in range(len(items)) if items[i][0] in made and begun.get(i, 0) <= 2 * bits
        ]

    def finish_all():
        for i in table[now[0]] if table is not None else ():
            step(i)
        while unfinished():
            for i in unfinished():
                step(i)

    def begin(c):
        core_copy(c).start()

    def put(ref, at, val):
        n = val.shape[0]
        for g in range(val.shape[1] // 128):
            ref[at + g * n : at + (g + 1) * n, :] = val[:, g * 128 : (g + 1) * 128].astype(BF16)

    gain1 = ga1[...].reshape(1, width)
    met = [False]

    def meet():
        if not met[0]:
            pl.semaphore_wait(barrier, n_dev - 1)
            met[0] = True

    def feed_forward(act, dg, hl, hlt, wuv, wdv):
        first = load(
            [(g2_i, g2), (act_i, act), (dr2_i, dr), (hl_i, hl), (dg_i, dg), (wd, wdv.at[t]),
             (wd_p, wdv.at[other]), (wu, wuv.at[t]), (wu_p, wuv.at[other])], 0,
        )
        first[0].wait()
        first[1].wait()
        mark()
        for c in range(n_cols):
            for h, ref in ((other, stage.at[c % 3]), (t, mine.at[c])):
                col = pl.ds(pl.multiple_of(h * ff_half + c * CH, CH), CH)
                put(ref, 0, dot_tn(act[:, col], g2[...]))
                if h is other:
                    meet()
                    begin(c)
                else:
                    made.add(c)
                mark()
        for cp in first[2:]:
            cp.wait()
        for k in range(groups):
            cols = slice(k * 128, (k + 1) * 128)
            hlt[cols, :] = hl[:, cols].astype(F32).T.astype(BF16)
        mark()
        for k in range(n_cols):
            c = n_cols + k
            for h, ref in ((other, stage.at[c % 3]), (t, mine.at[c])):
                col = pl.ds(pl.multiple_of(h * ff_half + k * CH, CH), CH)
                for b in range(full // 512):
                    rows = slice(b * 512, (b + 1) * 512)
                    da = dot_nt(g2[rows, :], wdv[h, k * CH : (k + 1) * CH, :])
                    dp = (da * dg[rows, col].astype(F32)).astype(BF16)
                    dg[rows, col] = dp
                    dr[rows, :] += dot_nt(dp, wuv[h, :, k * CH : (k + 1) * CH])
                mark()
                put(ref, 0, dot_nn(hlt[...], dg[:, col]))
                if h is other:
                    begin(c)
                else:
                    made.add(c)
                mark()

    vm = pltpu.VMEM
    ff = 2 * ff_half
    pl.run_scoped(
        feed_forward, vm((full, ff), BF16), vm((full, ff), BF16), vm((full, width), BF16),
        vm((width, full), BF16), vm((2,) + wu.shape, BF16), vm((2,) + wd.shape, BF16),
    )

    def norm_and_out(n1, rs1, ctxv, mav, wov, gov):
        first = load(
            [(n1_i, n1), (rs1_i, rs1), (ma_i, mav), (wo, wov.at[t]), (wo_p, wov.at[other]),
             (ctx_i, ctxv)], 9,
        )
        for cp in first[:3]:
            cp.wait()

        def norm_one_back(b, sums):
            rows = pl.ds(pl.multiple_of(b * 256, 256), 256)
            dh = dr[rows, :]
            n = n1[rows, :]
            g = dh * gain1
            r = (
                g - jnp.mean(g, axis=1, keepdims=True) - n * jnp.mean(g * n, axis=1, keepdims=True)
            ) * rs1[rows, :1]
            dr[rows, :] = r
            g2[rows, :] = (r * (mav[rows, :].astype(F32) * INV_KEEP)).astype(BF16)
            return (
                sums[0] + jnp.sum(dh * n, axis=0, keepdims=True),
                sums[1] + jnp.sum(dh, axis=0, keepdims=True),
            )

        zero = jnp.zeros((1, width), F32)
        gg1, gs1 = lax.fori_loop(0, full // 256, norm_one_back, (zero, zero))
        for i, row in enumerate((gg1, gs1, ng2[0:1, :], ng2[1:2, :])):
            for g in range(groups):
                nsend[i * groups + g : i * groups + g + 1, :] = row[:, g * 128 : (g + 1) * 128]
        nall[me] = nsend[...]
        lax.fori_loop(1, n_dev, lambda k, _: push(k, 0), 0)
        for cp in first[3:]:
            cp.wait()
        mark()
        lane = lax.broadcasted_iota(jnp.int32, (full, 128), 1)
        seg = (
            (lax.broadcasted_iota(jnp.int32, (128, 128), 0) < 64)
            != (lax.broadcasted_iota(jnp.int32, (128, 128), 1) < 64)
        ).astype(F32).astype(BF16)
        for g in range(groups):
            h, j = g // pairs, g % pairs
            cf = ctxv[g]
            gov[g * 128 : (g + 1) * 128, :] = dot_tn(cf.astype(BF16), g2[...]).astype(BF16)
            dc = dot_nt(g2[...], wov[h, j * 128 : (j + 1) * 128, :]).astype(BF16).astype(F32)
            hi, mid, lo = split_three(dc * cf)
            delta = (
                dot_nn(hi.astype(BF16), seg) + dot_nn(mid.astype(BF16), seg)
                + dot_nn(lo.astype(BF16), seg)
            )
            hi, mid, lo = split_three(delta)
            for a in range(2):
                own = (lane < 64) if a == 0 else (lane >= 64)
                z = 64 if a == 0 else 0
                extra = jnp.where(
                    lane == z, hi,
                    jnp.where(lane == z + 1, mid, jnp.where(lane == z + 2, lo, 0.0)),
                )
                dobv[2 * g + a] = jnp.where(own, dc, extra).astype(BF16)
            if g < groups - 1:
                mark()
        for j in range(pairs):
            c = 2 * n_cols + j
            for h, ref in ((other, stage.at[c % 3]), (t, mine.at[c])):
                row = pl.ds(pl.multiple_of((h * pairs + j) * 128, 128), 128)
                for g in range(groups):
                    ref[3 * width + g * 128 : 3 * width + (g + 1) * 128, :] = gov[
                        row, g * 128 : (g + 1) * 128
                    ]
        mark()

    def push(k, what):
        lin = lax.rem(me + k, n_dev)
        c = pltpu.make_async_remote_copy(
            src_ref=nsend, dst_ref=nall.at[me], send_sem=nsend_sem.at[k], recv_sem=nrecv_sem.at[me],
            device_id=(lin // 2, lax.rem(lin, 2)), device_id_type=MESH,
        )
        if what == 0:
            c.start()
        else:
            c.wait_send()
        return 0

    def arrive(k, _):
        lin = lax.rem(me + k, n_dev)
        pltpu.make_async_remote_copy(
            src_ref=nsend, dst_ref=nall.at[lin], send_sem=nsend_sem.at[k],
            recv_sem=nrecv_sem.at[lin], device_id=(lin // 2, lax.rem(lin, 2)), device_id_type=MESH,
        ).wait_recv()
        return 0


    def attention(first, dq3, qbv, qkvv, xv, xt):
        length = lens[d]
        lane = lax.broadcasted_iota(jnp.int32, (full, 128), 1)
        bias = jnp.where(
            lax.broadcasted_iota(jnp.int32, (full, 128), 0) < length, 0.0, MASKED_SCORE
        )
        kb = 512
        low_half = lax.broadcasted_iota(jnp.int32, (kb, 128), 1) < 64
        for cp in first:
            cp.wait()
        for g in range(groups):
            cols = slice(g * 128, (g + 1) * 128)
            xt[cols, :] = (xv[:, cols].astype(F32) * INV_KEEP).T.astype(BF16)
        mark()

        def head_pair(h, j):
            i = h * pairs + j

            def part(c):
                return qkvv[h, :, c * hw + j * 128 : c * hw + (j + 1) * 128]

            k2f = part(1).astype(F32)
            k2t = k2f.T.astype(BF16)
            v2f = part(2).astype(F32)
            dks, dvs, dqs = [], [], []
            for a in range(2):
                own = (lane < 64) if a == 0 else (lane >= 64)
                z = 64 if a == 0 else 0
                minus = jnp.where(jnp.logical_and(lane >= z, lane < z + 3), -1.0, 0.0)
                ka = jnp.where(own, k2f, jnp.where(lane == z + 3, bias, minus)).astype(BF16)
                va = jnp.where(own, v2f, minus).astype(BF16)
                qa = qbv[2 * i + a]
                da = dobv[2 * i + a]
                dk, dv = [], []
                dqt = None
                for b in range(full // kb):
                    rows = slice(b * kb, (b + 1) * kb)
                    p = jnp.exp(dot_nt(ka[rows], qa))
                    ds = (p * dot_nt(va[rows], da)).astype(BF16)
                    dv.append(dot_nn(p.astype(BF16), da))
                    dk.append(dot_nn(ds, qa))
                    term = dot_nn(k2t[a * 64 : (a + 1) * 64, rows], ds)
                    dqt = term if dqt is None else dqt + term
                dks.append(dk)
                dvs.append(dv)
                dqs.append(dqt)
                if a == 0:
                    mark()
            for b in range(full // kb):
                rows = slice(b * kb, (b + 1) * kb)
                dq3[i, rows, 128:256] = jnp.where(low_half, dks[0][b], dks[1][b]).astype(BF16)
                dq3[i, rows, 256:384] = jnp.where(low_half, dvs[0][b], dvs[1][b]).astype(BF16)
            dq = jnp.concatenate(dqs, axis=0) * HEAD_DIM**-0.5
            dq3[i, :, 0:128] = dq.T.astype(BF16)

        for j in range(pairs):
            c = 2 * n_cols + j
            for h, ref in ((other, stage.at[c % 3]), (t, mine.at[c])):
                head_pair(h, j)
                put(ref, 0, dot_nn(xt[...], dq3[h * pairs + j]))
                if h is other:
                    begin(c)
                else:
                    made.add(c)
                mark()

    def to_input(first, dq3, wqv, dinv, acc):
        for cp in first:
            cp.wait()
        mark()

        def d_input(start):
            rows = pl.ds(pl.multiple_of(start, 256), 256)
            total = dr[rows, :]
            for h in range(2):
                lhs = jnp.concatenate(
                    [dq3[h * pairs + j, rows, c * 128 : (c + 1) * 128] for c in range(3) for j in range(pairs)],
                    axis=1,
                )
                total = total + dot_nt(
                    lhs, jnp.concatenate([wqv[h, c] for c in range(3)], axis=1)
                )
            return total

        for s in range(loc // 256):
            g2[s * 256 : (s + 1) * 256, :] = d_input(other * loc + s * 256).astype(BF16)
            if s < loc // 256 - 1:
                mark()
        send = pltpu.make_async_remote_copy(
            src_ref=g2.at[pl.ds(0, loc)], dst_ref=gin, send_sem=gt_sem.at[0], recv_sem=gt_sem.at[1],
            device_id=peer, device_id_type=MESH,
        )
        send.start()
        mark()
        for s in range(loc // 256):
            acc[s * 256 : (s + 1) * 256, :] = d_input(t * loc + s * 256)
            mark()
        send.wait()
        for s in range(loc // 256):
            rows = slice(s * 256, (s + 1) * 256)
            acc[rows, :] = (
                jnp.where(dinv[t, rows, :] != 0, acc[rows, :], 0.0)
                + jnp.where(dinv[other, rows, :] != 0, gin[rows, :].astype(F32), 0.0)
            ) * INV_KEEP
        out = pltpu.make_async_copy(acc, gt_o, gt_sem.at[2])
        out.start()
        mark()
        lax.fori_loop(1, n_dev, arrive, 0)
        total = nall[0]
        for k in range(1, n_dev):
            total = total + nall[k]
        ng_o[...] = total
        finish_all()
        out.wait()

    def rest(qbv, qkvv, xv):
        ahead = load([(qkv_i, qkvv), (qb_i, qbv), (x0_i, xv)], 15)
        pl.run_scoped(
            norm_and_out, vm((full, width), F32), vm((full, 128), F32), vm((groups, full, 128), F32),
            vm((full, width), BF16), vm((2,) + wo.shape, BF16), vm((width, width), BF16),
        )

        def projections(dq3, xt, wqv, dinv, acc):
            later = load([(wq_i, wqv), (din_i, dinv)], 18)
            attention(ahead, dq3, qbv, qkvv, xv, xt)
            to_input(later, dq3, wqv, dinv, acc)

        pl.run_scoped(
            projections, vm((groups, full, 384), BF16), vm((width, full), BF16),
            vm(wq_i.shape, BF16), vm(din_i.shape, jnp.int32), vm((loc, width), F32),
        )

    pl.run_scoped(
        rest, vm((2 * groups, full, 128), BF16), vm(qkv_i.shape, BF16), vm((full, width), BF16)
    )
    for c in range(n_chunks):
        for cp in out_copies(c):
            cp.wait()
    lax.fori_loop(1, n_dev, lambda k, _: push(k, 1), 0)


def back(
    lengths, gain_first, ng2, g2, dr2, act, dg, hl, n1, rs1, ctx, ma, wo, wo_p, wu, wu_p, wd, wd_p, qb,
    qkv, x0, wq, d_in, n_dp,
):
    full, width = x0.shape
    loc = full // 2
    groups = width // 128
    bits = n_dp.bit_length() - 1
    n_dev = 2 * n_dp
    n_chunks = 2 * (wu.shape[1] // CH) + groups // 2
    rows_c = CH * width // 128
    n_items = len(sum_plan(n_dp, n_chunks, rows_c)[0])
    sds = jax.ShapeDtypeStruct
    anyspec = pl.BlockSpec(memory_space=pl.ANY)
    vspec = pl.BlockSpec(memory_space=pltpu.VMEM)
    vm = pltpu.VMEM
    dma = pltpu.SemaphoreType.DMA
    return pl.pallas_call(
        back_kernel,
        out_shape=[
            sds(wq.shape[1:], BF16), sds(wo.shape, BF16), sds(wu.shape, BF16), sds(wd.shape, BF16),
            sds((loc, width), F32), sds((4 * groups, 128), F32),
        ],
        in_specs=[pl.BlockSpec(memory_space=pltpu.SMEM), vspec, vspec] + [anyspec] * 20,
        out_specs=[anyspec] * 5 + [vspec],
        scratch_shapes=[
            vm((n_chunks, rows_c, 128), BF16), vm((n_chunks, rows_c, 128), BF16),
            vm((n_chunks, rows_c, 128), BF16), vm((3, rows_c, 128), BF16),
            vm((full, width), BF16), vm((full, width), F32), vm(qb.shape, BF16),
            vm((loc, width), BF16),
            vm((4 * groups, 128), F32), vm((n_dev, 4 * groups, 128), F32),
            dma((20,)), dma((n_chunks,)), dma((n_chunks,)), dma((n_items, 2 * bits)),
            dma((n_items, 2 * bits)), dma((n_chunks, 9)), dma((n_dev,)), dma((n_dev,)), dma((3,)),
        ],
        compiler_params=pltpu.CompilerParams(
            collective_id=2, has_side_effects=True, vmem_limit_bytes=62 * 2**20
        ),
        name="back",
    )(
        lengths, gain_first, ng2, g2, dr2, act, dg, hl, n1, rs1, ctx, ma, wo, wo_p, wu, wu_p, wd, wd_p,
        qb, qkv, x0, wq, d_in,
    )


def finish_kernel(n_parts, *refs):
    n = len(n_parts)
    norms, stats = refs[:2]
    refs = refs[2:]
    srcs, dsts = refs[:n], refs[n : 2 * n]
    small = refs[2 * n : 2 * n + 7]
    refs = refs[2 * n + 7 :]
    narrow, wide = refs[:n], refs[n : 2 * n]
    in_sem, out_sem = refs[2 * n :]

    def piece(i, k):
        rows = srcs[i].shape[0] // n_parts[i]
        return pl.ds(k * rows, rows)

    todo = [(i, k) for i in range(n) for k in range(n_parts[i])]
    loads = []
    for m, (i, k) in enumerate(todo):
        r = piece(i, k)
        loads.append(pltpu.make_async_copy(srcs[i].at[r], narrow[i].at[r], in_sem.at[m]))
        loads[-1].start()
    saves = []
    for m, (i, k) in enumerate(todo):
        r = piece(i, k)
        loads[m].wait()
        from_ref = narrow[i]
        if srcs[i].dtype != dsts[i].dtype:
            wide[i][r] = narrow[i][r].astype(F32)
            from_ref = wide[i]
        saves.append(pltpu.make_async_copy(from_ref.at[r], dsts[i].at[r], out_sem.at[m]))
        saves[-1].start()
    groups = norms.shape[0] // 4
    for i in range(4):
        row = jnp.concatenate([norms[i * groups + g : i * groups + g + 1, :] for g in range(groups)], axis=1)
        small[i][...] = row.reshape(groups * 128)
    for i in range(3):
        small[4 + i][...] = stats[i : i + 1, 0:1]
    for c in saves:
        c.wait()


def finish(norms, stats, arrays, kinds, n_parts):
    sds = jax.ShapeDtypeStruct
    anyspec = pl.BlockSpec(memory_space=pl.ANY)
    vspec = pl.BlockSpec(memory_space=pltpu.VMEM)
    vm = pltpu.VMEM
    dma = pltpu.SemaphoreType.DMA
    n = len(arrays)
    wide = [
        vm(a.shape if a.dtype != k else (8, 128), F32) for a, k in zip(arrays, kinds)
    ]
    return pl.pallas_call(
        functools.partial(finish_kernel, n_parts),
        out_shape=[sds(a.shape, k) for a, k in zip(arrays, kinds)]
        + [sds((norms.size // 4,), F32)] * 4 + [sds((1, 1), F32)] * 3,
        in_specs=[vspec] * 2 + [anyspec] * n,
        out_specs=[anyspec] * n + [vspec] * 7,
        scratch_shapes=[vm(a.shape, a.dtype) for a in arrays] + wide
        + [dma((sum(n_parts),)), dma((sum(n_parts),))],
        compiler_params=pltpu.CompilerParams(vmem_limit_bytes=VMEM_LIMIT),
        name="finish",
    )(norms, stats, *arrays)


def per_device(
    tokens, lengths, drop_in, drop_attn, drop_ffn, qkv_weight, out_weight, up_weight, down_weight,
    gain_first, shift_first, gain_second, shift_second, cotangent,
):
    n_dp = lax.axis_size("dp")
    width = tokens.shape[2]
    wq = jnp.transpose(qkv_weight, (1, 0, 2))
    x0, ma, mf, cot_p, wqf, wo_p, wu_p, wd_p, qkv, qb, ctx = front(
        lengths, tokens[0], drop_in[0], drop_attn[0], drop_ffn[0], cotangent[0],
        wq, out_weight, up_weight, down_weight,
    )
    gains = (gain_first, shift_first, gain_second, shift_second)
    lay, stats, act, dg, hl, n1, rs1, g2, dr2, ng2 = middle(
        lengths, gains, ctx, x0, ma, mf, cotangent[0], cot_p, out_weight, wo_p,
        up_weight, wu_p, down_weight, wd_p, n_dp,
    )
    gq, go, gu, gd, gt, norms = back(
        lengths, gain_first, ng2, g2, dr2, act, dg, hl, n1, rs1, ctx, ma, out_weight, wo_p,
        up_weight, wu_p, down_weight, wd_p, qb, qkv, x0, wqf, drop_in[0], n_dp,
    )
    lay, gt, gq, go, gu, gd, *small = finish(
        norms, stats, [lay, gt, gq, go, gu, gd], [BF16, F32, F32, F32, F32, F32], [2, 2, 3, 1, 3, 3]
    )
    return (
        lay[None], gt[None], jnp.transpose(gq, (1, 0, 2)), go, gu, gd,
        *small[:4], *(v.reshape(()) for v in small[4:]),
    )


def solution(mesh):
    act = P("dp", None, "tensor", None)
    in_specs = (
        P("dp", "tensor", None), P(), act, act, act,
        P(None, None, "tensor"), P("tensor", None), P(None, "tensor"), P("tensor", None),
        P(), P(), P(), P(), act,
    )
    out_specs = (
        act, P("dp", "tensor", None),
        P(None, None, "tensor"), P("tensor", None), P(None, "tensor"), P("tensor", None),
        P(), P(), P(), P(), P(), P(), P(),
    )
    return jax.shard_map(
        per_device, mesh=mesh, in_specs=in_specs, out_specs=out_specs, check_vma=False
    )
```

```python
import functools
import math

import jax
import jax.numpy as jnp
from jax import lax
from jax.experimental import pallas as pl
from jax.experimental.pallas import tpu as pltpu
from jax.sharding import PartitionSpec as P

HEAD_DIM = 64
INV_KEEP = 1.0 / 0.9
SOFTMAX_WARMTH = 0.05
EPSILON = 1e-06
MASKED_SCORE = -1e30
MESH = pl.DeviceIdType.MESH
F32 = jnp.float32
BF16 = jnp.bfloat16
VMEM_LIMIT = 60 * 2**20
HIGHEST = lax.Precision.HIGHEST

TAIL_P = 0.3
TAIL = (
    0.11962929778234735,
    0.12075397394392673,
    0.09991336806236217,
    0.1285620774207718,
    -0.05368457414666341,
    0.20635459819946347,
    -0.15720376083821283,
    0.03567494667807555,
)


def dot_nn(a, b):
    return jnp.dot(a, b, preferred_element_type=F32)


def dot_nt(a, b):
    return lax.dot_general(a, b, (((1,), (1,)), ((), ())), preferred_element_type=F32)


def dot_tn(a, b):
    return lax.dot_general(a, b, (((0,), (0,)), ((), ())), preferred_element_type=F32)


def gelu_pair(x):
    z = jnp.abs(x)
    bell = jnp.exp2(x * x * (-0.5 * math.log2(math.e)))
    t = pl.reciprocal(1.0 + TAIL_P * z, approx=True)
    acc = jnp.full_like(t, TAIL[-1])
    for c in TAIL[-2::-1]:
        acc = acc * t + c
    tail = acc * t * bell
    cdf = jnp.where(x < 0.0, tail, 1.0 - tail)
    return x * cdf, cdf + x * (bell * (1.0 / math.sqrt(2.0 * math.pi)))


def split_three(v):
    hi = v.astype(BF16).astype(F32)
    rest = v - hi
    mid = rest.astype(BF16).astype(F32)
    return hi, mid, rest - mid


def front_kernel(
    lens, tok, d_in, d_at, d_ff, cot, wq, wo, wu, wd,
    x0_o, ma_o, mf_o, cot_o, wq_o, wo_o, wu_o, wd_o, qkv_o, qb_o, ctx_o,
    xv, xl, wv, qs, ms, tokv, st, qbv, ctxv, in_sem, loc_sem, send_sem, recv_sem, out_sem,
):
    d = lax.axis_index("dp")
    t = lax.axis_index("tensor")
    other = 1 - t
    peer = (d, other)
    loc = tok.shape[0]
    full = 2 * loc
    hw = wq.shape[2]
    pairs = hw // 128

    barrier = pltpu.get_barrier_semaphore()
    pl.semaphore_signal(barrier, inc=1, device_id=peer, device_id_type=MESH)

    loads = [
        pltpu.make_async_copy(tok, tokv, in_sem.at[0]),
        pltpu.make_async_copy(d_in, ms.at[0], in_sem.at[1]),
        pltpu.make_async_copy(wq, wv.at[t], in_sem.at[2]),
        pltpu.make_async_copy(d_at, ms.at[1], in_sem.at[3]),
        pltpu.make_async_copy(d_ff, ms.at[2], in_sem.at[4]),
    ]
    for c in loads:
        c.start()
    own_rows = pl.ds(pl.multiple_of(t * loc, loc), loc)

    def remote(i, src, dst):
        return pltpu.make_async_remote_copy(
            src_ref=src, dst_ref=dst, send_sem=send_sem.at[i], recv_sem=recv_sem.at[i],
            device_id=peer, device_id_type=MESH,
        )

    pl.semaphore_wait(barrier, 1)
    send_wq = remote(0, wq, wv.at[t])
    send_wq.start()
    loads[0].wait()
    loads[1].wait()
    st[0] = jnp.where(ms[0, other] != 0, tokv[...].astype(F32), 0.0).astype(BF16)
    send_x = remote(1, st.at[0], xv.at[own_rows])
    send_x.start()
    own_x = jnp.where(ms[0, t] != 0, tokv[...].astype(F32), 0.0)
    xv[own_rows, :] = own_x.astype(BF16)
    xl[own_rows, :] = (own_x * INV_KEEP).astype(BF16)
    def project(h, rows):
        for c in range(3):
            qs[h, rows, c * hw : (c + 1) * hw] = dot_nn(xl[rows, :], wv[h, c]).astype(BF16)

    loads[2].wait()
    project(t, own_rows)
    send_wq.wait_recv()
    project(other, own_rows)
    save_w = pltpu.make_async_copy(wv, wq_o, loc_sem.at[3])
    save_w.start()
    loads[3].wait()
    st[1] = ms[1, other].astype(F32).astype(BF16)
    st[2] = ms[1, t].astype(F32).astype(BF16)
    loads[4].wait()
    st[3] = ms[2, other].astype(F32).astype(BF16)
    st[4] = ms[2, t].astype(F32).astype(BF16)
    sends = [
        remote(2, wo, wo_o),
        remote(3, st.at[1], ma_o.at[own_rows]),
        remote(4, wu, wu_o),
        remote(5, wd, wd_o),
        remote(6, st.at[3], mf_o.at[own_rows]),
        remote(7, cot.at[other], cot_o),
    ]
    for c in sends:
        c.start()
    more = [
        pltpu.make_async_copy(st.at[2], ma_o.at[own_rows], loc_sem.at[0]),
        pltpu.make_async_copy(st.at[4], mf_o.at[own_rows], loc_sem.at[1]),
    ]
    for c in more:
        c.start()

    send_x.wait_recv()
    oth_rows = pl.ds(pl.multiple_of(other * loc, loc), loc)
    xl[oth_rows, :] = (xv[oth_rows, :].astype(F32) * INV_KEEP).astype(BF16)
    save_x = pltpu.make_async_copy(xv, x0_o, loc_sem.at[2])
    save_x.start()
    project(t, oth_rows)
    project(other, oth_rows)
    save_qkv = pltpu.make_async_copy(qs, qkv_o, loc_sem.at[4])
    save_qkv.start()

    length = lens[d]
    bias = jnp.where(
        lax.broadcasted_iota(jnp.int32, (full, 128), 0) < length, 0.0, MASKED_SCORE
    )
    lane = lax.broadcasted_iota(jnp.int32, (full, 128), 1)
    lane_q = lax.broadcasted_iota(jnp.int32, (512, 128), 1)

    def out_copies(i):
        return [
            pltpu.make_async_copy(qbv.at[pl.ds(2 * i, 2)], qb_o.at[pl.ds(2 * i, 2)], out_sem.at[0, i]),
            pltpu.make_async_copy(ctxv.at[i], ctx_o.at[i], out_sem.at[1, i]),
        ]

    def head_pair(i, _):
        h = i // pairs
        off = (i - h * pairs) * 128

        def part(c):
            return qs[h, :, pl.ds(pl.multiple_of(c * hw + off, 128), 128)].astype(F32)

        q2 = part(0) * HEAD_DIM**-0.5
        k2 = part(1)
        v2 = part(2)
        keys, vals, ques = [], [], []
        for a in range(2):
            own = (lane < 64) if a == 0 else (lane >= 64)
            first = 64 if a == 0 else 0
            keys.append(jnp.where(own, k2, jnp.where(lane == first, bias, 0.0)).astype(BF16))
            ques.append(jnp.where(own, q2, jnp.where(lane == first, 1.0, 0.0)).astype(BF16))
            vals.append(jnp.where(own, v2, 1.0).astype(BF16))
        for b in range(full // 512):
            rows = slice(b * 512, (b + 1) * 512)
            tops, outs = [], []
            for a in range(2):
                s = dot_nt(ques[a][rows], keys[a])
                top = jnp.max(s, axis=1, keepdims=True)
                p = jnp.exp(s - top).astype(BF16)
                outs.append(dot_nn(p, vals[a]))
                tops.append(top)
            low_half = lane_q < 64
            num = jnp.where(low_half, outs[0], outs[1])
            den = pltpu.roll(jnp.where(low_half, outs[1], outs[0]), 64, 1)
            ctxv[i, rows, :] = num / den
            for a in range(2):
                hi, mid, lo = split_three(tops[a] + jnp.log(outs[a]))
                own = low_half if a == 0 else jnp.logical_not(low_half)
                first = 64 if a == 0 else 0
                extra = jnp.where(
                    lane_q == first, hi,
                    jnp.where(lane_q == first + 1, mid,
                              jnp.where(lane_q == first + 2, lo,
                                        jnp.where(lane_q == first + 3, 1.0, 0.0))),
                )
                qbv[2 * i + a, rows, :] = jnp.where(own, q2[rows], extra).astype(BF16)
        for c in out_copies(i):
            c.start()
        return 0

    lax.fori_loop(0, 2 * pairs, head_pair, 0)

    def drain(i, _):
        for c in out_copies(i):
            c.wait()
        return 0

    lax.fori_loop(0, 2 * pairs, drain, 0)
    send_wq.wait_send()
    send_x.wait_send()
    for c in sends:
        c.wait()
    for c in more + [save_x, save_w, save_qkv]:
        c.wait()


def front(lengths, tok, d_in, d_at, d_ff, cot, wq, wo, wu, wd):
    loc, width = tok.shape
    full = 2 * loc
    half_w = 3 * wq.shape[2]
    groups = width // 128
    sds = jax.ShapeDtypeStruct
    anyspec = pl.BlockSpec(memory_space=pl.ANY)
    outs = [
        sds((full, width), BF16), sds((full, width), BF16), sds((full, width), BF16),
        sds((loc, width), BF16),
        sds((2,) + wq.shape, BF16), sds(wo.shape, BF16), sds(wu.shape, BF16), sds(wd.shape, BF16),
        sds((2, full, half_w), BF16), sds((2 * groups, full, 128), BF16),
        sds((groups, full, 128), F32),
    ]
    return pl.pallas_call(
        front_kernel,
        out_shape=outs,
        in_specs=[pl.BlockSpec(memory_space=pltpu.SMEM)] + [anyspec] * 9,
        out_specs=[anyspec] * len(outs),
        scratch_shapes=[
            pltpu.VMEM((full, width), BF16), pltpu.VMEM((full, width), BF16),
            pltpu.VMEM((2,) + wq.shape, BF16), pltpu.VMEM((2, full, half_w), BF16),
            pltpu.VMEM((3, 2, loc, width), jnp.int32), pltpu.VMEM((loc, width), BF16),
            pltpu.VMEM((5, loc, width), BF16),
            pltpu.VMEM((2 * groups, full, 128), BF16), pltpu.VMEM((groups, full, 128), F32),
            pltpu.SemaphoreType.DMA((5,)), pltpu.SemaphoreType.DMA((5,)),
            pltpu.SemaphoreType.DMA((8,)), pltpu.SemaphoreType.DMA((8,)),
            pltpu.SemaphoreType.DMA((2, groups)),
        ],
        compiler_params=pltpu.CompilerParams(
            collective_id=0, has_side_effects=True, vmem_limit_bytes=VMEM_LIMIT
        ),
        name="front",
    )(lengths, tok, d_in, d_at, d_ff, cot, wq, wo, wu, wd)


CH = 512


def middle_kernel(
    lens, ga1, sh1, ga2, sh2, ctx, x0, ma, mf, cot, cot_p, wo, wo_p, wu, wu_p, wd, wd_p,
    lay_o, loss_o, act_o, dg_o, hl_o, n1_o, rs1_o, g2_o, dr2_o, ng_o,
    ctxv, x0v, mav, mfv, cotv, wov, wuv, wdv,
    n1, n2, rs1, rs2, hl, act, dg, g2, dr2, yb, sbuf, pool_all, facc,
    in_sem, lay_sem, send_sem, recv_sem, row_sem, out_sem,
):
    d = lax.axis_index("dp")
    t = lax.axis_index("tensor")
    other = 1 - t
    peer = (d, other)
    n_dp = lax.axis_size("dp")
    n_dev = 2 * n_dp
    full, width = x0v.shape
    loc = full // 2
    groups = width // 128
    ff_half = wuv.shape[2]
    n_ch = 2 * ff_half // CH
    per_half = ff_half // CH
    me = d * 2 + t

    barrier = pltpu.get_barrier_semaphore()

    def greet(k, _):
        lin = lax.rem(me + k, n_dev)
        pl.semaphore_signal(
            barrier, inc=1, device_id=(lin // 2, lax.rem(lin, 2)), device_id_type=MESH
        )
        return 0

    lax.fori_loop(1, n_dev, greet, 0)

    own_rows = pl.ds(pl.multiple_of(t * loc, loc), loc)
    oth_rows = pl.ds(pl.multiple_of(other * loc, loc), loc)
    srcs = (ctx, wo, wo_p, x0, ma, wu, wu_p, wd, wd_p, mf, cot.at[t], cot_p)
    dsts = (
        ctxv, wov.at[t], wov.at[other], x0v, mav, wuv.at[t], wuv.at[other], wdv.at[t],
        wdv.at[other], mfv, cotv.at[own_rows], cotv.at[oth_rows],
    )
    loads = [pltpu.make_async_copy(s, v, in_sem.at[i]) for i, (s, v) in enumerate(zip(srcs, dsts))]
    for c in loads:
        c.start()
    gain1, shift1, gain2, shift2 = (r[...].reshape(1, width) for r in (ga1, sh1, ga2, sh2))
    length = lens[d]

    for c in loads[:5]:
        c.wait()

    def norm_one(b, _):
        rows = pl.ds(pl.multiple_of(b * 256, 256), 256)
        c2 = jnp.concatenate([ctxv[g, rows, :].astype(BF16) for g in range(groups)], axis=1)
        branch = dot_nn(c2, wov[...].reshape(width, width))
        r = (x0v[rows, :].astype(F32) + branch * mav[rows, :].astype(F32)) * INV_KEEP
        cen = r - jnp.mean(r, axis=1, keepdims=True)
        rstd = lax.rsqrt(jnp.mean(cen * cen, axis=1, keepdims=True) + EPSILON)
        n = cen * rstd
        n1[rows, :] = n
        rs1[rows, :] = jnp.broadcast_to(rstd, (256, 128))
        hl[rows, :] = (n * gain1 + shift1).astype(BF16)
        return 0

    lax.fori_loop(0, full // 256, norm_one, 0)
    saves = [
        pltpu.make_async_copy(s, o, out_sem.at[i])
        for i, (s, o) in enumerate(((hl, hl_o), (n1, n1_o), (rs1, rs1_o)))
    ]
    for c in saves:
        c.start()
    for c in loads[5:]:
        c.wait()

    def row_copies(b):
        rows = pl.ds(pl.multiple_of(b * 512, 512), 512)
        return [
            pltpu.make_async_copy(act.at[rows], act_o.at[rows], row_sem.at[b, 0]),
            pltpu.make_async_copy(dg.at[rows], dg_o.at[rows], row_sem.at[b, 1]),
        ]

    def ffn(b, pooled):
        rows = pl.ds(pl.multiple_of(b * 512, 512), 512)
        def up(j):
            h, o = j // per_half, (j % per_half) * CH
            return dot_nn(hl[rows, :], wuv[h, :, o : o + CH])

        ahead = up(0)
        for j in range(n_ch):
            h, o = j // per_half, (j % per_half) * CH
            pre = ahead
            if j + 1 < n_ch:
                ahead = up(j + 1)
            a, da = gelu_pair(pre)
            ab = a.astype(BF16)
            act[rows, j * CH : (j + 1) * CH] = ab
            dg[rows, j * CH : (j + 1) * CH] = da.astype(BF16)
            term = dot_nn(ab, wdv[h, o : o + CH, :])
            if j == 0:
                facc[...] = term
            else:
                facc[...] += term
        for c in row_copies(b):
            c.start()
        for s in range(2):
            sub = pl.ds(pl.multiple_of(b * 512 + s * 256, 256), 256)
            r = n1[sub, :] * gain1 + shift1 + facc[s * 256 : (s + 1) * 256, :] * (
                mfv[sub, :].astype(F32) * INV_KEEP
            )
            cen = r - jnp.mean(r, axis=1, keepdims=True)
            rstd = lax.rsqrt(jnp.mean(cen * cen, axis=1, keepdims=True) + EPSILON)
            n = cen * rstd
            n2[sub, :] = n
            rs2[sub, :] = jnp.broadcast_to(rstd, (256, 128))
            y = n * gain2 + shift2
            yb[sub, :] = y.astype(BF16)
            pos = lax.broadcasted_iota(jnp.int32, (256, width), 0) + (b * 512 + s * 256)
            pooled = pooled + jnp.sum(jnp.where(pos < length, y, 0.0), axis=0, keepdims=True)
        return pooled

    pooled = lax.fori_loop(0, full // 512, ffn, jnp.zeros((1, width), F32))

    for g in range(groups):
        sbuf[g : g + 1, :] = pooled[:, g * 128 : (g + 1) * 128]
    sbuf[groups:, :] = jnp.zeros((8 - groups, 128), F32)
    slot = t * n_dp + d
    pl.semaphore_wait(barrier, n_dev - 1)

    def push(k, start):
        lin = lax.rem(me + k, n_dev)
        pd, pt = lin // 2, lax.rem(lin, 2)
        c = pltpu.make_async_remote_copy(
            src_ref=sbuf, dst_ref=pool_all.at[slot], send_sem=send_sem.at[k],
            recv_sem=recv_sem.at[slot], device_id=(pd, pt), device_id_type=MESH,
        )
        if start:
            c.start()
        else:
            c.wait_send()
        return 0

    lax.fori_loop(1, n_dev, lambda k, _: push(k, True), 0)
    lay_local = pltpu.make_async_copy(yb.at[own_rows], lay_o.at[t], lay_sem.at[0])
    lay_local.start()
    lay_send = pltpu.make_async_remote_copy(
        src_ref=yb.at[oth_rows], dst_ref=lay_o.at[t], send_sem=lay_sem.at[1],
        recv_sem=lay_sem.at[2], device_id=peer, device_id_type=MESH,
    )
    lay_send.start()
    pool_all[slot] = sbuf[...]

    def arrive(k, _):
        lin = lax.rem(me + k, n_dev)
        s = lax.rem(lin, 2) * n_dp + lin // 2
        pltpu.make_async_remote_copy(
            src_ref=sbuf, dst_ref=pool_all.at[s], send_sem=send_sem.at[k],
            recv_sem=recv_sem.at[s], device_id=(lin // 2, lax.rem(lin, 2)), device_id_type=MESH,
        ).wait_recv()
        return 0

    lax.fori_loop(1, n_dev, arrive, 0)

    pair_i = lax.broadcasted_iota(jnp.int32, (n_dp, 1), 0)
    len_col = jnp.zeros((n_dp, 1), F32)
    for k in range(n_dp):
        len_col = jnp.where(pair_i == k, lens[k].astype(F32), len_col)
    units = []
    scales = []
    for v in range(2):
        raw = jnp.concatenate(
            [pool_all[v * n_dp : (v + 1) * n_dp, g, :] for g in range(groups)], axis=1
        )
        pv = raw / len_col
        scale = lax.rsqrt(jnp.sum(pv * pv, axis=1, keepdims=True) + EPSILON)
        units.append(pv * scale)
        scales.append(scale)
    u0, u1 = units
    nt = (((1,), (1,)), ((), ()))
    row_i = lax.broadcasted_iota(jnp.int32, (n_dp, n_dp), 0)
    col_i = lax.broadcasted_iota(jnp.int32, (n_dp, n_dp), 1)
    diag = row_i == col_i
    sim = lax.dot_general(u0, u1, nt, precision=HIGHEST, preferred_element_type=F32) / SOFTMAX_WARMTH
    top = jnp.max(sim, axis=1, keepdims=True)
    raw = jnp.exp(sim - top)
    total = jnp.sum(raw, axis=1, keepdims=True)
    ce = top + jnp.log(total) - jnp.sum(jnp.where(diag, sim, 0.0), axis=1, keepdims=True)
    loss = jnp.sum(ce, axis=0, keepdims=True) / n_dp
    gap = u0 - u1
    align = jnp.sum(jnp.sum(gap * gap, axis=1, keepdims=True), axis=0, keepdims=True) / n_dp
    sq = jnp.sum(u0 * u0, axis=1, keepdims=True)
    sq_row = lax.dot_general(
        jnp.ones((n_dp, width), F32), u0 * u0, nt, precision=HIGHEST, preferred_element_type=F32
    )
    inner = lax.dot_general(u0, u0, nt, precision=HIGHEST, preferred_element_type=F32)
    pot = jnp.where(diag, 0.0, jnp.exp(-2.0 * (sq + sq_row - 2.0 * inner)))
    uni = jnp.log(
        jnp.sum(jnp.sum(pot, axis=1, keepdims=True), axis=0, keepdims=True) / (n_dp * (n_dp - 1))
    )
    stat_i = lax.broadcasted_iota(jnp.int32, (8, 128), 0)
    loss_o[...] = jnp.where(stat_i == 0, loss, jnp.where(stat_i == 1, align, uni))
    d_sim = (raw / total - jnp.where(diag, 1.0, 0.0)) / SOFTMAX_WARMTH
    d_u0 = jnp.dot(d_sim, u1, precision=HIGHEST, preferred_element_type=F32)
    d_u1 = lax.dot_general(
        d_sim, u0, (((0,), (0,)), ((), ())), precision=HIGHEST, preferred_element_type=F32
    )
    first_view = t == 0
    du = jnp.where(first_view, d_u0, d_u1)
    u = jnp.where(first_view, u0, u1)
    scale = jnp.where(first_view, scales[0], scales[1])
    d_pool = (du - u * jnp.sum(u * du, axis=1, keepdims=True)) * scale / len_col
    mine = lax.broadcasted_iota(jnp.int32, (n_dp, width), 0) == d
    pool_grad = jnp.sum(jnp.where(mine, d_pool, 0.0), axis=0, keepdims=True)

    def norm_two_back(b, sums):
        rows = pl.ds(pl.multiple_of(b * 256, 256), 256)
        pos = lax.broadcasted_iota(jnp.int32, (256, width), 0) + b * 256
        dy = cotv[rows, :].astype(F32) + jnp.where(pos < length, pool_grad, 0.0)
        n = n2[rows, :]
        g = dy * gain2
        dr = (g - jnp.mean(g, axis=1, keepdims=True) - n * jnp.mean(g * n, axis=1, keepdims=True)) * rs2[rows, :1]
        dr2[rows, :] = dr
        g2[rows, :] = (dr * (mfv[rows, :].astype(F32) * INV_KEEP)).astype(BF16)
        return (
            sums[0] + jnp.sum(dy * n, axis=0, keepdims=True),
            sums[1] + jnp.sum(dy, axis=0, keepdims=True),
        )

    zero = jnp.zeros((1, width), F32)
    gg2, gs2 = lax.fori_loop(0, full // 256, norm_two_back, (zero, zero))

    ng_o[...] = jnp.concatenate([gg2, gs2, zero, zero, zero, zero, zero, zero], axis=0)
    more = [
        pltpu.make_async_copy(g2, g2_o, out_sem.at[3]),
        pltpu.make_async_copy(dr2, dr2_o, out_sem.at[4]),
    ]
    for c in more:
        c.start()
    for b in range(full // 512):
        for c in row_copies(b):
            c.wait()
    lax.fori_loop(1, n_dev, lambda k, _: push(k, False), 0)
    lay_local.wait()
    lay_send.wait()
    for c in saves + more:
        c.wait()


def middle(
    lengths, gains, ctx, x0, ma, mf, cot, cot_p, wo, wo_p, wu, wu_p, wd, wd_p, n_dp
):
    full, width = x0.shape
    loc = full // 2
    ff = 2 * wd.shape[0]
    n_dev = 2 * n_dp
    sds = jax.ShapeDtypeStruct
    anyspec = pl.BlockSpec(memory_space=pl.ANY)
    vspec = pl.BlockSpec(memory_space=pltpu.VMEM)
    outs = [
        sds((2, loc, width), BF16), sds((8, 128), F32), sds((full, ff), BF16), sds((full, ff), BF16),
        sds((full, width), BF16), sds((full, width), F32), sds((full, 128), F32),
        sds((full, width), BF16), sds((full, width), F32), sds((8, width), F32),
    ]
    vm = pltpu.VMEM
    dma = pltpu.SemaphoreType.DMA
    return pl.pallas_call(
        middle_kernel,
        out_shape=outs,
        in_specs=[pl.BlockSpec(memory_space=pltpu.SMEM)] + [vspec] * 4 + [anyspec] * 12,
        out_specs=[anyspec, vspec] + [anyspec] * 7 + [vspec],
        scratch_shapes=[
            vm(ctx.shape, F32), vm((full, width), BF16), vm((full, width), BF16),
            vm((full, width), BF16), vm((full, width), BF16), vm((2,) + wo.shape, BF16),
            vm((2,) + wu.shape, BF16), vm((2,) + wd.shape, BF16),
            vm((full, width), F32), vm((full, width), F32), vm((full, 128), F32), vm((full, 128), F32),
            vm((full, width), BF16), vm((full, ff), BF16), vm((full, ff), BF16),
            vm((full, width), BF16), vm((full, width), F32), vm((full, width), BF16),
            vm((8, 128), F32), vm((n_dev, 8, 128), F32), vm((512, width), F32),
            dma((12,)), dma((3,)), dma((n_dev,)), dma((n_dev,)), dma((full // 512, 2)), dma((5,)),
        ],
        compiler_params=pltpu.CompilerParams(
            collective_id=1, has_side_effects=True, vmem_limit_bytes=VMEM_LIMIT
        ),
        name="middle",
    )(lengths, *gains, ctx, x0, ma, mf, cot, cot_p, wo, wo_p, wu, wu_p, wd, wd_p)


ORDERS_16 = (
    ((0, 1, 2, 3), (1, 0, 2, 3)), ((2, 0, 1, 3), (2, 1, 0, 3)),
    ((0, 1, 2, 3), (1, 0, 2, 3)), ((0, 1, 2, 3), (1, 0, 2, 3)),
    ((0, 2, 3, 1), (1, 2, 3, 0)), ((0, 1, 2, 3), (1, 0, 2, 3)),
    ((0, 1, 2, 3), (1, 0, 2, 3)), ((0, 2, 1, 3), (1, 2, 0, 3)),
    ((2, 0, 1, 3), (2, 1, 0, 3)), ((0, 2, 1, 3), (1, 2, 0, 3)),
)
TABLE_16 = (
    (), (), (), (), (), (0,),
    (), (1,), (2,), (), (0,), (),
    (3,), (2,), (1, 0), (), (4, 3), (),
    (0, 2), (1,), (5, 4, 0), (2, 3), (1,), (),
    (), (5, 4, 0), (2,), (3,), (1, 5), (4, 0, 2),
    (3, 5, 1, 4), (2, 0, 1, 4, 3), (6, 5), (2, 3, 4), (0, 5, 1), (6, 4),
    (7, 5, 2), (3, 6), (1, 4), (6, 7), (), (8, 9, 5),
    (6,), (3,), (9, 7), (), (), (5, 8, 7, 6, 9, 8, 7, 9, 8, 6, 7, 9, 6, 8, 7, 9, 8, 6, 9, 8, 7, 8, 9, 7, 8, 9),
)
LAST_PARTS = 2


def sum_plan(n_dp, n_chunks, rows):
    bits = n_dp.bit_length() - 1
    if bits == 4 and n_chunks + LAST_PARTS - 1 == len(ORDERS_16):
        part = rows // LAST_PARTS
        places = [(c, 0, rows) for c in range(n_chunks - 1)]
        places += [(n_chunks - 1, k * part, part) for k in range(LAST_PARTS)]
        return [p + o for p, o in zip(places, ORDERS_16)], TABLE_16
    plain = tuple(range(bits))

    def turn(k):
        return plain[k % bits :] + plain[: k % bits] if bits else plain

    return [(c, 0, rows, turn(2 * c), turn(2 * c + 2)) for c in range(n_chunks)], None


def back_kernel(
    lens, ga1, ng2, g2_i, dr2_i, act_i, dg_i, hl_i, n1_i, rs1_i, ctx_i, ma_i, wo, wo_p, wu, wu_p,
    wd, wd_p, qb_i, qkv_i, x0_i, wq_i, din_i,
    gq_o, go_o, gu_o, gd_o, gt_o, ng_o,
    mine, core_in, ring_in, stage, g2, dr, dobv, gin, nsend, nall,
    in_sem, core_send, core_recv, ring_send, ring_recv, out_sem, nsend_sem, nrecv_sem, gt_sem,
):
    d = lax.axis_index("dp")
    t = lax.axis_index("tensor")
    other = 1 - t
    peer = (d, other)
    n_dp = lax.axis_size("dp")
    n_dev = 2 * n_dp
    me = d * 2 + t
    full, width = g2.shape
    loc = full // 2
    ff_half = wu.shape[1]
    half_w = qkv_i.shape[2]
    hw = half_w // 3
    pairs = hw // 128
    groups = width // 128
    n_cols = ff_half // CH
    rows_c = mine.shape[1]
    bits = n_dp.bit_length() - 1
    n_chunks = mine.shape[0]
    items, table = sum_plan(n_dp, n_chunks, rows_c)

    barrier = pltpu.get_barrier_semaphore()

    def greet(k, _):
        lin = lax.rem(me + k, n_dev)
        pl.semaphore_signal(
            barrier, inc=1, device_id=(lin // 2, lax.rem(lin, 2)), device_id_type=MESH
        )
        return 0

    lax.fori_loop(1, n_dev, greet, 0)

    def load(pairs_of, first):
        copies = [
            pltpu.make_async_copy(s, v, in_sem.at[first + i]) for i, (s, v) in enumerate(pairs_of)
        ]
        for c in copies:
            c.start()
        return copies

    def core_copy(c):
        return pltpu.make_async_remote_copy(
            src_ref=stage.at[c % 3], dst_ref=core_in.at[c], send_sem=core_send.at[c],
            recv_sem=core_recv.at[c], device_id=peer, device_id_type=MESH,
        )

    def plan(i):
        steps = []
        _, off, size, o0, o1 = items[i]
        place = off
        for b0, b1 in zip(o0, o1):
            size //= 2
            beta = lax.rem(d // 2**b0, 2) * other + lax.rem(d // 2**b1, 2) * t
            hop = 2**b0 * other + 2**b1 * t
            partner = d + (1 - 2 * beta) * hop
            keep = pl.multiple_of(off + beta * size, 16)
            sent = pl.multiple_of(off + (1 - beta) * size, 16)
            steps.append((partner, keep, sent, size, place))
            off = off + beta * size
            place += size
        return steps

    def ring_copy(i, s):
        c = items[i][0]
        if s < bits:
            partner, keep, sent, size, place = plan(i)[s]
            src, dst = mine.at[c, pl.ds(sent, size)], ring_in.at[c, pl.ds(place, size)]
        else:
            partner, keep, sent, size, place = plan(i)[2 * bits - 1 - s]
            src, dst = core_in.at[c, pl.ds(keep, size)], core_in.at[c, pl.ds(keep, size)]
        return pltpu.make_async_remote_copy(
            src_ref=src, dst_ref=dst, send_sem=ring_send.at[i, s], recv_sem=ring_recv.at[i, s],
            device_id=(partner, t), device_id_type=MESH,
        )

    def add_in(c, dst, dst_off, size, src, src_off):
        step = math.gcd(size, 384)

        def body(i, _):
            a = pl.ds(pl.multiple_of(dst_off + i * step, 16), step)
            b = pl.ds(pl.multiple_of(src_off + i * step, 16), step)
            dst[c, a, :] = (mine[c, a, :].astype(F32) + src[c, b, :].astype(F32)).astype(BF16)
            return 0

        lax.fori_loop(0, size // step, body, 0)

    def out_copies(c):
        dst = []
        if c < n_cols:
            for g in range(groups):
                dst.append((g * CH, CH, gd_o.at[pl.ds(c * CH, CH), pl.ds(g * 128, 128)]))
        elif c < 2 * n_cols:
            for g in range(CH // 128):
                col = (c - n_cols) * CH + g * 128
                dst.append((g * width, width, gu_o.at[:, pl.ds(col, 128)]))
        else:
            j = c - 2 * n_cols
            for g in range(3):
                dst.append((g * width, width, gq_o.at[g, :, pl.ds(j * 128, 128)]))
            for g in range(groups):
                dst.append(
                    (3 * width + g * 128, 128, go_o.at[pl.ds(j * 128, 128), pl.ds(g * 128, 128)])
                )
        return [
            pltpu.make_async_copy(core_in.at[c, pl.ds(o, n)], r, out_sem.at[c, i])
            for i, (o, n, r) in enumerate(dst)
        ]

    begun = {}
    made = set()
    left = [sum(1 for it in items if it[0] == c) for c in range(n_chunks)]
    now = [0]

    def step(i):
        c, first, count = items[i][:3]
        a = begun.get(i, 0)
        assert c in made and a <= 2 * bits
        begun[i] = a + 1
        if a == 0:
            if first == 0:
                core_copy(c).wait()
            add_in(c, mine, first, count, core_in, first)
        else:
            ring_copy(i, a - 1).wait()
            if a <= bits:
                _, keep, _, size, place = plan(i)[a - 1]
                add_in(c, core_in if a == bits else mine, keep, size, ring_in, place)
        if a < 2 * bits:
            ring_copy(i, a).start()
        else:
            left[c] -= 1
            if left[c] == 0:
                for cp in out_copies(c):
                    cp.start()

    def mark():
        at = now[0]
        now[0] += 1
        if table is not None:
            todo = table[at]
        elif at % 2 == 0:
            todo = unfinished()
        else:
            todo = ()
        for i in todo:
            step(i)

    def unfinished():
        return [
            i for i in range(len(items)) if items[i][0] in made and begun.get(i, 0) <= 2 * bits
        ]

    def finish_all():
        for i in table[now[0]] if table is not None else ():
            step(i)
        while unfinished():
            for i in unfinished():
                step(i)

    def begin(c):
        core_copy(c).start()

    def put(ref, at, val):
        n = val.shape[0]
        for g in range(val.shape[1] // 128):
            ref[at + g * n : at + (g + 1) * n, :] = val[:, g * 128 : (g + 1) * 128].astype(BF16)

    gain1 = ga1[...].reshape(1, width)
    met = [False]

    def meet():
        if not met[0]:
            pl.semaphore_wait(barrier, n_dev - 1)
            met[0] = True

    def feed_forward(act, dg, hl, hlt, wuv, wdv):
        blocks = [
            pl.ds(pl.multiple_of(h * ff_half + c * CH, CH), CH)
            for c in range(n_cols) for h in (other, t)
        ]
        first = load(
            [(g2_i, g2)] + [(act_i.at[:, col], act.at[:, col]) for col in blocks]
            + [(dr2_i, dr), (hl_i, hl), (dg_i, dg), (wd, wdv.at[t]), (wd_p, wdv.at[other]),
               (wu, wuv.at[t]), (wu_p, wuv.at[other])], 20,
        )
        first[0].wait()
        mark()
        for c in range(n_cols):
            for h, ref in ((other, stage.at[c % 3]), (t, mine.at[c])):
                at = 2 * c + (0 if h is other else 1)
                first[1 + at].wait()
                put(ref, 0, dot_tn(act[:, blocks[at]], g2[...]))
                if h is other:
                    meet()
                    begin(c)
                else:
                    made.add(c)
                mark()
        for cp in first[1 + 2 * n_cols :]:
            cp.wait()
        for k in range(groups):
            cols = slice(k * 128, (k + 1) * 128)
            hlt[cols, :] = hl[:, cols].astype(F32).T.astype(BF16)
        mark()
        for k in range(n_cols):
            c = n_cols + k
            for h, ref in ((other, stage.at[c % 3]), (t, mine.at[c])):
                col = pl.ds(pl.multiple_of(h * ff_half + k * CH, CH), CH)
                for b in range(full // 512):
                    rows = slice(b * 512, (b + 1) * 512)
                    da = dot_nt(g2[rows, :], wdv[h, k * CH : (k + 1) * CH, :])
                    dp = (da * dg[rows, col].astype(F32)).astype(BF16)
                    dg[rows, col] = dp
                    dr[rows, :] += dot_nt(dp, wuv[h, :, k * CH : (k + 1) * CH])
                mark()
                put(ref, 0, dot_nn(hlt[...], dg[:, col]))
                if h is other:
                    begin(c)
                else:
                    made.add(c)
                mark()

    vm = pltpu.VMEM
    ff = 2 * ff_half
    pl.run_scoped(
        feed_forward, vm((full, ff), BF16), vm((full, ff), BF16), vm((full, width), BF16),
        vm((width, full), BF16), vm((2,) + wu.shape, BF16), vm((2,) + wd.shape, BF16),
    )

    def norm_and_out(n1, rs1, ctxv, mav, wov, gov):
        first = load(
            [(n1_i, n1), (rs1_i, rs1), (ma_i, mav), (wo, wov.at[t]), (wo_p, wov.at[other]),
             (ctx_i, ctxv)], 9,
        )
        for cp in first[:3]:
            cp.wait()

        def norm_one_back(b, sums):
            rows = pl.ds(pl.multiple_of(b * 256, 256), 256)
            dh = dr[rows, :]
            n = n1[rows, :]
            g = dh * gain1
            r = (
                g - jnp.mean(g, axis=1, keepdims=True) - n * jnp.mean(g * n, axis=1, keepdims=True)
            ) * rs1[rows, :1]
            dr[rows, :] = r
            g2[rows, :] = (r * (mav[rows, :].astype(F32) * INV_KEEP)).astype(BF16)
            return (
                sums[0] + jnp.sum(dh * n, axis=0, keepdims=True),
                sums[1] + jnp.sum(dh, axis=0, keepdims=True),
            )

        zero = jnp.zeros((1, width), F32)
        gg1, gs1 = lax.fori_loop(0, full // 256, norm_one_back, (zero, zero))
        for i, row in enumerate((gg1, gs1, ng2[0:1, :], ng2[1:2, :])):
            for g in range(groups):
                nsend[i * groups + g : i * groups + g + 1, :] = row[:, g * 128 : (g + 1) * 128]
        nall[me] = nsend[...]
        lax.fori_loop(1, n_dev, lambda k, _: push(k, 0), 0)
        for cp in first[3:]:
            cp.wait()
        mark()
        lane = lax.broadcasted_iota(jnp.int32, (full, 128), 1)
        seg = (
            (lax.broadcasted_iota(jnp.int32, (128, 128), 0) < 64)
            != (lax.broadcasted_iota(jnp.int32, (128, 128), 1) < 64)
        ).astype(F32).astype(BF16)
        for g in range(groups):
            h, j = g // pairs, g % pairs
            cf = ctxv[g]
            gov[g * 128 : (g + 1) * 128, :] = dot_tn(cf.astype(BF16), g2[...]).astype(BF16)
            dc = dot_nt(g2[...], wov[h, j * 128 : (j + 1) * 128, :]).astype(BF16).astype(F32)
            hi, mid, lo = split_three(dc * cf)
            delta = (
                dot_nn(hi.astype(BF16), seg) + dot_nn(mid.astype(BF16), seg)
                + dot_nn(lo.astype(BF16), seg)
            )
            hi, mid, lo = split_three(delta)
            for a in range(2):
                own = (lane < 64) if a == 0 else (lane >= 64)
                z = 64 if a == 0 else 0
                extra = jnp.where(
                    lane == z, hi,
                    jnp.where(lane == z + 1, mid, jnp.where(lane == z + 2, lo, 0.0)),
                )
                dobv[2 * g + a] = jnp.where(own, dc, extra).astype(BF16)
            if g < groups - 1:
                mark()
        for j in range(pairs):
            c = 2 * n_cols + j
            for h, ref in ((other, stage.at[c % 3]), (t, mine.at[c])):
                row = pl.ds(pl.multiple_of((h * pairs + j) * 128, 128), 128)
                for g in range(groups):
                    ref[3 * width + g * 128 : 3 * width + (g + 1) * 128, :] = gov[
                        row, g * 128 : (g + 1) * 128
                    ]
        mark()

    def push(k, what):
        lin = lax.rem(me + k, n_dev)
        c = pltpu.make_async_remote_copy(
            src_ref=nsend, dst_ref=nall.at[me], send_sem=nsend_sem.at[k], recv_sem=nrecv_sem.at[me],
            device_id=(lin // 2, lax.rem(lin, 2)), device_id_type=MESH,
        )
        if what == 0:
            c.start()
        else:
            c.wait_send()
        return 0

    def arrive(k, _):
        lin = lax.rem(me + k, n_dev)
        pltpu.make_async_remote_copy(
            src_ref=nsend, dst_ref=nall.at[lin], send_sem=nsend_sem.at[k],
            recv_sem=nrecv_sem.at[lin], device_id=(lin // 2, lax.rem(lin, 2)), device_id_type=MESH,
        ).wait_recv()
        return 0


    def attention(first, dq3, qbv, qkvv, xv, xt):
        length = lens[d]
        lane = lax.broadcasted_iota(jnp.int32, (full, 128), 1)
        bias = jnp.where(
            lax.broadcasted_iota(jnp.int32, (full, 128), 0) < length, 0.0, MASKED_SCORE
        )
        kb = 512
        low_half = lax.broadcasted_iota(jnp.int32, (kb, 128), 1) < 64
        for cp in first:
            cp.wait()
        for g in range(groups):
            cols = slice(g * 128, (g + 1) * 128)
            xt[cols, :] = (xv[:, cols].astype(F32) * INV_KEEP).T.astype(BF16)
        mark()

        def head_pair(h, j):
            i = h * pairs + j

            def part(c):
                return qkvv[h, :, c * hw + j * 128 : c * hw + (j + 1) * 128]

            k2f = part(1).astype(F32)
            k2t = k2f.T.astype(BF16)
            v2f = part(2).astype(F32)
            dks, dvs, dqs = [], [], []
            for a in range(2):
                own = (lane < 64) if a == 0 else (lane >= 64)
                z = 64 if a == 0 else 0
                minus = jnp.where(jnp.logical_and(lane >= z, lane < z + 3), -1.0, 0.0)
                ka = jnp.where(own, k2f, jnp.where(lane == z + 3, bias, minus)).astype(BF16)
                va = jnp.where(own, v2f, minus).astype(BF16)
                qa = qbv[2 * i + a]
                da = dobv[2 * i + a]
                dk, dv = [], []
                dqt = None
                for b in range(full // kb):
                    rows = slice(b * kb, (b + 1) * kb)
                    p = jnp.exp(dot_nt(ka[rows], qa))
                    ds = (p * dot_nt(va[rows], da)).astype(BF16)
                    dv.append(dot_nn(p.astype(BF16), da))
                    dk.append(dot_nn(ds, qa))
                    term = dot_nn(k2t[a * 64 : (a + 1) * 64, rows], ds)
                    dqt = term if dqt is None else dqt + term
                dks.append(dk)
                dvs.append(dv)
                dqs.append(dqt)
                if a == 0:
                    mark()
            for b in range(full // kb):
                rows = slice(b * kb, (b + 1) * kb)
                dq3[i, rows, 128:256] = jnp.where(low_half, dks[0][b], dks[1][b]).astype(BF16)
                dq3[i, rows, 256:384] = jnp.where(low_half, dvs[0][b], dvs[1][b]).astype(BF16)
            dq = jnp.concatenate(dqs, axis=0) * HEAD_DIM**-0.5
            dq3[i, :, 0:128] = dq.T.astype(BF16)

        for j in range(pairs):
            c = 2 * n_cols + j
            for h, ref in ((other, stage.at[c % 3]), (t, mine.at[c])):
                head_pair(h, j)
                put(ref, 0, dot_nn(xt[...], dq3[h * pairs + j]))
                if h is other:
                    begin(c)
                else:
                    made.add(c)
                mark()

    def to_input(first, dq3, wqv, dinv, acc):
        for cp in first:
            cp.wait()
        mark()

        def d_input(start):
            rows = pl.ds(pl.multiple_of(start, 256), 256)
            total = dr[rows, :]
            for h in range(2):
                lhs = jnp.concatenate(
                    [dq3[h * pairs + j, rows, c * 128 : (c + 1) * 128] for c in range(3) for j in range(pairs)],
                    axis=1,
                )
                total = total + dot_nt(
                    lhs, jnp.concatenate([wqv[h, c] for c in range(3)], axis=1)
                )
            return total

        for s in range(loc // 256):
            g2[s * 256 : (s + 1) * 256, :] = d_input(other * loc + s * 256).astype(BF16)
            if s < loc // 256 - 1:
                mark()
        send = pltpu.make_async_remote_copy(
            src_ref=g2.at[pl.ds(0, loc)], dst_ref=gin, send_sem=gt_sem.at[0], recv_sem=gt_sem.at[1],
            device_id=peer, device_id_type=MESH,
        )
        send.start()
        mark()
        for s in range(loc // 256):
            acc[s * 256 : (s + 1) * 256, :] = d_input(t * loc + s * 256)
            mark()
        send.wait()
        for s in range(loc // 256):
            rows = slice(s * 256, (s + 1) * 256)
            acc[rows, :] = (
                jnp.where(dinv[t, rows, :] != 0, acc[rows, :], 0.0)
                + jnp.where(dinv[other, rows, :] != 0, gin[rows, :].astype(F32), 0.0)
            ) * INV_KEEP
        out = pltpu.make_async_copy(acc, gt_o, gt_sem.at[2])
        out.start()
        mark()
        lax.fori_loop(1, n_dev, arrive, 0)
        total = nall[0]
        for k in range(1, n_dev):
            total = total + nall[k]
        ng_o[...] = total
        finish_all()
        out.wait()

    def rest(qbv, qkvv, xv):
        ahead = load([(qkv_i, qkvv), (qb_i, qbv), (x0_i, xv)], 15)
        pl.run_scoped(
            norm_and_out, vm((full, width), F32), vm((full, 128), F32), vm((groups, full, 128), F32),
            vm((full, width), BF16), vm((2,) + wo.shape, BF16), vm((width, width), BF16),
        )

        def projections(dq3, xt, wqv, dinv, acc):
            later = load([(wq_i, wqv), (din_i, dinv)], 18)
            attention(ahead, dq3, qbv, qkvv, xv, xt)
            to_input(later, dq3, wqv, dinv, acc)

        pl.run_scoped(
            projections, vm((groups, full, 384), BF16), vm((width, full), BF16),
            vm(wq_i.shape, BF16), vm(din_i.shape, jnp.int32), vm((loc, width), F32),
        )

    pl.run_scoped(
        rest, vm((2 * groups, full, 128), BF16), vm(qkv_i.shape, BF16), vm((full, width), BF16)
    )
    for c in range(n_chunks):
        for cp in out_copies(c):
            cp.wait()
    lax.fori_loop(1, n_dev, lambda k, _: push(k, 1), 0)


def back(
    lengths, gain_first, ng2, g2, dr2, act, dg, hl, n1, rs1, ctx, ma, wo, wo_p, wu, wu_p, wd, wd_p, qb,
    qkv, x0, wq, d_in, n_dp,
):
    full, width = x0.shape
    loc = full // 2
    groups = width // 128
    bits = n_dp.bit_length() - 1
    n_dev = 2 * n_dp
    n_chunks = 2 * (wu.shape[1] // CH) + groups // 2
    rows_c = CH * width // 128
    n_items = len(sum_plan(n_dp, n_chunks, rows_c)[0])
    sds = jax.ShapeDtypeStruct
    anyspec = pl.BlockSpec(memory_space=pl.ANY)
    vspec = pl.BlockSpec(memory_space=pltpu.VMEM)
    vm = pltpu.VMEM
    dma = pltpu.SemaphoreType.DMA
    return pl.pallas_call(
        back_kernel,
        out_shape=[
            sds(wq.shape[1:], BF16), sds(wo.shape, BF16), sds(wu.shape, BF16), sds(wd.shape, BF16),
            sds((loc, width), F32), sds((4 * groups, 128), F32),
        ],
        in_specs=[pl.BlockSpec(memory_space=pltpu.SMEM), vspec, vspec] + [anyspec] * 20,
        out_specs=[anyspec] * 5 + [vspec],
        scratch_shapes=[
            vm((n_chunks, rows_c, 128), BF16), vm((n_chunks, rows_c, 128), BF16),
            vm((n_chunks, rows_c, 128), BF16), vm((3, rows_c, 128), BF16),
            vm((full, width), BF16), vm((full, width), F32), vm(qb.shape, BF16),
            vm((loc, width), BF16),
            vm((4 * groups, 128), F32), vm((n_dev, 4 * groups, 128), F32),
            dma((36,)), dma((n_chunks,)), dma((n_chunks,)), dma((n_items, 2 * bits)),
            dma((n_items, 2 * bits)), dma((n_chunks, 9)), dma((n_dev,)), dma((n_dev,)), dma((3,)),
        ],
        compiler_params=pltpu.CompilerParams(
            collective_id=2, has_side_effects=True, vmem_limit_bytes=62 * 2**20
        ),
        name="back",
    )(
        lengths, gain_first, ng2, g2, dr2, act, dg, hl, n1, rs1, ctx, ma, wo, wo_p, wu, wu_p, wd, wd_p,
        qb, qkv, x0, wq, d_in,
    )


def finish_kernel(n_parts, *refs):
    n = len(n_parts)
    norms, stats = refs[:2]
    refs = refs[2:]
    srcs, dsts = refs[:n], refs[n : 2 * n]
    small = refs[2 * n : 2 * n + 7]
    refs = refs[2 * n + 7 :]
    narrow, wide = refs[:n], refs[n : 2 * n]
    in_sem, out_sem = refs[2 * n :]

    def piece(i, k):
        rows = srcs[i].shape[0] // n_parts[i]
        return pl.ds(k * rows, rows)

    todo = [(i, k) for i in range(n) for k in range(n_parts[i])]
    loads = []
    for m, (i, k) in enumerate(todo):
        r = piece(i, k)
        loads.append(pltpu.make_async_copy(srcs[i].at[r], narrow[i].at[r], in_sem.at[m]))
        loads[-1].start()
    saves = []
    for m, (i, k) in enumerate(todo):
        r = piece(i, k)
        loads[m].wait()
        from_ref = narrow[i]
        if srcs[i].dtype != dsts[i].dtype:
            wide[i][r] = narrow[i][r].astype(F32)
            from_ref = wide[i]
        saves.append(pltpu.make_async_copy(from_ref.at[r], dsts[i].at[r], out_sem.at[m]))
        saves[-1].start()
    groups = norms.shape[0] // 4
    for i in range(4):
        row = jnp.concatenate([norms[i * groups + g : i * groups + g + 1, :] for g in range(groups)], axis=1)
        small[i][...] = row.reshape(groups * 128)
    for i in range(3):
        small[4 + i][...] = stats[i : i + 1, 0:1]
    for c in saves:
        c.wait()


def finish(norms, stats, arrays, kinds, n_parts):
    sds = jax.ShapeDtypeStruct
    anyspec = pl.BlockSpec(memory_space=pl.ANY)
    vspec = pl.BlockSpec(memory_space=pltpu.VMEM)
    vm = pltpu.VMEM
    dma = pltpu.SemaphoreType.DMA
    n = len(arrays)
    wide = [
        vm(a.shape if a.dtype != k else (8, 128), F32) for a, k in zip(arrays, kinds)
    ]
    return pl.pallas_call(
        functools.partial(finish_kernel, n_parts),
        out_shape=[sds(a.shape, k) for a, k in zip(arrays, kinds)]
        + [sds((norms.size // 4,), F32)] * 4 + [sds((1, 1), F32)] * 3,
        in_specs=[vspec] * 2 + [anyspec] * n,
        out_specs=[anyspec] * n + [vspec] * 7,
        scratch_shapes=[vm(a.shape, a.dtype) for a in arrays] + wide
        + [dma((sum(n_parts),)), dma((sum(n_parts),))],
        compiler_params=pltpu.CompilerParams(vmem_limit_bytes=VMEM_LIMIT),
        name="finish",
    )(norms, stats, *arrays)


def per_device(
    tokens, lengths, drop_in, drop_attn, drop_ffn, qkv_weight, out_weight, up_weight, down_weight,
    gain_first, shift_first, gain_second, shift_second, cotangent,
):
    n_dp = lax.axis_size("dp")
    width = tokens.shape[2]
    wq = jnp.transpose(qkv_weight, (1, 0, 2))
    x0, ma, mf, cot_p, wqf, wo_p, wu_p, wd_p, qkv, qb, ctx = front(
        lengths, tokens[0], drop_in[0], drop_attn[0], drop_ffn[0], cotangent[0],
        wq, out_weight, up_weight, down_weight,
    )
    gains = (gain_first, shift_first, gain_second, shift_second)
    lay, stats, act, dg, hl, n1, rs1, g2, dr2, ng2 = middle(
        lengths, gains, ctx, x0, ma, mf, cotangent[0], cot_p, out_weight, wo_p,
        up_weight, wu_p, down_weight, wd_p, n_dp,
    )
    gq, go, gu, gd, gt, norms = back(
        lengths, gain_first, ng2, g2, dr2, act, dg, hl, n1, rs1, ctx, ma, out_weight, wo_p,
        up_weight, wu_p, down_weight, wd_p, qb, qkv, x0, wqf, drop_in[0], n_dp,
    )
    lay, gt, gq, go, gu, gd, *small = finish(
        norms, stats, [lay, gt, gq, go, gu, gd], [BF16, F32, F32, F32, F32, F32], [2, 2, 3, 1, 3, 3]
    )
    return (
        lay[None], gt[None], jnp.transpose(gq, (1, 0, 2)), go, gu, gd,
        *small[:4], *(v.reshape(()) for v in small[4:]),
    )


def solution(mesh):
    act = P("dp", None, "tensor", None)
    in_specs = (
        P("dp", "tensor", None), P(), act, act, act,
        P(None, None, "tensor"), P("tensor", None), P(None, "tensor"), P("tensor", None),
        P(), P(), P(), P(), act,
    )
    out_specs = (
        act, P("dp", "tensor", None),
        P(None, None, "tensor"), P("tensor", None), P(None, "tensor"), P("tensor", None),
        P(), P(), P(), P(), P(), P(), P(),
    )
    return jax.shard_map(
        per_device, mesh=mesh, in_specs=in_specs, out_specs=out_specs, check_vma=False
    )
```

```python
import functools
import math

import jax
import jax.numpy as jnp
from jax import lax
from jax.experimental import pallas as pl
from jax.experimental.pallas import tpu as pltpu
from jax.sharding import PartitionSpec as P

HEAD_DIM = 64
INV_KEEP = 1.0 / 0.9
SOFTMAX_WARMTH = 0.05
EPSILON = 1e-06
MASKED_SCORE = -1e30
MESH = pl.DeviceIdType.MESH
F32 = jnp.float32
BF16 = jnp.bfloat16
VMEM_LIMIT = 60 * 2**20
HIGHEST = lax.Precision.HIGHEST

TAIL_P = 0.3
TAIL = (
    0.11962929778234735,
    0.12075397394392673,
    0.09991336806236217,
    0.1285620774207718,
    -0.05368457414666341,
    0.20635459819946347,
    -0.15720376083821283,
    0.03567494667807555,
)


def dot_nn(a, b):
    return jnp.dot(a, b, preferred_element_type=F32)


def dot_nt(a, b):
    return lax.dot_general(a, b, (((1,), (1,)), ((), ())), preferred_element_type=F32)


def dot_tn(a, b):
    return lax.dot_general(a, b, (((0,), (0,)), ((), ())), preferred_element_type=F32)


def gelu_pair(x):
    z = jnp.abs(x)
    bell = jnp.exp2(x * x * (-0.5 * math.log2(math.e)))
    t = pl.reciprocal(1.0 + TAIL_P * z, approx=True)
    acc = jnp.full_like(t, TAIL[-1])
    for c in TAIL[-2::-1]:
        acc = acc * t + c
    tail = acc * t * bell
    cdf = jnp.where(x < 0.0, tail, 1.0 - tail)
    return x * cdf, cdf + x * (bell * (1.0 / math.sqrt(2.0 * math.pi)))


def split_three(v):
    hi = v.astype(BF16).astype(F32)
    rest = v - hi
    mid = rest.astype(BF16).astype(F32)
    return hi, mid, rest - mid


def front_kernel(
    lens, tok, d_in, d_at, d_ff, cot, wq, wo, wu, wd,
    x0_o, ma_o, mf_o, cot_o, wq_o, wo_o, wu_o, wd_o, qkv_o, qb_o, ctx_o,
    xv, xl, wv, qs, ms, tokv, st, qbv, ctxv, in_sem, loc_sem, send_sem, recv_sem, out_sem,
):
    d = lax.axis_index("dp")
    t = lax.axis_index("tensor")
    other = 1 - t
    peer = (d, other)
    loc = tok.shape[0]
    full = 2 * loc
    hw = wq.shape[2]
    pairs = hw // 128

    barrier = pltpu.get_barrier_semaphore()
    pl.semaphore_signal(barrier, inc=1, device_id=peer, device_id_type=MESH)

    loads = [
        pltpu.make_async_copy(tok, tokv, in_sem.at[0]),
        pltpu.make_async_copy(d_in, ms.at[0], in_sem.at[1]),
        pltpu.make_async_copy(wq, wv.at[t], in_sem.at[2]),
        pltpu.make_async_copy(d_at, ms.at[1], in_sem.at[3]),
        pltpu.make_async_copy(d_ff, ms.at[2], in_sem.at[4]),
    ]
    for c in loads:
        c.start()
    own_rows = pl.ds(pl.multiple_of(t * loc, loc), loc)

    def remote(i, src, dst):
        return pltpu.make_async_remote_copy(
            src_ref=src, dst_ref=dst, send_sem=send_sem.at[i], recv_sem=recv_sem.at[i],
            device_id=peer, device_id_type=MESH,
        )

    pl.semaphore_wait(barrier, 1)
    send_wq = remote(0, wq, wv.at[t])
    send_wq.start()
    loads[0].wait()
    loads[1].wait()
    st[0] = jnp.where(ms[0, other] != 0, tokv[...].astype(F32), 0.0).astype(BF16)
    send_x = remote(1, st.at[0], xv.at[own_rows])
    send_x.start()
    own_x = jnp.where(ms[0, t] != 0, tokv[...].astype(F32), 0.0)
    xv[own_rows, :] = own_x.astype(BF16)
    xl[own_rows, :] = (own_x * INV_KEEP).astype(BF16)
    def project(h, rows):
        for c in range(3):
            qs[h, rows, c * hw : (c + 1) * hw] = dot_nn(xl[rows, :], wv[h, c]).astype(BF16)

    loads[2].wait()
    project(t, own_rows)
    send_wq.wait_recv()
    project(other, own_rows)
    save_w = pltpu.make_async_copy(wv, wq_o, loc_sem.at[3])
    save_w.start()
    loads[3].wait()
    st[1] = ms[1, other].astype(F32).astype(BF16)
    st[2] = ms[1, t].astype(F32).astype(BF16)
    loads[4].wait()
    st[3] = ms[2, other].astype(F32).astype(BF16)
    st[4] = ms[2, t].astype(F32).astype(BF16)
    sends = [
        remote(2, wo, wo_o),
        remote(3, st.at[1], ma_o.at[own_rows]),
        remote(4, wu, wu_o),
        remote(5, wd, wd_o),
        remote(6, st.at[3], mf_o.at[own_rows]),
        remote(7, cot.at[other], cot_o),
    ]
    for c in sends:
        c.start()
    more = [
        pltpu.make_async_copy(st.at[2], ma_o.at[own_rows], loc_sem.at[0]),
        pltpu.make_async_copy(st.at[4], mf_o.at[own_rows], loc_sem.at[1]),
    ]
    for c in more:
        c.start()

    send_x.wait_recv()
    oth_rows = pl.ds(pl.multiple_of(other * loc, loc), loc)
    xl[oth_rows, :] = (xv[oth_rows, :].astype(F32) * INV_KEEP).astype(BF16)
    save_x = pltpu.make_async_copy(xv, x0_o, loc_sem.at[2])
    save_x.start()
    project(t, oth_rows)
    project(other, oth_rows)
    save_qkv = pltpu.make_async_copy(qs, qkv_o, loc_sem.at[4])
    save_qkv.start()

    length = lens[d]
    bias = jnp.where(
        lax.broadcasted_iota(jnp.int32, (full, 128), 0) < length, 0.0, MASKED_SCORE
    )
    lane = lax.broadcasted_iota(jnp.int32, (full, 128), 1)
    lane_q = lax.broadcasted_iota(jnp.int32, (512, 128), 1)

    def out_copies(i):
        return [
            pltpu.make_async_copy(qbv.at[pl.ds(2 * i, 2)], qb_o.at[pl.ds(2 * i, 2)], out_sem.at[0, i]),
            pltpu.make_async_copy(ctxv.at[i], ctx_o.at[i], out_sem.at[1, i]),
        ]

    def head_pair(i, _):
        h = i // pairs
        off = (i - h * pairs) * 128

        def part(c):
            return qs[h, :, pl.ds(pl.multiple_of(c * hw + off, 128), 128)].astype(F32)

        q2 = part(0) * HEAD_DIM**-0.5
        k2 = part(1)
        v2 = part(2)
        keys, vals, ques = [], [], []
        for a in range(2):
            own = (lane < 64) if a == 0 else (lane >= 64)
            first = 64 if a == 0 else 0
            keys.append(jnp.where(own, k2, jnp.where(lane == first, bias, 0.0)).astype(BF16))
            ques.append(jnp.where(own, q2, jnp.where(lane == first, 1.0, 0.0)).astype(BF16))
            vals.append(jnp.where(own, v2, 1.0).astype(BF16))
        for b in range(full // 512):
            rows = slice(b * 512, (b + 1) * 512)
            tops, outs = [], []
            for a in range(2):
                s = dot_nt(ques[a][rows], keys[a])
                top = jnp.max(s, axis=1, keepdims=True)
                p = jnp.exp(s - top).astype(BF16)
                outs.append(dot_nn(p, vals[a]))
                tops.append(top)
            low_half = lane_q < 64
            num = jnp.where(low_half, outs[0], outs[1])
            den = pltpu.roll(jnp.where(low_half, outs[1], outs[0]), 64, 1)
            ctxv[i, rows, :] = num / den
            for a in range(2):
                hi, mid, lo = split_three(tops[a] + jnp.log(outs[a]))
                own = low_half if a == 0 else jnp.logical_not(low_half)
                first = 64 if a == 0 else 0
                extra = jnp.where(
                    lane_q == first, hi,
                    jnp.where(lane_q == first + 1, mid,
                              jnp.where(lane_q == first + 2, lo,
                                        jnp.where(lane_q == first + 3, 1.0, 0.0))),
                )
                qbv[2 * i + a, rows, :] = jnp.where(own, q2[rows], extra).astype(BF16)
        for c in out_copies(i):
            c.start()
        return 0

    lax.fori_loop(0, 2 * pairs, head_pair, 0)

    def drain(i, _):
        for c in out_copies(i):
            c.wait()
        return 0

    lax.fori_loop(0, 2 * pairs, drain, 0)
    send_wq.wait_send()
    send_x.wait_send()
    for c in sends:
        c.wait()
    for c in more + [save_x, save_w, save_qkv]:
        c.wait()


def front(lengths, tok, d_in, d_at, d_ff, cot, wq, wo, wu, wd):
    loc, width = tok.shape
    full = 2 * loc
    half_w = 3 * wq.shape[2]
    groups = width // 128
    sds = jax.ShapeDtypeStruct
    anyspec = pl.BlockSpec(memory_space=pl.ANY)
    outs = [
        sds((full, width), BF16), sds((full, width), BF16), sds((full, width), BF16),
        sds((loc, width), BF16),
        sds((2,) + wq.shape, BF16), sds(wo.shape, BF16), sds(wu.shape, BF16), sds(wd.shape, BF16),
        sds((2, full, half_w), BF16), sds((2 * groups, full, 128), BF16),
        sds((groups, full, 128), F32),
    ]
    return pl.pallas_call(
        front_kernel,
        out_shape=outs,
        in_specs=[pl.BlockSpec(memory_space=pltpu.SMEM)] + [anyspec] * 9,
        out_specs=[anyspec] * len(outs),
        scratch_shapes=[
            pltpu.VMEM((full, width), BF16), pltpu.VMEM((full, width), BF16),
            pltpu.VMEM((2,) + wq.shape, BF16), pltpu.VMEM((2, full, half_w), BF16),
            pltpu.VMEM((3, 2, loc, width), jnp.int32), pltpu.VMEM((loc, width), BF16),
            pltpu.VMEM((5, loc, width), BF16),
            pltpu.VMEM((2 * groups, full, 128), BF16), pltpu.VMEM((groups, full, 128), F32),
            pltpu.SemaphoreType.DMA((5,)), pltpu.SemaphoreType.DMA((5,)),
            pltpu.SemaphoreType.DMA((8,)), pltpu.SemaphoreType.DMA((8,)),
            pltpu.SemaphoreType.DMA((2, groups)),
        ],
        compiler_params=pltpu.CompilerParams(
            collective_id=0, has_side_effects=True, vmem_limit_bytes=VMEM_LIMIT
        ),
        name="front",
    )(lengths, tok, d_in, d_at, d_ff, cot, wq, wo, wu, wd)


CH = 512


def middle_kernel(
    lens, ga1, sh1, ga2, sh2, ctx, x0, ma, mf, cot, cot_p, wo, wo_p, wu, wu_p, wd, wd_p,
    lay_o, loss_o, act_o, dg_o, hl_o, n1_o, rs1_o, g2_o, dr2_o, ng_o,
    ctxv, x0v, mav, mfv, cotv, wov, wuv, wdv,
    n1, n2, rs1, rs2, hl, act, dg, g2, dr2, yb, sbuf, pool_all, facc,
    in_sem, lay_sem, send_sem, recv_sem, row_sem, out_sem,
):
    d = lax.axis_index("dp")
    t = lax.axis_index("tensor")
    other = 1 - t
    peer = (d, other)
    n_dp = lax.axis_size("dp")
    n_dev = 2 * n_dp
    full, width = x0v.shape
    loc = full // 2
    groups = width // 128
    ff_half = wuv.shape[2]
    n_ch = 2 * ff_half // CH
    per_half = ff_half // CH
    me = d * 2 + t

    barrier = pltpu.get_barrier_semaphore()

    def greet(k, _):
        lin = lax.rem(me + k, n_dev)
        pl.semaphore_signal(
            barrier, inc=1, device_id=(lin // 2, lax.rem(lin, 2)), device_id_type=MESH
        )
        return 0

    lax.fori_loop(1, n_dev, greet, 0)

    own_rows = pl.ds(pl.multiple_of(t * loc, loc), loc)
    oth_rows = pl.ds(pl.multiple_of(other * loc, loc), loc)
    srcs = (ctx, wo, wo_p, x0, ma, wu, wu_p, wd, wd_p, mf, cot.at[t], cot_p)
    dsts = (
        ctxv, wov.at[t], wov.at[other], x0v, mav, wuv.at[t], wuv.at[other], wdv.at[t],
        wdv.at[other], mfv, cotv.at[own_rows], cotv.at[oth_rows],
    )
    loads = [pltpu.make_async_copy(s, v, in_sem.at[i]) for i, (s, v) in enumerate(zip(srcs, dsts))]
    for c in loads:
        c.start()
    gain1, shift1, gain2, shift2 = (r[...].reshape(1, width) for r in (ga1, sh1, ga2, sh2))
    length = lens[d]

    for c in loads[:5]:
        c.wait()

    def norm_one(b, _):
        rows = pl.ds(pl.multiple_of(b * 256, 256), 256)
        c2 = jnp.concatenate([ctxv[g, rows, :].astype(BF16) for g in range(groups)], axis=1)
        branch = dot_nn(c2, wov[...].reshape(width, width))
        r = (x0v[rows, :].astype(F32) + branch * mav[rows, :].astype(F32)) * INV_KEEP
        cen = r - jnp.mean(r, axis=1, keepdims=True)
        rstd = lax.rsqrt(jnp.mean(cen * cen, axis=1, keepdims=True) + EPSILON)
        n = cen * rstd
        n1[rows, :] = n
        rs1[rows, :] = jnp.broadcast_to(rstd, (256, 128))
        hl[rows, :] = (n * gain1 + shift1).astype(BF16)
        return 0

    lax.fori_loop(0, full // 256, norm_one, 0)
    saves = [
        pltpu.make_async_copy(s, o, out_sem.at[i])
        for i, (s, o) in enumerate(((hl, hl_o), (n1, n1_o), (rs1, rs1_o)))
    ]
    for c in saves:
        c.start()
    for c in loads[5:]:
        c.wait()

    def row_copies(b):
        rows = pl.ds(pl.multiple_of(b * 512, 512), 512)
        return [
            pltpu.make_async_copy(act.at[rows], act_o.at[rows], row_sem.at[b, 0]),
            pltpu.make_async_copy(dg.at[rows], dg_o.at[rows], row_sem.at[b, 1]),
        ]

    def ffn(b, pooled):
        rows = pl.ds(pl.multiple_of(b * 512, 512), 512)
        def up(j):
            h, o = j // per_half, (j % per_half) * CH
            return dot_nn(hl[rows, :], wuv[h, :, o : o + CH])

        ahead = up(0)
        for j in range(n_ch):
            h, o = j // per_half, (j % per_half) * CH
            pre = ahead
            if j + 1 < n_ch:
                ahead = up(j + 1)
            a, da = gelu_pair(pre)
            ab = a.astype(BF16)
            act[rows, j * CH : (j + 1) * CH] = ab
            dg[rows, j * CH : (j + 1) * CH] = da.astype(BF16)
            term = dot_nn(ab, wdv[h, o : o + CH, :])
            if j == 0:
                facc[...] = term
            else:
                facc[...] += term
        for c in row_copies(b):
            c.start()
        for s in range(2):
            sub = pl.ds(pl.multiple_of(b * 512 + s * 256, 256), 256)
            r = n1[sub, :] * gain1 + shift1 + facc[s * 256 : (s + 1) * 256, :] * (
                mfv[sub, :].astype(F32) * INV_KEEP
            )
            cen = r - jnp.mean(r, axis=1, keepdims=True)
            rstd = lax.rsqrt(jnp.mean(cen * cen, axis=1, keepdims=True) + EPSILON)
            n = cen * rstd
            n2[sub, :] = n
            rs2[sub, :] = jnp.broadcast_to(rstd, (256, 128))
            y = n * gain2 + shift2
            yb[sub, :] = y.astype(BF16)
            pos = lax.broadcasted_iota(jnp.int32, (256, width), 0) + (b * 512 + s * 256)
            pooled = pooled + jnp.sum(jnp.where(pos < length, y, 0.0), axis=0, keepdims=True)
        return pooled

    pooled = lax.fori_loop(0, full // 512, ffn, jnp.zeros((1, width), F32))

    for g in range(groups):
        sbuf[g : g + 1, :] = pooled[:, g * 128 : (g + 1) * 128]
    sbuf[groups:, :] = jnp.zeros((8 - groups, 128), F32)
    slot = t * n_dp + d
    pl.semaphore_wait(barrier, n_dev - 1)

    def push(k, start):
        lin = lax.rem(me + k, n_dev)
        pd, pt = lin // 2, lax.rem(lin, 2)
        c = pltpu.make_async_remote_copy(
            src_ref=sbuf, dst_ref=pool_all.at[slot], send_sem=send_sem.at[k],
            recv_sem=recv_sem.at[slot], device_id=(pd, pt), device_id_type=MESH,
        )
        if start:
            c.start()
        else:
            c.wait_send()
        return 0

    lax.fori_loop(1, n_dev, lambda k, _: push(k, True), 0)
    lay_local = pltpu.make_async_copy(yb.at[own_rows], lay_o.at[t], lay_sem.at[0])
    lay_local.start()
    lay_send = pltpu.make_async_remote_copy(
        src_ref=yb.at[oth_rows], dst_ref=lay_o.at[t], send_sem=lay_sem.at[1],
        recv_sem=lay_sem.at[2], device_id=peer, device_id_type=MESH,
    )
    lay_send.start()
    pool_all[slot] = sbuf[...]

    def arrive(k, _):
        lin = lax.rem(me + k, n_dev)
        s = lax.rem(lin, 2) * n_dp + lin // 2
        pltpu.make_async_remote_copy(
            src_ref=sbuf, dst_ref=pool_all.at[s], send_sem=send_sem.at[k],
            recv_sem=recv_sem.at[s], device_id=(lin // 2, lax.rem(lin, 2)), device_id_type=MESH,
        ).wait_recv()
        return 0

    lax.fori_loop(1, n_dev, arrive, 0)

    pair_i = lax.broadcasted_iota(jnp.int32, (n_dp, 1), 0)
    len_col = jnp.zeros((n_dp, 1), F32)
    for k in range(n_dp):
        len_col = jnp.where(pair_i == k, lens[k].astype(F32), len_col)
    units = []
    scales = []
    for v in range(2):
        raw = jnp.concatenate(
            [pool_all[v * n_dp : (v + 1) * n_dp, g, :] for g in range(groups)], axis=1
        )
        pv = raw / len_col
        scale = lax.rsqrt(jnp.sum(pv * pv, axis=1, keepdims=True) + EPSILON)
        units.append(pv * scale)
        scales.append(scale)
    u0, u1 = units
    nt = (((1,), (1,)), ((), ()))
    row_i = lax.broadcasted_iota(jnp.int32, (n_dp, n_dp), 0)
    col_i = lax.broadcasted_iota(jnp.int32, (n_dp, n_dp), 1)
    diag = row_i == col_i
    sim = lax.dot_general(u0, u1, nt, precision=HIGHEST, preferred_element_type=F32) / SOFTMAX_WARMTH
    top = jnp.max(sim, axis=1, keepdims=True)
    raw = jnp.exp(sim - top)
    total = jnp.sum(raw, axis=1, keepdims=True)
    ce = top + jnp.log(total) - jnp.sum(jnp.where(diag, sim, 0.0), axis=1, keepdims=True)
    loss = jnp.sum(ce, axis=0, keepdims=True) / n_dp
    gap = u0 - u1
    align = jnp.sum(jnp.sum(gap * gap, axis=1, keepdims=True), axis=0, keepdims=True) / n_dp
    sq = jnp.sum(u0 * u0, axis=1, keepdims=True)
    sq_row = lax.dot_general(
        jnp.ones((n_dp, width), F32), u0 * u0, nt, precision=HIGHEST, preferred_element_type=F32
    )
    inner = lax.dot_general(u0, u0, nt, precision=HIGHEST, preferred_element_type=F32)
    pot = jnp.where(diag, 0.0, jnp.exp(-2.0 * (sq + sq_row - 2.0 * inner)))
    uni = jnp.log(
        jnp.sum(jnp.sum(pot, axis=1, keepdims=True), axis=0, keepdims=True) / (n_dp * (n_dp - 1))
    )
    stat_i = lax.broadcasted_iota(jnp.int32, (8, 128), 0)
    loss_o[...] = jnp.where(stat_i == 0, loss, jnp.where(stat_i == 1, align, uni))
    d_sim = (raw / total - jnp.where(diag, 1.0, 0.0)) / SOFTMAX_WARMTH
    d_u0 = jnp.dot(d_sim, u1, precision=HIGHEST, preferred_element_type=F32)
    d_u1 = lax.dot_general(
        d_sim, u0, (((0,), (0,)), ((), ())), precision=HIGHEST, preferred_element_type=F32
    )
    first_view = t == 0
    du = jnp.where(first_view, d_u0, d_u1)
    u = jnp.where(first_view, u0, u1)
    scale = jnp.where(first_view, scales[0], scales[1])
    d_pool = (du - u * jnp.sum(u * du, axis=1, keepdims=True)) * scale / len_col
    mine = lax.broadcasted_iota(jnp.int32, (n_dp, width), 0) == d
    pool_grad = jnp.sum(jnp.where(mine, d_pool, 0.0), axis=0, keepdims=True)

    def norm_two_back(b, sums):
        rows = pl.ds(pl.multiple_of(b * 256, 256), 256)
        pos = lax.broadcasted_iota(jnp.int32, (256, width), 0) + b * 256
        dy = cotv[rows, :].astype(F32) + jnp.where(pos < length, pool_grad, 0.0)
        n = n2[rows, :]
        g = dy * gain2
        dr = (g - jnp.mean(g, axis=1, keepdims=True) - n * jnp.mean(g * n, axis=1, keepdims=True)) * rs2[rows, :1]
        dr2[rows, :] = dr
        g2[rows, :] = (dr * (mfv[rows, :].astype(F32) * INV_KEEP)).astype(BF16)
        return (
            sums[0] + jnp.sum(dy * n, axis=0, keepdims=True),
            sums[1] + jnp.sum(dy, axis=0, keepdims=True),
        )

    zero = jnp.zeros((1, width), F32)
    gg2, gs2 = lax.fori_loop(0, full // 256, norm_two_back, (zero, zero))

    ng_o[...] = jnp.concatenate([gg2, gs2, zero, zero, zero, zero, zero, zero], axis=0)
    more = [
        pltpu.make_async_copy(g2, g2_o, out_sem.at[3]),
        pltpu.make_async_copy(dr2, dr2_o, out_sem.at[4]),
    ]
    for c in more:
        c.start()
    for b in range(full // 512):
        for c in row_copies(b):
            c.wait()
    lax.fori_loop(1, n_dev, lambda k, _: push(k, False), 0)
    lay_local.wait()
    lay_send.wait()
    for c in saves + more:
        c.wait()


def middle(
    lengths, gains, ctx, x0, ma, mf, cot, cot_p, wo, wo_p, wu, wu_p, wd, wd_p, n_dp
):
    full, width = x0.shape
    loc = full // 2
    ff = 2 * wd.shape[0]
    n_dev = 2 * n_dp
    sds = jax.ShapeDtypeStruct
    anyspec = pl.BlockSpec(memory_space=pl.ANY)
    vspec = pl.BlockSpec(memory_space=pltpu.VMEM)
    outs = [
        sds((2, loc, width), BF16), sds((8, 128), F32), sds((full, ff), BF16), sds((full, ff), BF16),
        sds((full, width), BF16), sds((full, width), F32), sds((full, 128), F32),
        sds((full, width), BF16), sds((full, width), F32), sds((8, width), F32),
    ]
    vm = pltpu.VMEM
    dma = pltpu.SemaphoreType.DMA
    return pl.pallas_call(
        middle_kernel,
        out_shape=outs,
        in_specs=[pl.BlockSpec(memory_space=pltpu.SMEM)] + [vspec] * 4 + [anyspec] * 12,
        out_specs=[anyspec, vspec] + [anyspec] * 7 + [vspec],
        scratch_shapes=[
            vm(ctx.shape, F32), vm((full, width), BF16), vm((full, width), BF16),
            vm((full, width), BF16), vm((full, width), BF16), vm((2,) + wo.shape, BF16),
            vm((2,) + wu.shape, BF16), vm((2,) + wd.shape, BF16),
            vm((full, width), F32), vm((full, width), F32), vm((full, 128), F32), vm((full, 128), F32),
            vm((full, width), BF16), vm((full, ff), BF16), vm((full, ff), BF16),
            vm((full, width), BF16), vm((full, width), F32), vm((full, width), BF16),
            vm((8, 128), F32), vm((n_dev, 8, 128), F32), vm((512, width), F32),
            dma((12,)), dma((3,)), dma((n_dev,)), dma((n_dev,)), dma((full // 512, 2)), dma((5,)),
        ],
        compiler_params=pltpu.CompilerParams(
            collective_id=1, has_side_effects=True, vmem_limit_bytes=VMEM_LIMIT
        ),
        name="middle",
    )(lengths, *gains, ctx, x0, ma, mf, cot, cot_p, wo, wo_p, wu, wu_p, wd, wd_p)


ORDERS_16 = (
    ((0, 1, 2, 3), (1, 0, 2, 3)), ((2, 0, 1, 3), (2, 1, 0, 3)),
    ((0, 1, 2, 3), (1, 0, 2, 3)), ((0, 1, 2, 3), (1, 0, 2, 3)),
    ((0, 2, 3, 1), (1, 2, 3, 0)), ((0, 1, 2, 3), (1, 0, 2, 3)),
    ((0, 1, 2, 3), (1, 0, 2, 3)), ((0, 2, 1, 3), (1, 2, 0, 3)),
    ((2, 0, 1, 3), (2, 1, 0, 3)), ((0, 2, 1, 3), (1, 2, 0, 3)),
)
TABLE_16 = (
    (), (), (), (), (), (0,),
    (), (1,), (2,), (), (0,), (),
    (3,), (2,), (1, 0), (), (4, 3), (),
    (0, 2), (1,), (5, 4, 0), (2, 3), (1,), (),
    (), (5, 4, 0), (2,), (3,), (1, 5), (4, 0, 2),
    (3, 5, 1, 4), (2, 0, 1, 4, 3), (6, 5), (2, 3, 4), (0, 5, 1), (6, 4),
    (7, 5, 2), (3, 6), (1, 4), (6, 7), (), (8, 9, 5),
    (6,), (3,), (9, 7), (), (), (5, 8, 7, 6, 9, 8, 7, 9, 8, 6, 7, 9, 6, 8, 7, 9, 8, 6, 9, 8, 7, 8, 9, 7, 8, 9),
)
LAST_PARTS = 2


def sum_plan(n_dp, n_chunks, rows):
    bits = n_dp.bit_length() - 1
    if bits == 4 and n_chunks + LAST_PARTS - 1 == len(ORDERS_16):
        part = rows // LAST_PARTS
        places = [(c, 0, rows) for c in range(n_chunks - 1)]
        places += [(n_chunks - 1, k * part, part) for k in range(LAST_PARTS)]
        return [p + o for p, o in zip(places, ORDERS_16)], TABLE_16
    plain = tuple(range(bits))

    def turn(k):
        return plain[k % bits :] + plain[: k % bits] if bits else plain

    return [(c, 0, rows, turn(2 * c), turn(2 * c + 2)) for c in range(n_chunks)], None


def back_kernel(
    lens, ga1, ng2, g2_i, dr2_i, act_i, dg_i, hl_i, n1_i, rs1_i, ctx_i, ma_i, wo, wo_p, wu, wu_p,
    wd, wd_p, qb_i, qkv_i, x0_i, wq_i, din_i,
    gq_o, go_o, gu_o, gd_o, gt_o, ng_o,
    mine, core_in, ring_in, stage, g2, dr, dobv, gin, nsend, nall,
    in_sem, core_send, core_recv, ring_send, ring_recv, out_sem, nsend_sem, nrecv_sem, gt_sem,
):
    d = lax.axis_index("dp")
    t = lax.axis_index("tensor")
    other = 1 - t
    peer = (d, other)
    n_dp = lax.axis_size("dp")
    n_dev = 2 * n_dp
    me = d * 2 + t
    full, width = g2.shape
    loc = full // 2
    ff_half = wu.shape[1]
    half_w = qkv_i.shape[2]
    hw = half_w // 3
    pairs = hw // 128
    groups = width // 128
    n_cols = ff_half // CH
    rows_c = mine.shape[1]
    bits = n_dp.bit_length() - 1
    n_chunks = mine.shape[0]
    items, table = sum_plan(n_dp, n_chunks, rows_c)

    barrier = pltpu.get_barrier_semaphore()

    def greet(k, _):
        lin = lax.rem(me + k, n_dev)
        pl.semaphore_signal(
            barrier, inc=1, device_id=(lin // 2, lax.rem(lin, 2)), device_id_type=MESH
        )
        return 0

    lax.fori_loop(1, n_dev, greet, 0)

    def load(pairs_of, first):
        copies = [
            pltpu.make_async_copy(s, v, in_sem.at[first + i]) for i, (s, v) in enumerate(pairs_of)
        ]
        for c in copies:
            c.start()
        return copies

    def core_copy(c):
        return pltpu.make_async_remote_copy(
            src_ref=stage.at[c % 3], dst_ref=core_in.at[c], send_sem=core_send.at[c],
            recv_sem=core_recv.at[c], device_id=peer, device_id_type=MESH,
        )

    def plan(i):
        steps = []
        _, off, size, o0, o1 = items[i]
        place = off
        for b0, b1 in zip(o0, o1):
            size //= 2
            beta = lax.rem(d // 2**b0, 2) * other + lax.rem(d // 2**b1, 2) * t
            hop = 2**b0 * other + 2**b1 * t
            partner = d + (1 - 2 * beta) * hop
            keep = pl.multiple_of(off + beta * size, 16)
            sent = pl.multiple_of(off + (1 - beta) * size, 16)
            steps.append((partner, keep, sent, size, place))
            off = off + beta * size
            place += size
        return steps

    def ring_copy(i, s):
        c = items[i][0]
        if s < bits:
            partner, keep, sent, size, place = plan(i)[s]
            src, dst = mine.at[c, pl.ds(sent, size)], ring_in.at[c, pl.ds(place, size)]
        else:
            partner, keep, sent, size, place = plan(i)[2 * bits - 1 - s]
            src, dst = core_in.at[c, pl.ds(keep, size)], core_in.at[c, pl.ds(keep, size)]
        return pltpu.make_async_remote_copy(
            src_ref=src, dst_ref=dst, send_sem=ring_send.at[i, s], recv_sem=ring_recv.at[i, s],
            device_id=(partner, t), device_id_type=MESH,
        )

    def add_in(c, dst, dst_off, size, src, src_off):
        step = math.gcd(size, 384)

        def body(i, _):
            a = pl.ds(pl.multiple_of(dst_off + i * step, 16), step)
            b = pl.ds(pl.multiple_of(src_off + i * step, 16), step)
            dst[c, a, :] = (mine[c, a, :].astype(F32) + src[c, b, :].astype(F32)).astype(BF16)
            return 0

        lax.fori_loop(0, size // step, body, 0)

    def out_copies(c):
        dst = []
        if c < n_cols:
            for g in range(groups):
                dst.append((g * CH, CH, gd_o.at[pl.ds(c * CH, CH), pl.ds(g * 128, 128)]))
        elif c < 2 * n_cols:
            for g in range(CH // 128):
                col = (c - n_cols) * CH + g * 128
                dst.append((g * width, width, gu_o.at[:, pl.ds(col, 128)]))
        else:
            j = c - 2 * n_cols
            for g in range(3):
                dst.append((g * width, width, gq_o.at[g, :, pl.ds(j * 128, 128)]))
            for g in range(groups):
                dst.append(
                    (3 * width + g * 128, 128, go_o.at[pl.ds(j * 128, 128), pl.ds(g * 128, 128)])
                )
        return [
            pltpu.make_async_copy(core_in.at[c, pl.ds(o, n)], r, out_sem.at[c, i])
            for i, (o, n, r) in enumerate(dst)
        ]

    begun = {}
    made = set()
    left = [sum(1 for it in items if it[0] == c) for c in range(n_chunks)]
    now = [0]

    def step(i):
        c, first, count = items[i][:3]
        a = begun.get(i, 0)
        assert c in made and a <= 2 * bits
        begun[i] = a + 1
        if a == 0:
            if first == 0:
                core_copy(c).wait()
            add_in(c, mine, first, count, core_in, first)
        else:
            ring_copy(i, a - 1).wait()
            if a <= bits:
                _, keep, _, size, place = plan(i)[a - 1]
                add_in(c, core_in if a == bits else mine, keep, size, ring_in, place)
        if a < 2 * bits:
            ring_copy(i, a).start()
        else:
            left[c] -= 1
            if left[c] == 0:
                for cp in out_copies(c):
                    cp.start()

    def mark():
        at = now[0]
        now[0] += 1
        if table is not None:
            todo = table[at]
        elif at % 2 == 0:
            todo = unfinished()
        else:
            todo = ()
        for i in todo:
            step(i)

    def unfinished():
        return [
            i for i in range(len(items)) if items[i][0] in made and begun.get(i, 0) <= 2 * bits
        ]

    def finish_all():
        for i in table[now[0]] if table is not None else ():
            step(i)
        while unfinished():
            for i in unfinished():
                step(i)

    def begin(c):
        core_copy(c).start()

    def put(ref, at, val):
        n = val.shape[0]
        for g in range(val.shape[1] // 128):
            ref[at + g * n : at + (g + 1) * n, :] = val[:, g * 128 : (g + 1) * 128].astype(BF16)

    gain1 = ga1[...].reshape(1, width)
    met = [False]

    def meet():
        if not met[0]:
            pl.semaphore_wait(barrier, n_dev - 1)
            met[0] = True

    def feed_forward(act, dg, hl, hlt, wuv, wdv):
        blocks = [
            pl.ds(pl.multiple_of(h * ff_half + c * CH, CH), CH)
            for c in range(n_cols) for h in (other, t)
        ]
        first = load(
            [(g2_i, g2)] + [(act_i.at[:, col], act.at[:, col]) for col in blocks]
            + [(dr2_i, dr), (hl_i, hl), (dg_i, dg), (wd, wdv.at[t]), (wd_p, wdv.at[other]),
               (wu, wuv.at[t]), (wu_p, wuv.at[other])], 20,
        )
        first[0].wait()
        mark()
        for c in range(n_cols):
            for h, ref in ((other, stage.at[c % 3]), (t, mine.at[c])):
                at = 2 * c + (0 if h is other else 1)
                first[1 + at].wait()
                put(ref, 0, dot_tn(act[:, blocks[at]], g2[...]))
                if h is other:
                    meet()
                    begin(c)
                else:
                    made.add(c)
                mark()
        for cp in first[1 + 2 * n_cols :]:
            cp.wait()
        for k in range(groups):
            cols = slice(k * 128, (k + 1) * 128)
            hlt[cols, :] = hl[:, cols].astype(F32).T.astype(BF16)
        mark()
        for k in range(n_cols):
            c = n_cols + k
            for h, ref in ((other, stage.at[c % 3]), (t, mine.at[c])):
                col = pl.ds(pl.multiple_of(h * ff_half + k * CH, CH), CH)
                for b in range(full // 512):
                    rows = slice(b * 512, (b + 1) * 512)
                    da = dot_nt(g2[rows, :], wdv[h, k * CH : (k + 1) * CH, :])
                    dp = (da * dg[rows, col].astype(F32)).astype(BF16)
                    dg[rows, col] = dp
                    dr[rows, :] += dot_nt(dp, wuv[h, :, k * CH : (k + 1) * CH])
                mark()
                put(ref, 0, dot_nn(hlt[...], dg[:, col]))
                if h is other:
                    begin(c)
                else:
                    made.add(c)
                mark()

    vm = pltpu.VMEM
    ff = 2 * ff_half
    pl.run_scoped(
        feed_forward, vm((full, ff), BF16), vm((full, ff), BF16), vm((full, width), BF16),
        vm((width, full), BF16), vm((2,) + wu.shape, BF16), vm((2,) + wd.shape, BF16),
    )

    def norm_and_out(n1, rs1, ctxv, mav, wov, gov):
        first = load(
            [(n1_i, n1), (rs1_i, rs1), (ma_i, mav), (wo, wov.at[t]), (wo_p, wov.at[other]),
             (ctx_i, ctxv)], 9,
        )
        for cp in first[:3]:
            cp.wait()

        def norm_one_back(b, sums):
            rows = pl.ds(pl.multiple_of(b * 256, 256), 256)
            dh = dr[rows, :]
            n = n1[rows, :]
            g = dh * gain1
            r = (
                g - jnp.mean(g, axis=1, keepdims=True) - n * jnp.mean(g * n, axis=1, keepdims=True)
            ) * rs1[rows, :1]
            dr[rows, :] = r
            g2[rows, :] = (r * (mav[rows, :].astype(F32) * INV_KEEP)).astype(BF16)
            return (
                sums[0] + jnp.sum(dh * n, axis=0, keepdims=True),
                sums[1] + jnp.sum(dh, axis=0, keepdims=True),
            )

        zero = jnp.zeros((1, width), F32)
        gg1, gs1 = lax.fori_loop(0, full // 256, norm_one_back, (zero, zero))
        for i, row in enumerate((gg1, gs1, ng2[0:1, :], ng2[1:2, :])):
            for g in range(groups):
                nsend[i * groups + g : i * groups + g + 1, :] = row[:, g * 128 : (g + 1) * 128]
        nall[me] = nsend[...]
        lax.fori_loop(1, n_dev, lambda k, _: push(k, 0), 0)
        for cp in first[3:]:
            cp.wait()
        mark()
        lane = lax.broadcasted_iota(jnp.int32, (full, 128), 1)
        seg = (
            (lax.broadcasted_iota(jnp.int32, (128, 128), 0) < 64)
            != (lax.broadcasted_iota(jnp.int32, (128, 128), 1) < 64)
        ).astype(F32).astype(BF16)
        for g in range(groups):
            h, j = g // pairs, g % pairs
            cf = ctxv[g]
            gov[g * 128 : (g + 1) * 128, :] = dot_tn(cf.astype(BF16), g2[...]).astype(BF16)
            dc = dot_nt(g2[...], wov[h, j * 128 : (j + 1) * 128, :]).astype(BF16).astype(F32)
            hi, mid, lo = split_three(dc * cf)
            delta = (
                dot_nn(hi.astype(BF16), seg) + dot_nn(mid.astype(BF16), seg)
                + dot_nn(lo.astype(BF16), seg)
            )
            hi, mid, lo = split_three(delta)
            for a in range(2):
                own = (lane < 64) if a == 0 else (lane >= 64)
                z = 64 if a == 0 else 0
                extra = jnp.where(
                    lane == z, hi,
                    jnp.where(lane == z + 1, mid, jnp.where(lane == z + 2, lo, 0.0)),
                )
                dobv[2 * g + a] = jnp.where(own, dc, extra).astype(BF16)
            if g < groups - 1:
                mark()
        for j in range(pairs):
            c = 2 * n_cols + j
            for h, ref in ((other, stage.at[c % 3]), (t, mine.at[c])):
                row = pl.ds(pl.multiple_of((h * pairs + j) * 128, 128), 128)
                for g in range(groups):
                    ref[3 * width + g * 128 : 3 * width + (g + 1) * 128, :] = gov[
                        row, g * 128 : (g + 1) * 128
                    ]
        mark()

    def push(k, what):
        lin = lax.rem(me + k, n_dev)
        c = pltpu.make_async_remote_copy(
            src_ref=nsend, dst_ref=nall.at[me], send_sem=nsend_sem.at[k], recv_sem=nrecv_sem.at[me],
            device_id=(lin // 2, lax.rem(lin, 2)), device_id_type=MESH,
        )
        if what == 0:
            c.start()
        else:
            c.wait_send()
        return 0

    def arrive(k, _):
        lin = lax.rem(me + k, n_dev)
        pltpu.make_async_remote_copy(
            src_ref=nsend, dst_ref=nall.at[lin], send_sem=nsend_sem.at[k],
            recv_sem=nrecv_sem.at[lin], device_id=(lin // 2, lax.rem(lin, 2)), device_id_type=MESH,
        ).wait_recv()
        return 0


    def attention(first, dq3, qbv, qkvv, xv, xt):
        length = lens[d]
        lane = lax.broadcasted_iota(jnp.int32, (full, 128), 1)
        bias = jnp.where(
            lax.broadcasted_iota(jnp.int32, (full, 128), 0) < length, 0.0, MASKED_SCORE
        )
        kb = 512
        low_half = lax.broadcasted_iota(jnp.int32, (kb, 128), 1) < 64
        for cp in first:
            cp.wait()
        for g in range(groups):
            cols = slice(g * 128, (g + 1) * 128)
            xt[cols, :] = (xv[:, cols].astype(F32) * INV_KEEP).T.astype(BF16)
        mark()

        def head_pair(h, j):
            i = h * pairs + j

            def part(c):
                return qkvv[h, :, c * hw + j * 128 : c * hw + (j + 1) * 128]

            k2f = part(1).astype(F32)
            k2t = k2f.T.astype(BF16)
            v2f = part(2).astype(F32)
            dks, dvs, dqs = [], [], []
            for a in range(2):
                own = (lane < 64) if a == 0 else (lane >= 64)
                z = 64 if a == 0 else 0
                minus = jnp.where(jnp.logical_and(lane >= z, lane < z + 3), -1.0, 0.0)
                ka = jnp.where(own, k2f, jnp.where(lane == z + 3, bias, minus)).astype(BF16)
                va = jnp.where(own, v2f, minus).astype(BF16)
                qa = qbv[2 * i + a]
                da = dobv[2 * i + a]
                dk, dv = [], []
                dqt = None
                for b in range(full // kb):
                    rows = slice(b * kb, (b + 1) * kb)
                    p = jnp.exp(dot_nt(ka[rows], qa))
                    ds = (p * dot_nt(va[rows], da)).astype(BF16)
                    dv.append(dot_nn(p.astype(BF16), da))
                    dk.append(dot_nn(ds, qa))
                    term = dot_nn(k2t[a * 64 : (a + 1) * 64, rows], ds)
                    dqt = term if dqt is None else dqt + term
                dks.append(dk)
                dvs.append(dv)
                dqs.append(dqt)
                if a == 0:
                    mark()
            for b in range(full // kb):
                rows = slice(b * kb, (b + 1) * kb)
                dq3[i, rows, 128:256] = jnp.where(low_half, dks[0][b], dks[1][b]).astype(BF16)
                dq3[i, rows, 256:384] = jnp.where(low_half, dvs[0][b], dvs[1][b]).astype(BF16)
            dq = jnp.concatenate(dqs, axis=0) * HEAD_DIM**-0.5
            dq3[i, :, 0:128] = dq.T.astype(BF16)

        for j in range(pairs):
            c = 2 * n_cols + j
            for h, ref in ((other, stage.at[c % 3]), (t, mine.at[c])):
                head_pair(h, j)
                put(ref, 0, dot_nn(xt[...], dq3[h * pairs + j]))
                if h is other:
                    begin(c)
                else:
                    made.add(c)
                mark()

    def to_input(first, dq3, wqv, dinv, acc):
        for cp in first:
            cp.wait()
        mark()

        def d_input(start):
            rows = pl.ds(pl.multiple_of(start, 256), 256)
            total = dr[rows, :]
            for h in range(2):
                lhs = jnp.concatenate(
                    [dq3[h * pairs + j, rows, c * 128 : (c + 1) * 128] for c in range(3) for j in range(pairs)],
                    axis=1,
                )
                total = total + dot_nt(
                    lhs, jnp.concatenate([wqv[h, c] for c in range(3)], axis=1)
                )
            return total

        for s in range(loc // 256):
            g2[s * 256 : (s + 1) * 256, :] = d_input(other * loc + s * 256).astype(BF16)
            if s < loc // 256 - 1:
                mark()
        send = pltpu.make_async_remote_copy(
            src_ref=g2.at[pl.ds(0, loc)], dst_ref=gin, send_sem=gt_sem.at[0], recv_sem=gt_sem.at[1],
            device_id=peer, device_id_type=MESH,
        )
        send.start()
        mark()
        for s in range(loc // 256):
            acc[s * 256 : (s + 1) * 256, :] = d_input(t * loc + s * 256)
            mark()
        send.wait()
        for s in range(loc // 256):
            rows = slice(s * 256, (s + 1) * 256)
            acc[rows, :] = (
                jnp.where(dinv[t, rows, :] != 0, acc[rows, :], 0.0)
                + jnp.where(dinv[other, rows, :] != 0, gin[rows, :].astype(F32), 0.0)
            ) * INV_KEEP
        out = pltpu.make_async_copy(acc, gt_o, gt_sem.at[2])
        out.start()
        mark()
        lax.fori_loop(1, n_dev, arrive, 0)
        total = nall[0]
        for k in range(1, n_dev):
            total = total + nall[k]
        ng_o[...] = total
        finish_all()
        out.wait()

    def rest(qbv, qkvv, xv):
        ahead = load([(qkv_i, qkvv), (qb_i, qbv), (x0_i, xv)], 15)
        pl.run_scoped(
            norm_and_out, vm((full, width), F32), vm((full, 128), F32), vm((groups, full, 128), F32),
            vm((full, width), BF16), vm((2,) + wo.shape, BF16), vm((width, width), BF16),
        )

        def projections(dq3, xt, wqv, dinv, acc):
            later = load([(wq_i, wqv), (din_i, dinv)], 18)
            attention(ahead, dq3, qbv, qkvv, xv, xt)
            to_input(later, dq3, wqv, dinv, acc)

        pl.run_scoped(
            projections, vm((groups, full, 384), BF16), vm((width, full), BF16),
            vm(wq_i.shape, BF16), vm(din_i.shape, jnp.int32), vm((loc, width), F32),
        )

    pl.run_scoped(
        rest, vm((2 * groups, full, 128), BF16), vm(qkv_i.shape, BF16), vm((full, width), BF16)
    )
    for c in range(n_chunks):
        for cp in out_copies(c):
            cp.wait()
    lax.fori_loop(1, n_dev, lambda k, _: push(k, 1), 0)


def back(
    lengths, gain_first, ng2, g2, dr2, act, dg, hl, n1, rs1, ctx, ma, wo, wo_p, wu, wu_p, wd, wd_p, qb,
    qkv, x0, wq, d_in, n_dp,
):
    full, width = x0.shape
    loc = full // 2
    groups = width // 128
    bits = n_dp.bit_length() - 1
    n_dev = 2 * n_dp
    n_chunks = 2 * (wu.shape[1] // CH) + groups // 2
    rows_c = CH * width // 128
    n_items = len(sum_plan(n_dp, n_chunks, rows_c)[0])
    sds = jax.ShapeDtypeStruct
    anyspec = pl.BlockSpec(memory_space=pl.ANY)
    vspec = pl.BlockSpec(memory_space=pltpu.VMEM)
    vm = pltpu.VMEM
    dma = pltpu.SemaphoreType.DMA
    return pl.pallas_call(
        back_kernel,
        out_shape=[
            sds(wq.shape[1:], BF16), sds(wo.shape, BF16), sds(wu.shape, BF16), sds(wd.shape, BF16),
            sds((loc, width), F32), sds((4 * groups, 128), F32),
        ],
        in_specs=[pl.BlockSpec(memory_space=pltpu.SMEM), vspec, vspec] + [anyspec] * 20,
        out_specs=[anyspec] * 5 + [vspec],
        scratch_shapes=[
            vm((n_chunks, rows_c, 128), BF16), vm((n_chunks, rows_c, 128), BF16),
            vm((n_chunks, rows_c, 128), BF16), vm((3, rows_c, 128), BF16),
            vm((full, width), BF16), vm((full, width), F32), vm(qb.shape, BF16),
            vm((loc, width), BF16),
            vm((4 * groups, 128), F32), vm((n_dev, 4 * groups, 128), F32),
            dma((36,)), dma((n_chunks,)), dma((n_chunks,)), dma((n_items, 2 * bits)),
            dma((n_items, 2 * bits)), dma((n_chunks, 9)), dma((n_dev,)), dma((n_dev,)), dma((3,)),
        ],
        compiler_params=pltpu.CompilerParams(
            collective_id=2, has_side_effects=True, vmem_limit_bytes=62 * 2**20
        ),
        name="back",
    )(
        lengths, gain_first, ng2, g2, dr2, act, dg, hl, n1, rs1, ctx, ma, wo, wo_p, wu, wu_p, wd, wd_p,
        qb, qkv, x0, wq, d_in,
    )


def finish_kernel(n_parts, *refs):
    n = len(n_parts)
    norms, stats = refs[:2]
    refs = refs[2:]
    srcs, dsts = refs[:n], refs[n : 2 * n]
    small = refs[2 * n : 2 * n + 7]
    refs = refs[2 * n + 7 :]
    narrow, wide = refs[:n], refs[n : 2 * n]
    in_sem, out_sem = refs[2 * n :]

    def piece(i, k):
        rows = srcs[i].shape[0] // n_parts[i]
        return pl.ds(k * rows, rows)

    def widen(i, k):
        flat = len(srcs[i].shape) == 2
        first = k * (srcs[i].shape[0] // n_parts[i]) if flat else 0
        count = srcs[i].shape[0] // n_parts[i] if flat else srcs[i].shape[1]
        src = narrow[i] if flat else narrow[i].at[k]
        dst = wide[i] if flat else wide[i].at[k]

        def body(b, _):
            rows = pl.ds(pl.multiple_of(first + b * 64, 64), 64)
            dst[rows, :] = src[rows, :].astype(F32)
            return 0

        lax.fori_loop(0, count // 64, body, 0)

    todo = [(i, k) for i in range(n) for k in range(n_parts[i])]
    loads = []
    for m, (i, k) in enumerate(todo):
        r = piece(i, k)
        loads.append(pltpu.make_async_copy(srcs[i].at[r], narrow[i].at[r], in_sem.at[m]))
        loads[-1].start()
    saves = []
    for m, (i, k) in enumerate(todo):
        r = piece(i, k)
        loads[m].wait()
        from_ref = narrow[i]
        if srcs[i].dtype != dsts[i].dtype:
            widen(i, k)
            from_ref = wide[i]
        saves.append(pltpu.make_async_copy(from_ref.at[r], dsts[i].at[r], out_sem.at[m]))
        saves[-1].start()
    groups = norms.shape[0] // 4
    for i in range(4):
        row = jnp.concatenate([norms[i * groups + g : i * groups + g + 1, :] for g in range(groups)], axis=1)
        small[i][...] = row.reshape(groups * 128)
    for i in range(3):
        small[4 + i][...] = stats[i : i + 1, 0:1]
    for c in saves:
        c.wait()


def finish(norms, stats, arrays, kinds, n_parts):
    sds = jax.ShapeDtypeStruct
    anyspec = pl.BlockSpec(memory_space=pl.ANY)
    vspec = pl.BlockSpec(memory_space=pltpu.VMEM)
    vm = pltpu.VMEM
    dma = pltpu.SemaphoreType.DMA
    n = len(arrays)
    wide = [
        vm(a.shape if a.dtype != k else (8, 128), F32) for a, k in zip(arrays, kinds)
    ]
    return pl.pallas_call(
        functools.partial(finish_kernel, n_parts),
        out_shape=[sds(a.shape, k) for a, k in zip(arrays, kinds)]
        + [sds((norms.size // 4,), F32)] * 4 + [sds((1, 1), F32)] * 3,
        in_specs=[vspec] * 2 + [anyspec] * n,
        out_specs=[anyspec] * n + [vspec] * 7,
        scratch_shapes=[vm(a.shape, a.dtype) for a in arrays] + wide
        + [dma((sum(n_parts),)), dma((sum(n_parts),))],
        compiler_params=pltpu.CompilerParams(vmem_limit_bytes=VMEM_LIMIT),
        name="finish",
    )(norms, stats, *arrays)


def per_device(
    tokens, lengths, drop_in, drop_attn, drop_ffn, qkv_weight, out_weight, up_weight, down_weight,
    gain_first, shift_first, gain_second, shift_second, cotangent,
):
    n_dp = lax.axis_size("dp")
    width = tokens.shape[2]
    wq = jnp.transpose(qkv_weight, (1, 0, 2))
    x0, ma, mf, cot_p, wqf, wo_p, wu_p, wd_p, qkv, qb, ctx = front(
        lengths, tokens[0], drop_in[0], drop_attn[0], drop_ffn[0], cotangent[0],
        wq, out_weight, up_weight, down_weight,
    )
    gains = (gain_first, shift_first, gain_second, shift_second)
    lay, stats, act, dg, hl, n1, rs1, g2, dr2, ng2 = middle(
        lengths, gains, ctx, x0, ma, mf, cotangent[0], cot_p, out_weight, wo_p,
        up_weight, wu_p, down_weight, wd_p, n_dp,
    )
    gq, go, gu, gd, gt, norms = back(
        lengths, gain_first, ng2, g2, dr2, act, dg, hl, n1, rs1, ctx, ma, out_weight, wo_p,
        up_weight, wu_p, down_weight, wd_p, qb, qkv, x0, wqf, drop_in[0], n_dp,
    )
    lay, gt, gq, go, gu, gd, *small = finish(
        norms, stats, [lay, gt, gq, go, gu, gd], [BF16, F32, F32, F32, F32, F32], [2, 2, 3, 1, 3, 3]
    )
    return (
        lay[None], gt[None], jnp.transpose(gq, (1, 0, 2)), go, gu, gd,
        *small[:4], *(v.reshape(()) for v in small[4:]),
    )


def solution(mesh):
    act = P("dp", None, "tensor", None)
    in_specs = (
        P("dp", "tensor", None), P(), act, act, act,
        P(None, None, "tensor"), P("tensor", None), P(None, "tensor"), P("tensor", None),
        P(), P(), P(), P(), act,
    )
    out_specs = (
        act, P("dp", "tensor", None),
        P(None, None, "tensor"), P("tensor", None), P(None, "tensor"), P("tensor", None),
        P(), P(), P(), P(), P(), P(), P(),
    )
    return jax.shard_map(
        per_device, mesh=mesh, in_specs=in_specs, out_specs=out_specs, check_vma=False
    )
```
